256 devices in a mesh: ctx: 128 (over z, y, x), head: 2 (over core).
Axes of the slice: x: 4, y: 4, z: 8, core: 2. Of those that a mesh axis runs over, the one named last changes fastest.
Arguments:
- hidden_in: bfloat16 [2, 16384, 4096], P(None, 'ctx', 'head'), may hold values from -5 to 5
- norm_gain: bfloat16 [4096], replicated, may hold values from 0.099609375 to 1.8984375
- w_query: bfloat16 [4096, 2048], P('ctx', 'head'), may hold values from -0.35 to 0.35
- w_key: bfloat16 [4096, 512], P('ctx', 'head'), may hold values from -0.35 to 0.35
- w_value: bfloat16 [4096, 512], P('ctx', 'head'), may hold values from -0.09375 to 0.09375
- doc_ids: int32 [2, 16384], P(None, 'ctx'), may hold values from 0 to 31, never falling along the last dimension, each value on 1 to 1920 neighbouring positions
Outputs:
- attended: bfloat16 [2, 16384, 2048], P(None, 'ctx', 'head')
The draws below stay inside these ranges and needn't reach their ends.
Inputs may be any that keep to these rules, and one draw needn't show every extreme that they name: `doc_ids`: document numbers never fall along a sequence; each document of each sequence has 1 to 1920 positions and one has exactly 1920.
All inputs are finite; a program needn't handle non-finite values.
Results may differ from the reference program's by a relative error of at most 0.012.
Values may be sent and summed in bfloat16 or wider, within the bound.
No kernel may reach another device: no remote copies, remote signals or barrier semaphores. Data moves between devices by JAX's collectives and lax.ppermute only.
A program may use at most 128 MiB of HBM per device.

```python
import math
import jax
import jax.numpy as jnp
import numpy as np
from jax import lax

D = 4096
HD = 128
HQ = 16
HK = 4
BLK = 128
REACH = 15
SEQS = 2
LENGTH = 16384
DOCS = 32
DOC_MOST = 1920


def draw_hidden_in(key, part):
    key = jax.random.fold_in(key, 5)
    normal_rows = jnp.clip(jax.random.normal(key, (SEQS, LENGTH, D), jnp.float32), -5.0, 5.0)
    return normal_rows.astype(jnp.bfloat16)


def draw_w_query(key, part):
    key = jax.random.fold_in(key, 11)
    independent = jax.random.normal(key, (D, HQ, HD), jnp.float32)
    clip_bound = min(6.0 * D ** (-0.5), 0.35)
    drawn_weights = jnp.clip(independent * D ** (-0.5), -clip_bound, clip_bound)
    return drawn_weights.reshape(D, HQ * HD).astype(jnp.bfloat16)


def draw_w_key(key, part):
    key = jax.random.fold_in(key, 12)
    independent = jax.random.normal(key, (D, HK, HD), jnp.float32)
    clip_bound = min(6.0 * D ** (-0.5), 0.35)
    drawn_weights = jnp.clip(independent * D ** (-0.5), -clip_bound, clip_bound)
    return drawn_weights.reshape(D, HK * HD).astype(jnp.bfloat16)


def level_of(own_key, shape, split, least, high):
    gain, own = 1.0, jax.random.fold_in(own_key, 6)
    for axis_at, parts in split:
        steps = jnp.exp(jax.random.uniform(jax.random.fold_in(own, axis_at), (parts,), jnp.float32, least / len(split), high / len(split)))
        gain = gain * jnp.repeat(steps, shape[axis_at] // parts).reshape([-1 if axis == axis_at else 1 for axis in range(len(shape))])
    return gain


def profile(number_of, total, most, slope):
    loads = [(1 << 20) // math.isqrt(standing ** slope) + 1 for standing in range(2, number_of + 1)]
    spare, holding = total - most - (number_of - 1), [1] * (number_of - 1)
    while spare > 0:
        candidates = [i for i in range(number_of - 1) if holding[i] < most]
        mass, remaining = sum([loads[i] for i in candidates]), spare
        for i in candidates:
            addition = min(most - holding[i], max(1, remaining * loads[i] // mass), spare)
            holding[i] = holding[i] + addition
            spare = spare - addition
    return np.array([most] + holding)


def ragged_sizes(own_key, amount, total, limit, lean):
    if amount == 2:
        one = jax.random.randint(own_key, (), max(1, total - limit), min(limit, total - 1) + 1)
        return jnp.stack([one, total - one])
    lengths = jnp.asarray(profile(amount, total, limit, lean), jnp.int32)
    couples = (amount - 1) // 2
    source_of, sink = lengths[1:1 + 2 * couples:2], lengths[2:2 + 2 * couples:2]
    slack = jnp.minimum(source_of - 1, limit - sink)
    moved = jax.random.randint(jax.random.fold_in(own_key, 1), (couples,), 0, 1 << 20) % (slack + 1)
    lengths = lengths.at[1:1 + 2 * couples:2].set(source_of - moved).at[2:2 + 2 * couples:2].set(sink + moved)
    return lengths[jax.random.permutation(jax.random.fold_in(own_key, 2), amount)]


def centred(key, dims, scale, most, split=(), kind=jnp.bfloat16):
    values = scale * jax.random.normal(key, dims, jnp.float32)
    if split:
        values = values * level_of(key, dims, split, -0.22, 0.18)
    return jnp.clip(values, -most, most).astype(kind)


def setup_inputs(seed: int = 0) -> dict:
    arg_keys = jax.random.split(jax.random.key(seed), 7)
    return {
        "hidden_in": draw_hidden_in(jax.random.fold_in(arg_keys[6], 71), 0),
        "norm_gain": jnp.clip(1.0 + 0.18 * jax.random.normal(arg_keys[1], (D,), jnp.float32), 0.099609375, 1.8984375).astype(jnp.bfloat16),
        "w_query": draw_w_query(jax.random.fold_in(arg_keys[6], 71), 0),
        "w_key": draw_w_key(jax.random.fold_in(arg_keys[6], 71), 0),
        "w_value": centred(arg_keys[4], (D, HK * HD), D ** -0.5, 0.09375, ((0, 128), (1, 2))),
        "doc_ids": jax.vmap(lambda own: jnp.searchsorted(jnp.cumsum(ragged_sizes(own, DOCS, LENGTH, DOC_MOST, 2)), jnp.arange(LENGTH), side="right"))(jax.random.split(arg_keys[5], SEQS)).reshape((SEQS, LENGTH)).astype(jnp.int32),
    }


theta_base = 500000.0
epsilon = 1e-05

def rotate(tensor, positions):
    half_dim = tensor.shape[-1] // 2
    inverse_freq = theta_base ** (-jnp.arange(half_dim, dtype=jnp.float32) * 2.0 / tensor.shape[-1])
    angles = positions[:, None] * inverse_freq[None, :]
    cosine = jnp.cos(angles)[None, :, None, :]
    sine = jnp.sin(angles)[None, :, None, :]
    first_half = tensor[..., :half_dim]
    second_half = tensor[..., half_dim:]
    return jnp.concatenate([first_half * cosine - second_half * sine, second_half * cosine + first_half * sine], axis=-1)

def normalize(hidden_in, norm_gain):
    wide_x = hidden_in.astype(jnp.float32)
    mean_square = lax.optimization_barrier(jnp.mean(wide_x * wide_x, axis=-1, keepdims=True))
    return (wide_x * lax.rsqrt(mean_square + epsilon) * norm_gain.astype(jnp.float32)).astype(jnp.bfloat16)

def reference(hidden_in, norm_gain, w_query, w_key, w_value, doc_ids):
    normed = normalize(hidden_in, norm_gain).reshape(SEQS * LENGTH, D)
    queries = jnp.dot(normed, w_query, preferred_element_type=jnp.float32).reshape(SEQS, LENGTH, HQ, HD)
    keys = jnp.dot(normed, w_key, preferred_element_type=jnp.float32).reshape(SEQS, LENGTH, HK, HD)
    values = jnp.dot(normed, w_value, preferred_element_type=jnp.float32).reshape(SEQS, LENGTH, HK, HD)
    positions = jnp.arange(LENGTH).astype(jnp.float32)
    query_bf = rotate(queries, positions).astype(jnp.bfloat16)
    key_bf = rotate(keys, positions).astype(jnp.bfloat16)
    value_bf = values.astype(jnp.bfloat16)
    query_bf, key_bf, value_bf = lax.optimization_barrier((query_bf, key_bf, value_bf))
    front = REACH * BLK
    window = (REACH + 1) * BLK
    key_padded = jnp.concatenate([jnp.zeros((SEQS, front, HK, HD), jnp.bfloat16), key_bf], axis=1)
    value_padded = jnp.concatenate([jnp.zeros((SEQS, front, HK, HD), jnp.bfloat16), value_bf], axis=1)
    doc_padded = jnp.concatenate([jnp.full((SEQS, front), -1, jnp.int32), doc_ids.astype(jnp.int32)], axis=1)
    group_size = HQ // HK
    score_scale = HD ** (-0.5)

    def one_block(block_index):
        start = (block_index * BLK).astype(jnp.int32)
        query_rows = lax.dynamic_slice_in_dim(query_bf, start, BLK, 1).astype(jnp.float32)
        query_rows = query_rows.reshape(SEQS, BLK, HK, group_size, HD)
        key_rows = lax.dynamic_slice_in_dim(key_padded, start, window, 1).astype(jnp.float32)
        value_rows = lax.dynamic_slice_in_dim(value_padded, start, window, 1).astype(jnp.float32)
        query_docs = lax.dynamic_slice_in_dim(doc_ids.astype(jnp.int32), start, BLK, 1)
        key_docs = lax.dynamic_slice_in_dim(doc_padded, start, window, 1)
        query_pos = start + jnp.arange(BLK, dtype=jnp.int32)
        key_pos = start - front + jnp.arange(window, dtype=jnp.int32)
        visible = (query_docs[:, :, None] == key_docs[:, None, :]) & (key_pos[None, None, :] <= query_pos[None, :, None])
        visible = visible[:, None, None]
        scores = jnp.einsum('sqkgd,swkd->skgqw', query_rows, key_rows) * score_scale
        scores = jnp.where(visible, scores, -1e+30)
        row_max = lax.optimization_barrier(jnp.max(scores, axis=-1, keepdims=True))
        probs = jnp.where(visible, jnp.exp(scores - row_max), 0.0)
        row_total = lax.optimization_barrier(jnp.sum(probs, axis=-1))
        probs_bf = lax.optimization_barrier(probs.astype(jnp.bfloat16)).astype(jnp.float32)
        mixed = jnp.einsum('skgqw,swkd->skgqd', probs_bf, value_rows) / row_total[..., None]
        return mixed.transpose(0, 3, 1, 2, 4).reshape(SEQS, BLK, HQ * HD).astype(jnp.bfloat16)
    blocks = lax.map(one_block, jnp.arange(LENGTH // BLK, dtype=jnp.int32))
    return blocks.transpose(1, 0, 2, 3).reshape(SEQS, LENGTH, HQ * HD)
```

```python
import jax
import jax.numpy as jnp
from jax import lax
from jax.experimental import pallas as pl
from jax.experimental.pallas import tpu as pltpu
from jax.sharding import Mesh, PartitionSpec as P

HD = 128
NZ, NY, NX, NC = 8, 4, 4, 2
AXES = ("z", "y", "x", "head")
THETA = 500000.0
EPS = 1e-05
WIDTH = 4096
HALF = WIDTH // 2
COLS = 6 * HD
LOG2E = 1.4426950408889634
BF = jnp.bfloat16
F32 = jnp.float32


def flat(z, y, x, c):
    return ((z * NY + y) * NX + x) * NC + c


def permute(value, to):
    pairs = [
        (flat(z, y, x, c), flat(*to(z, y, x, c)))
        for z in range(NZ)
        for y in range(NY)
        for x in range(NX)
        for c in range(NC)
    ]
    return lax.ppermute(value, AXES, pairs)


def along_x(value, by):
    return permute(value, lambda z, y, x, c: (z, y, (x + by) % NX, c))


def along_z(value, by):
    return permute(value, lambda z, y, x, c: ((z + by) % NZ, y, x, c))


def spread(by):
    def to(z, y, x, c):
        b = (x + by) % 2
        return 2 * (z % 4) + y // 2, 2 * (y % 2) + x // 2, 2 * c + b, z // 4

    return to


def back(k):
    def to(z, y, x, c):
        return z, y, (2 * (x % 2) + c) ^ k, x // 2

    return to


VMEM = pl.BlockSpec(memory_space=pltpu.VMEM)
SMEM = pl.BlockSpec(memory_space=pltpu.SMEM)


def project_kernel(idx, gain, *refs):
    hidden = refs[:8]
    weights = refs[8:17]
    keep, send, w_all, x_all, squares = refs[17:]
    z, x, c = idx[0], idx[2], idx[3]
    for d, ref in zip((0, -1, -2, -3, 1, 2, 3), weights[:7]):
        at = lax.rem(z + d + NZ, NZ) * 256
        w_all[pl.ds(pl.multiple_of(at, 256), 256), :] = ref[...]
    at = lax.rem(z + 4, NZ) * 256
    w_all[pl.ds(pl.multiple_of(at, 128), 128), :] = weights[7][...]
    w_all[pl.ds(pl.multiple_of(at + 128, 128), 128), :] = weights[8][...]
    g = gain[...].astype(F32)
    for n, ref in enumerate(hidden):
        s, d = n // 4, (0, -1, 1, 2)[n % 4]
        other = jnp.where(c == s, 0, 512)
        base = other + lax.rem(x + d + NX, NX) * 128

        def rows(t, carry, ref=ref, base=base):
            at = pl.multiple_of(base + t * 16, 16)
            wide = ref[pl.ds(pl.multiple_of(t * 16, 16), 16), :].astype(F32)
            total = jnp.sum(wide * wide, axis=-1, keepdims=True)
            squares[pl.ds(at, 16), :] = jnp.broadcast_to(total, (16, HD))
            x_all[pl.ds(at, 16), :] = (wide * g).astype(BF)
            return carry

        lax.fori_loop(0, 8, rows, 0)
    lane = lax.broadcasted_iota(jnp.int32, (256, HD), 1)
    for t in range(2):
        at = t * 256
        send[at : at + 256, :COLS] = jnp.dot(
            x_all[512 + at : 768 + at, :], w_all[...], preferred_element_type=F32
        ).astype(BF)
        total = squares[512 + at : 768 + at, :]
        high = total.astype(BF).astype(F32)
        send[at : at + 256, COLS:] = jnp.where(lane < 64, high, total - high).astype(BF)
    for t in range(2):
        at = t * 256
        keep[at : at + 256, :COLS] = jnp.dot(
            x_all[at : at + 256, :], w_all[...], preferred_element_type=F32
        )
        keep[at : at + 256, COLS:] = squares[at : at + 256, :]


def rotate_kernel(keep, got, cosine, sine, query, kv):
    for i in range(4):
        rows = slice(i * 128, i * 128 + 128)
        extra = got[rows, COLS:].astype(F32)
        squares = keep[rows, COLS:] + extra + pltpu.roll(extra, 64, 1)
        scale = lax.rsqrt(squares * (1.0 / WIDTH) + EPS)
        cos, sin = cosine[rows, :], sine[rows, :]
        for h in range(6):
            cols = slice(h * 128, h * 128 + 128)
            value = (keep[rows, cols] + got[rows, cols].astype(F32)) * scale
            if h < 5:
                value = value * cos + pltpu.roll(value, 64, 1) * sin
            if h < 4:
                query[i, h * 128 : h * 128 + 128, :] = (value * (LOG2E * HD**-0.5)).astype(BF)
            elif h == 4:
                kv[i, 0, :, :] = value.astype(BF)
            else:
                kv[i, 1, :, :] = value.T.astype(BF)


def attend_kernel(idx, query, own, near, far, start, out, kv, scores):
    y, x, c = idx[1], idx[2], idx[3]
    kv[0:4] = far[...]
    for n in range(1, 4):
        kv[4 * n : 4 * n + 4] = near[lax.rem(y + n, NY)]
    kv[16:20] = own[...]
    slot = 2 * lax.rem(x, 2) + c
    sub = lax.broadcasted_iota(jnp.int32, (256, 512), 0)
    lane = lax.rem(lax.broadcasted_iota(jnp.int32, (256, 512), 1), 128)
    contract = (((1,), (1,)), ((), ()))
    for i in range(4):
        first = start[i]
        last = (i + 16) // 2
        low = jnp.minimum(lax.div(jnp.maximum(idx[4 + i], 0), 256), last)

        def score(p):
            pair = kv[pl.ds(2 * p, 2), 0].reshape(256, HD)
            return lax.dot_general(pair, query[i], contract, preferred_element_type=F32)

        def top(s):
            return jnp.max(s.reshape(32, 8, 512), axis=0)

        def scan(p, best):
            s = jnp.where(sub + 256 * p >= first, score(p), -1e30)
            scores[pl.ds(pl.multiple_of(p * 256, 256), 256), :] = s
            return jnp.maximum(best, top(s))

        s = score(last)
        pos = sub + 256 * last
        s = jnp.where((pos >= first) & (pos <= lane + (2048 + 128 * i)), s, -1e30)
        scores[256 * last : 256 * last + 256, :] = s
        best = lax.fori_loop(low, last, scan, top(s))
        best = jnp.max(best, axis=0, keepdims=True)

        def gather(p, carry):
            total, acc = carry
            e = jnp.exp2(scores[pl.ds(pl.multiple_of(p * 256, 256), 256), :] - best)
            total = total + jnp.sum(e.reshape(32, 8, 512), axis=0)
            pair = jnp.concatenate([kv[2 * p, 1], kv[2 * p + 1, 1]], axis=1)
            acc = acc + jnp.dot(pair, e.astype(BF), preferred_element_type=F32)
            return total, acc

        total, acc = lax.fori_loop(
            low, last + 1, gather, (jnp.zeros((8, 512), F32), jnp.zeros((HD, 512), F32))
        )
        total = jnp.sum(total, axis=0, keepdims=True)
        mixed = acc * (1.0 / total)
        to = jnp.bitwise_xor(slot, i)
        for h in range(4):
            cols = slice(h * 128, h * 128 + 128)
            out[to, :, cols] = mixed[:, cols].T.astype(BF)


def place_kernel(idx, *refs):
    out = refs[4]
    for k in range(4):
        slot = jnp.bitwise_xor(idx[2], k)
        at = pl.multiple_of(lax.div(slot, 2) * 512, 512)
        out[lax.rem(slot, 2), :, pl.ds(at, 512)] = refs[k][...]


def call(kernel, shapes, args, scratch=(), cost=None, smem=1):
    return pl.pallas_call(
        kernel,
        out_shape=shapes,
        in_specs=[SMEM] * smem + [VMEM] * (len(args) - smem),
        out_specs=jax.tree.map(lambda _: VMEM, shapes),
        scratch_shapes=list(scratch),
        cost_estimate=cost,
        compiler_params=pltpu.CompilerParams(vmem_limit_bytes=48 * 1024 * 1024),
    )(*args)


def local(hidden_in, norm_gain, w_query, w_key, w_value, doc_ids):
    z, y, x, c = (lax.axis_index(a) for a in AXES)
    group = z * NY + y
    shape = jax.ShapeDtypeStruct

    seq_a, seq_b = hidden_in[0], hidden_in[1]
    right_a, left_b = along_x(seq_a, 1), along_x(seq_b, -1)
    right_b, left_a = along_x(seq_b, 1), along_x(seq_a, -1)
    far_a, far_b = along_x(right_a, 1), along_x(left_b, -1)

    pieces = [
        jnp.concatenate(
            [
                w_query[:, b * 512 : b * 512 + 512],
                w_key[:, b * 128 : b * 128 + 128],
                w_value[:, b * 128 : b * 128 + 128],
            ],
            axis=1,
        )
        for b in range(2)
    ]
    odd = x % 2 == 1
    first = permute(jnp.where(odd, pieces[1], pieces[0]), spread(0))
    second = permute(jnp.where(odd, pieces[0], pieces[1]), spread(1))
    rows = jnp.concatenate([jnp.where(odd, second, first), jnp.where(odd, first, second)], axis=0)
    mine = lax.all_gather(rows, "y", axis=0, tiled=True)
    up1, down1 = along_z(mine, 1), along_z(mine, -1)
    up2, down2 = along_z(up1, 1), along_z(down1, -1)
    up3, down3 = along_z(up2, 1), along_z(down2, -1)
    up4, down4 = along_z(up3[:128], 1), along_z(down3[128:], -1)

    plane = lax.all_gather(doc_ids, ("y", "x"), axis=1, tiled=True)
    before = jnp.where(z == 0, -1, along_z(plane, 1))
    window = lax.dynamic_index_in_dim(jnp.concatenate([before, plane], axis=1), c, 0, False)
    docs = lax.dynamic_slice_in_dim(window, 2048 + 512 * y, 512, 0)
    start = jnp.sum((window[None, :] < docs[:, None]).astype(jnp.int32), axis=1) - 512 * y
    start_rows = jnp.tile(start.reshape(4, 1, 128), (1, 1, 4))
    idx = jnp.concatenate([jnp.stack([z, y, x, c]).astype(jnp.int32), start[::128]])

    position = (512 * group + jnp.arange(512, dtype=jnp.int32)).astype(F32)
    inverse = THETA ** (-jnp.arange(64, dtype=F32) * 2.0 / HD)
    angle = position[:, None] * inverse[None, :]
    cos, sin = jnp.cos(angle), jnp.sin(angle)
    cosine = jnp.concatenate([cos, cos], axis=1)
    sine = jnp.concatenate([-sin, sin], axis=1)

    gain = lax.dynamic_index_in_dim(norm_gain.reshape(2, HALF), c, 0, True)
    where = jnp.stack([z, y, x, c]).astype(jnp.int32)
    keep, send = call(
        project_kernel,
        (shape((512, COLS + HD), F32), shape((512, COLS + HD), BF)),
        (where, gain, seq_a, right_a, left_a, far_a, seq_b, right_b, left_b, far_b)
        + (mine, up1, up2, up3, down1, down2, down3, up4, down4),
        (pltpu.VMEM((HALF, COLS), BF), pltpu.VMEM((1024, HALF), BF), pltpu.VMEM((1024, HD), F32)),
        pl.CostEstimate(flops=2 * 1024 * HALF * COLS, bytes_accessed=10 << 20, transcendentals=0),
    )
    got = permute(send, lambda z, y, x, c: (z, y, x, 1 - c))
    query, own = call(
        rotate_kernel,
        (shape((4, 512, HD), BF), shape((4, 2, 128, HD), BF)),
        (keep, got, cosine, sine),
        cost=pl.CostEstimate(flops=5 << 20, bytes_accessed=4 << 20, transcendentals=512),
        smem=0,
    )
    far = along_z(own, 1)
    later = (jnp.arange(NY) > y)[:, None, None, None, None]
    near = lax.all_to_all(jnp.where(later, own[None], far[None]), "y", 0, 0, tiled=True)
    attended = call(
        attend_kernel,
        shape((4, 128, 512), BF),
        (idx, query, own, near, far, start_rows),
        (pltpu.VMEM((20, 2, 128, HD), BF), pltpu.VMEM((2560, 512), F32)),
        pl.CostEstimate(flops=2 << 30, bytes_accessed=4 << 20, transcendentals=4 << 20),
    )
    blocks = [permute(attended[k], back(k)) for k in range(4)]
    return call(
        place_kernel,
        shape((2, 128, 1024), BF),
        (where, *blocks),
        cost=pl.CostEstimate(flops=0, bytes_accessed=1 << 20, transcendentals=0),
    )


def solution(mesh):
    fine = Mesh(mesh.devices.reshape(NZ, NY, NX, NC), AXES)
    ctx = ("z", "y", "x")
    return jax.shard_map(
        local,
        mesh=fine,
        in_specs=(
            P(None, ctx, "head"),
            P(),
            P(ctx, "head"),
            P(ctx, "head"),
            P(ctx, "head"),
            P(None, ctx),
        ),
        out_specs=P(None, ctx, "head"),
        check_vma=False,
    )
```

```python
import jax
import jax.numpy as jnp
from jax import lax
from jax.experimental import pallas as pl
from jax.experimental.pallas import tpu as pltpu
from jax.sharding import Mesh, PartitionSpec as P

HD = 128
NZ, NY, NX, NC = 8, 4, 4, 2
AXES = ("z", "y", "x", "head")
THETA = 500000.0
EPS = 1e-05
WIDTH = 4096
HALF = WIDTH // 2
COLS = 6 * HD
LOG2E = 1.4426950408889634
BF = jnp.bfloat16
F32 = jnp.float32


def flat(z, y, x, c):
    return ((z * NY + y) * NX + x) * NC + c


def permute(value, to):
    pairs = [
        (flat(z, y, x, c), flat(*to(z, y, x, c)))
        for z in range(NZ)
        for y in range(NY)
        for x in range(NX)
        for c in range(NC)
    ]
    return lax.ppermute(value, AXES, pairs)


def along_x(value, by):
    return permute(value, lambda z, y, x, c: (z, y, (x + by) % NX, c))


def along_z(value, by):
    return permute(value, lambda z, y, x, c: ((z + by) % NZ, y, x, c))


def spread(by):
    def to(z, y, x, c):
        b = (x + by) % 2
        return 2 * (z % 4) + y // 2, 2 * (y % 2) + x // 2, 2 * c + b, z // 4

    return to


def back(k):
    def to(z, y, x, c):
        return z, y, (2 * (x % 2) + c) ^ k, x // 2

    return to


VMEM = pl.BlockSpec(memory_space=pltpu.VMEM)
SMEM = pl.BlockSpec(memory_space=pltpu.SMEM)


def pack_kernel(idx, query, key, value, first, second):
    x = idx[2]
    for by, out in ((0, first), (1, second)):
        b = lax.rem(x + by, 2)
        out[:, :512] = query[:, pl.ds(pl.multiple_of(b * 512, 512), 512)]
        out[:, 512:640] = key[:, pl.ds(pl.multiple_of(b * 128, 128), 128)]
        out[:, 640:] = value[:, pl.ds(pl.multiple_of(b * 128, 128), 128)]


def assemble(z, pieces, w_all):
    for d, ref in zip((0, -1, -2, -3, 1, 2, 3), pieces[:7]):
        at = lax.rem(z + d + NZ, NZ) * 256
        w_all[pl.ds(pl.multiple_of(at, 256), 256), :] = ref[...]
    at = lax.rem(z + 4, NZ) * 256
    w_all[pl.ds(pl.multiple_of(at, 128), 128), :] = pieces[7][...]
    w_all[pl.ds(pl.multiple_of(at + 128, 128), 128), :] = pieces[8][...]


def multiply(x_all, w_all, keep, send):
    for t in range(2):
        at = t * 256
        send[at : at + 256, :] = jnp.dot(
            x_all[512 + at : 768 + at, :], w_all[...], preferred_element_type=F32
        )
    for t in range(2):
        at = t * 256
        keep[at : at + 256, :] = jnp.dot(
            x_all[at : at + 256, :], w_all[...], preferred_element_type=F32
        )


def project_kv_kernel(idx, *refs):
    hidden, pieces = refs[:8], refs[8:17]
    keep, send, x_all, w_all = refs[17:]
    z, x, c = idx[0], idx[2], idx[3]
    assemble(z, pieces, w_all)
    for n, ref in enumerate(hidden):
        s, d = n // 4, (0, -1, 1, 2)[n % 4]
        base = jnp.where(c == s, 0, 512) + lax.rem(x + d + NX, NX) * 128
        x_all[pl.ds(pl.multiple_of(base, 128), 128), :] = ref[...]
    multiply(x_all, w_all, keep, send)


def project_q_kernel(idx, x_all, *refs):
    pieces = refs[:9]
    keep, send, w_all = refs[9:]
    assemble(idx[0], pieces, w_all)
    multiply(x_all, w_all, keep, send)


def turned(value, cosine, sine):
    return value * cosine + pltpu.roll(value, 64, 1) * sine


def rotate_kv_kernel(keep, got, cosine, sine, kv):
    for i in range(4):
        rows = slice(i * 128, i * 128 + 128)
        value = keep[rows, :] + got[rows, :]
        kv[i, 0, :, :] = turned(value[:, :128], cosine[rows, :], sine[rows, :]).astype(BF)
        kv[i, 1, :, :] = value[:, 128:].T.astype(BF)


def rotate_q_kernel(keep, got, cosine, sine, query):
    for i in range(4):
        rows = slice(i * 128, i * 128 + 128)
        cos, sin = cosine[rows, :], sine[rows, :]
        for h in range(4):
            cols = slice(h * 128, h * 128 + 128)
            value = keep[rows, cols] + got[rows, cols]
            query[i, h * 128 : h * 128 + 128, :] = turned(value, cos, sin).astype(BF)


def attend(idx, query, start, kv, scores, outs, pair):
    slot = 2 * lax.rem(idx[2], 2) + idx[3]
    sub = lax.broadcasted_iota(jnp.int32, (256, 512), 0)
    lane = lax.rem(lax.broadcasted_iota(jnp.int32, (256, 512), 1), 128)
    contract = (((1,), (1,)), ((), ()))
    for k in range(2):
        i = jnp.bitwise_xor(slot, 2 * pair + k)
        first, q_rows = start[i], query[i]
        last = lax.div(i + 16, 2)
        low = jnp.minimum(lax.div(jnp.maximum(idx[4 + i], 0), 256), last)

        def score(p):
            keys = kv[pl.ds(2 * p, 2), 0].reshape(256, HD)
            return lax.dot_general(keys, q_rows, contract, preferred_element_type=F32)

        def top(s):
            return jnp.max(s.reshape(32, 8, 512), axis=0)

        def scan(p, best):
            s = jnp.where(sub + 256 * p >= first, score(p), -1e30)
            scores[pl.ds(pl.multiple_of(p * 256, 256), 256), :] = s
            return jnp.maximum(best, top(s))

        s = score(last)
        pos = sub + 256 * last
        s = jnp.where((pos >= first) & (pos <= lane + (2048 + 128 * i)), s, -1e30)
        scores[pl.ds(pl.multiple_of(256 * last, 256), 256), :] = s
        best = lax.fori_loop(low, last, scan, top(s))
        best = jnp.max(best, axis=0, keepdims=True)

        def gather(p, carry):
            total, acc = carry
            s = scores[pl.ds(pl.multiple_of(p * 256, 256), 256), :]
            e = jnp.exp2((s - best) * (LOG2E * HD**-0.5))
            total = total + jnp.sum(e.reshape(32, 8, 512), axis=0)
            values = jnp.concatenate([kv[2 * p, 1], kv[2 * p + 1, 1]], axis=1)
            acc = acc + jnp.dot(values, e.astype(BF), preferred_element_type=F32)
            return total, acc

        total, acc = lax.fori_loop(
            low, last + 1, gather, (jnp.zeros((8, 512), F32), jnp.zeros((HD, 512), F32))
        )
        mixed = acc / jnp.sum(total, axis=0, keepdims=True)
        for h in range(4):
            cols = slice(h * 128, h * 128 + 128)
            outs[k][:, cols] = mixed[:, cols].T.astype(BF)


def attend_first_kernel(idx, query, own, near, far, start, out0, out1, kv, scores):
    y = idx[1]
    kv[0:4] = far[...]
    for n in range(1, 4):
        kv[4 * n : 4 * n + 4] = near[lax.rem(y + n, NY)]
    kv[16:20] = own[...]
    attend(idx, query, start, kv, scores, (out0, out1), 0)


def attend_second_kernel(idx, query, kv, start, out0, out1, scores):
    attend(idx, query, start, kv, scores, (out0, out1), 1)


def place_kernel(idx, *refs):
    out = refs[4]
    for k in range(4):
        slot = jnp.bitwise_xor(idx[2], k)
        at = pl.multiple_of(lax.div(slot, 2) * 512, 512)
        out[lax.rem(slot, 2), :, pl.ds(at, 512)] = refs[k][...]


def call(kernel, shapes, args, scratch=(), cost=None, smem=1, mib=16):
    return pl.pallas_call(
        kernel,
        out_shape=shapes,
        in_specs=[SMEM] * smem + [VMEM] * (len(args) - smem),
        out_specs=jax.tree.map(lambda _: VMEM, shapes),
        scratch_shapes=list(scratch),
        cost_estimate=cost,
        compiler_params=pltpu.CompilerParams(vmem_limit_bytes=mib * 1024 * 1024),
    )(*args)


def cost(flops, nbytes):
    return pl.CostEstimate(flops=flops, bytes_accessed=nbytes, transcendentals=0)


def tie(*values):
    return lax.optimization_barrier(values)


def copies(value, axis):
    return lax.all_to_all(jnp.broadcast_to(value[None], (4, *value.shape)), axis, 0, 0, tiled=True)


def local(hidden_in, norm_gain, w_query, w_key, w_value, doc_ids):
    z, y, x, c = (lax.axis_index(a) for a in AXES)
    group = z * NY + y
    shape = jax.ShapeDtypeStruct
    where = jnp.stack([z, y, x, c]).astype(jnp.int32)

    piece = shape((32, COLS), BF)
    first, second = call(
        pack_kernel, (piece, piece), (where, w_query, w_key, w_value), cost=cost(0, 1 << 18)
    )
    first, second = permute(first, spread(0)), permute(second, spread(1))

    wide = hidden_in.astype(F32)
    squares = jnp.sum(wide * wide, axis=-1)
    squares = squares + permute(squares, lambda z, y, x, c: (z, y, x, 1 - c))
    gain = lax.dynamic_index_in_dim(norm_gain.reshape(2, HALF), c, 0, False).astype(F32)
    scale = lax.rsqrt(squares * (1.0 / WIDTH) + EPS)
    normed = (wide * scale[..., None] * gain).astype(BF)
    seq_a, seq_b = normed[0], normed[1]

    odd = x % 2 == 1
    rows = jnp.concatenate([jnp.where(odd, second, first), jnp.where(odd, first, second)], axis=0)
    rows, seq_a, seq_b = tie(rows, seq_a, seq_b)

    right_a, left_b = along_x(seq_a, 1), along_x(seq_b, -1)
    right_b, left_a = along_x(seq_b, 1), along_x(seq_a, -1)

    mine = copies(rows, "y").reshape(256, COLS)
    kv0, q0 = mine[:, 512:], mine[:, :512]
    kv_up1, kv_down1 = along_z(kv0, 1), along_z(kv0, -1)
    q_up1, q_down1 = along_z(q0, 1), along_z(q0, -1)

    row_docs = copies(doc_ids, "x")
    row_docs = lax.dynamic_index_in_dim(row_docs, c, 1, False)
    plane = copies(row_docs, "y").reshape(2048)
    before = jnp.where(z == 0, -1, along_z(plane, 1))

    kv_up1, kv_down1, right_a, left_b = tie(kv_up1, kv_down1, right_a, left_b)
    far_a, far_b = along_x(right_a, 1), along_x(left_b, -1)
    kv_up2, kv_down2 = along_z(kv_up1, 1), along_z(kv_down1, -1)
    q_up2, q_down2 = along_z(q_up1, 1), along_z(q_down1, -1)
    kv_up3, kv_down3 = along_z(kv_up2, 1), along_z(kv_down2, -1)
    q_up3, q_down3 = along_z(q_up2, 1), along_z(q_down2, -1)
    kv_up3, kv_down3, right_b, left_a, plane, before = tie(
        kv_up3, kv_down3, right_b, left_a, plane, before
    )
    kv_up4, kv_down4 = along_z(kv_up3[:128], 1), along_z(kv_down3[128:], -1)
    q_up4, q_down4 = along_z(q_up3[:128], 1), along_z(q_down3[128:], -1)

    window = jnp.concatenate([before, plane])
    docs = lax.dynamic_slice_in_dim(window, 2048 + 512 * y, 512, 0)
    start = jnp.sum((window[None, :] < docs[:, None]).astype(jnp.int32), axis=1) - 512 * y
    start_rows = jnp.tile(start.reshape(4, 1, 128), (1, 1, 4))
    idx = jnp.concatenate([where, start[::128]])

    position = (512 * group + jnp.arange(512, dtype=jnp.int32)).astype(F32)
    inverse = THETA ** (-jnp.arange(64, dtype=F32) * 2.0 / HD)
    angle = position[:, None] * inverse[None, :]
    cos, sin = jnp.cos(angle), jnp.sin(angle)
    cosine = jnp.concatenate([cos, cos], axis=1)
    sine = jnp.concatenate([-sin, sin], axis=1)

    kv_up4, idx, start_rows, cosine, sine = tie(kv_up4, idx, start_rows, cosine, sine)
    keep, send, x_all = call(
        project_kv_kernel,
        (shape((512, 256), F32), shape((512, 256), F32), shape((1024, HALF), BF)),
        (where, seq_a, right_a, left_a, far_a, seq_b, right_b, left_b, far_b)
        + (kv0, kv_up1, kv_up2, kv_up3, kv_down1, kv_down2, kv_down3, kv_up4, kv_down4),
        (pltpu.VMEM((HALF, 256), BF),),
        cost(2 * 1024 * HALF * 256, 10 << 20),
        mib=24,
    )
    got = permute(send, lambda z, y, x, c: (z, y, x, 1 - c))
    own = call(
        rotate_kv_kernel,
        shape((4, 2, 128, HD), BF),
        (keep, got, cosine, sine),
        cost=cost(1 << 20, 2 << 20),
        smem=0,
    )
    far = along_z(own, 1)
    keep, send = call(
        project_q_kernel,
        (shape((512, 512), F32), shape((512, 512), F32)),
        (where, x_all, q0, q_up1, q_up2, q_up3, q_down1, q_down2, q_down3, q_up4, q_down4),
        (pltpu.VMEM((HALF, 512), BF),),
        cost(2 * 1024 * HALF * 512, 10 << 20),
        mib=24,
    )
    got = permute(send, lambda z, y, x, c: (z, y, x, 1 - c))
    later = (jnp.arange(NY) > y)[:, None, None, None, None]
    near = lax.all_to_all(jnp.where(later, own[None], far[None]), "y", 0, 0, tiled=True)
    query = call(
        rotate_q_kernel,
        shape((4, 512, HD), BF),
        (keep, got, cosine, sine),
        cost=cost(4 << 20, 3 << 20),
        smem=0,
    )
    block = shape((128, 512), BF)
    scores = pltpu.VMEM((2560, 512), F32)
    out0, out1, kv = call(
        attend_first_kernel,
        (block, block, shape((20, 2, 128, HD), BF)),
        (idx, query, own, near, far, start_rows),
        (scores,),
        cost(1 << 30, 4 << 20),
        mib=20,
    )
    out0, out1 = permute(out0, back(0)), permute(out1, back(1))
    out2, out3 = call(
        attend_second_kernel,
        (block, block),
        (idx, query, kv, start_rows),
        (scores,),
        cost(1 << 30, 4 << 20),
        mib=20,
    )
    out0, out1, out2, out3 = tie(out0, out1, out2, out3)
    out2, out3 = permute(out2, back(2)), permute(out3, back(3))
    return call(
        place_kernel, shape((2, 128, 1024), BF), (where, out0, out1, out2, out3), cost=cost(0, 1 << 20)
    )


def solution(mesh):
    fine = Mesh(mesh.devices.reshape(NZ, NY, NX, NC), AXES)
    ctx = ("z", "y", "x")
    return jax.shard_map(
        local,
        mesh=fine,
        in_specs=(
            P(None, ctx, "head"),
            P(),
            P(ctx, "head"),
            P(ctx, "head"),
            P(ctx, "head"),
            P(None, ctx),
        ),
        out_specs=P(None, ctx, "head"),
        check_vma=False,
    )
```

```python
import jax
import jax.numpy as jnp
from jax import lax
from jax.experimental import pallas as pl
from jax.experimental.pallas import tpu as pltpu
from jax.sharding import Mesh, PartitionSpec as P

HD = 128
NZ, NY, NX, NC = 8, 4, 4, 2
AXES = ("z", "y", "x", "head")
THETA = 500000.0
EPS = 1e-05
WIDTH = 4096
HALF = WIDTH // 2
COLS = 6 * HD
LOG2E = 1.4426950408889634
BF = jnp.bfloat16
F32 = jnp.float32


def flat(z, y, x, c):
    return ((z * NY + y) * NX + x) * NC + c


def permute(value, to):
    pairs = [
        (flat(z, y, x, c), flat(*to(z, y, x, c)))
        for z in range(NZ)
        for y in range(NY)
        for x in range(NX)
        for c in range(NC)
    ]
    return lax.ppermute(value, AXES, pairs)


def along_x(value, by):
    return permute(value, lambda z, y, x, c: (z, y, (x + by) % NX, c))


def along_z(value, by):
    return permute(value, lambda z, y, x, c: ((z + by) % NZ, y, x, c))


def along_y(value, by):
    return permute(value, lambda z, y, x, c: (z, (y + by) % NY, x, c))


def spread(by):
    def to(z, y, x, c):
        b = (x + by) % 2
        return 2 * (z % 4) + y // 2, 2 * (y % 2) + x // 2, 2 * c + b, z // 4

    return to


def back(k):
    def to(z, y, x, c):
        return z, y, (2 * (x % 2) + c) ^ k, x // 2

    return to


VMEM = pl.BlockSpec(memory_space=pltpu.VMEM)
SMEM = pl.BlockSpec(memory_space=pltpu.SMEM)
ROWS = 8 * HD + 16


def begin_kernel(idx, hidden, query, key, value, first, second, squares):
    x = idx[2]
    for by, out in ((0, first), (1, second)):
        b = lax.rem(x + by, 2)
        out[:, :512] = query[:, pl.ds(pl.multiple_of(b * 512, 512), 512)]
        out[:, 512:640] = key[:, pl.ds(pl.multiple_of(b * 128, 128), 128)]
        out[:, 640:] = value[:, pl.ds(pl.multiple_of(b * 128, 128), 128)]

    for s in range(2):
        wide = hidden[s].astype(F32)
        total = jnp.sum(wide * wide, axis=-1, keepdims=True)
        squares[s : s + 1, :] = jnp.broadcast_to(total, (HD, HD)).T[:1, :]


def tell_kernel(squares, others, docs, out):
    scale = lax.rsqrt((squares[...] + others[...]) * (1.0 / WIDTH) + EPS)
    for n in range(NX):
        out[n, 0:2, :] = docs[...].astype(F32)
        out[n, 2:4, :] = scale


def merge_kernel(idx, first, second, out):
    odd = lax.rem(idx[2], 2) == 1
    top, low = first[...].astype(F32), second[...].astype(F32)
    out[:32, :] = jnp.where(odd, low, top).astype(BF)
    out[32:, :] = jnp.where(odd, top, low).astype(BF)


def norm_kernel(idx, told, gain, *refs):
    hidden, x_all = refs[:8], refs[8]
    x, c = idx[2], idx[3]
    g = gain[:, pl.ds(pl.multiple_of(c * HALF, HALF), HALF)].astype(F32)
    for n, ref in enumerate(hidden):
        s, d = n // 4, (0, -1, 1, 2)[n % 4]
        chip = lax.rem(x + d + NX, NX)
        base = jnp.where(c == s, 0, 512) + chip * 128
        scale = jnp.broadcast_to(told[chip, 2 + s : 3 + s, :], (HD, HD)).T
        for t in range(4):
            rows = slice(t * 32, t * 32 + 32)
            wide = ref[rows, :].astype(F32) * scale[rows, :1] * g
            x_all[pl.ds(pl.multiple_of(base + t * 32, 32), 32), :] = wide.astype(BF)


def multiply(x_all, w_all, keep, send):
    for t in range(2):
        at = t * 256
        send[at : at + 256, :] = jnp.dot(
            x_all[512 + at : 768 + at, :], w_all, preferred_element_type=F32
        )
    for t in range(2):
        at = t * 256
        keep[at : at + 256, :] = jnp.dot(
            x_all[at : at + 256, :], w_all, preferred_element_type=F32
        )


def project_kernel(idx, x_all, own, up, down, far_up, far_down, keep, send, w_all):
    columns = own.shape[1]
    for ref, d, first in ((own, 0, 0), (up, -1, 0), (down, 1, 0), (far_up, 2, 0), (far_down, 2, 4)):
        shift = pl.multiple_of(lax.rem(idx[1] + d + NY, NY) * 64, 64)
        for z in range(ref.shape[0] // 64):
            w_all[first + z, pl.ds(shift, 64), :] = ref[z * 64 : z * 64 + 64, :]
    multiply(x_all, w_all[...].reshape(HALF, columns), keep, send)


def turned(value, cos, sin):
    cosine = jnp.concatenate([cos, cos], axis=1)
    sine = jnp.concatenate([-sin, sin], axis=1)
    return value * cosine + pltpu.roll(value, 64, 1) * sine


def rotate_kv_kernel(idx, keep, got, cos, sin, docs, kv):
    for i in range(4):
        rows = slice(i * 128, i * 128 + 128)
        value = keep[rows, :] + got[rows, :]
        at = i * 256
        kv[at : at + 128, :] = turned(value[:, :128], cos[rows, :], sin[rows, :]).astype(BF)
        kv[at + 128 : at + 256, :] = value[:, 128:].T.astype(BF)
    own = jnp.where(idx[3] == 0, docs[:, 0, :], docs[:, 1, :])
    kv[1024:1040, :] = jnp.concatenate([own, jnp.zeros((12, HD), F32)], axis=0).astype(BF)


def rotate_q_kernel(keep, got, cos, sin, query):
    for i in range(4):
        rows = slice(i * 128, i * 128 + 128)
        for h in range(4):
            cols = slice(h * 128, h * 128 + 128)
            value = keep[rows, cols] + got[rows, cols]
            query[i, h * 128 : h * 128 + 128, :] = turned(value, cos[rows, :], sin[rows, :]).astype(BF)


def attend(idx, query, start, kv, scores, outs, pair):
    slot = 2 * lax.rem(idx[2], 2) + idx[3]
    sub = lax.broadcasted_iota(jnp.int32, (256, 512), 0)
    lane = lax.rem(lax.broadcasted_iota(jnp.int32, (256, 512), 1), 128)
    contract = (((1,), (1,)), ((), ()))
    for k in range(2):
        i = jnp.bitwise_xor(slot, 2 * pair + k)
        first, q_rows = start[i], query[i]
        last = lax.div(i + 16, 2)
        low = jnp.minimum(lax.div(jnp.maximum(jnp.min(first), 0), 256), last)

        def score(p):
            keys = kv[pl.ds(2 * p, 2), 0].reshape(256, HD)
            return lax.dot_general(keys, q_rows, contract, preferred_element_type=F32)

        def top(s):
            return jnp.max(s.reshape(32, 8, 512), axis=0)

        def scan(p, best):
            s = jnp.where(sub + 256 * p >= first, score(p), -1e30)
            scores[pl.ds(pl.multiple_of(p * 256, 256), 256), :] = s
            return jnp.maximum(best, top(s))

        s = score(last)
        pos = sub + 256 * last
        s = jnp.where((pos >= first) & (pos <= lane + (2048 + 128 * i)), s, -1e30)
        scores[pl.ds(pl.multiple_of(256 * last, 256), 256), :] = s
        best = lax.fori_loop(low, last, scan, top(s))
        best = jnp.max(best, axis=0, keepdims=True)

        def gather(p, carry):
            total, acc = carry
            s = scores[pl.ds(pl.multiple_of(p * 256, 256), 256), :]
            e = jnp.exp2((s - best) * (LOG2E * HD**-0.5))
            total = total + jnp.sum(e.reshape(32, 8, 512), axis=0)
            values = jnp.concatenate([kv[2 * p, 1], kv[2 * p + 1, 1]], axis=1)
            acc = acc + jnp.dot(values, e.astype(BF), preferred_element_type=F32)
            return total, acc

        total, acc = lax.fori_loop(
            low, last + 1, gather, (jnp.zeros((8, 512), F32), jnp.zeros((HD, 512), F32))
        )
        mixed = acc / jnp.sum(total, axis=0, keepdims=True)
        for h in range(4):
            cols = slice(h * 128, h * 128 + 128)
            outs[k][:, cols] = mixed[:, cols].T.astype(BF)


def attend_first_kernel(idx, query, own, near, far, out0, out1, kv, start, scores, docs):
    z, y = idx[0], idx[1]
    docs[...] = jnp.zeros((128, HD), F32)
    for n in range(5):
        if n in (0, 4):
            piece = (far, own)[n // 4]
            kv[4 * n : 4 * n + 4] = piece[:1024, :].reshape(4, 2, 128, HD)
            tile = piece[1024:1040, :]
        else:
            at = lax.rem(y + n, NY)
            kv[4 * n : 4 * n + 4] = near[at, :1024, :].reshape(4, 2, 128, HD)
            tile = near[at, 1024:1040, :]
        before = (z == 0) & (y + n < 4)
        docs[4 * n : 4 * n + 4, :] = jnp.where(before, -1.0, tile.astype(F32)[:4, :])
    columns = docs[...].T
    mine = jnp.concatenate([docs[16 + i : 17 + i, :] for i in range(4)], axis=1)
    count = jnp.zeros((8, 512), F32)
    for n in range(20):
        smaller = jnp.where(columns[:, n : n + 1] < mine, 1.0, 0.0)
        count = count + jnp.sum(smaller.reshape(16, 8, 512), axis=0)
    count = jnp.sum(count, axis=0, keepdims=True).astype(jnp.int32)
    for i in range(4):
        row = count[:, i * 128 : i * 128 + 128]
        start[i] = jnp.concatenate([row] * 4, axis=1)
    attend(idx, query, start, kv, scores, (out0, out1), 0)


def attend_second_kernel(idx, query, kv, start, out0, out1, scores):
    attend(idx, query, start, kv, scores, (out0, out1), 1)


def place_kernel(idx, *refs):
    out = refs[4]
    for k in range(4):
        slot = jnp.bitwise_xor(idx[2], k)
        at = pl.multiple_of(lax.div(slot, 2) * 512, 512)
        out[lax.rem(slot, 2), :, pl.ds(at, 512)] = refs[k][...]


def call(kernel, shapes, args, scratch=(), cost=None, smem=1, mib=16):
    return pl.pallas_call(
        kernel,
        out_shape=shapes,
        in_specs=[SMEM] * smem + [VMEM] * (len(args) - smem),
        out_specs=jax.tree.map(lambda _: VMEM, shapes),
        scratch_shapes=list(scratch),
        cost_estimate=cost,
        compiler_params=pltpu.CompilerParams(vmem_limit_bytes=mib * 1024 * 1024),
    )(*args)


def cost(flops, nbytes):
    return pl.CostEstimate(flops=flops, bytes_accessed=nbytes, transcendentals=0)


def tie(*values):
    return lax.optimization_barrier(values)


def copies(value, axis, count):
    return lax.all_to_all(
        jnp.broadcast_to(value[None], (count, *value.shape)), axis, 0, 0, tiled=True
    )


def local(hidden_in, norm_gain, w_query, w_key, w_value, doc_ids):
    z, y, x, c = (lax.axis_index(a) for a in AXES)
    shape = jax.ShapeDtypeStruct
    where = jnp.stack([z, y, x, c]).astype(jnp.int32)

    seq_a, seq_b = hidden_in[0], hidden_in[1]
    right_a, left_b = along_x(seq_a, 1), along_x(seq_b, -1)
    right_b, left_a = along_x(seq_b, 1), along_x(seq_a, -1)

    piece = shape((32, COLS), BF)
    first, second, squares = call(
        begin_kernel,
        (piece, piece, shape((2, HD), F32)),
        (where, hidden_in, w_query, w_key, w_value),
        cost=cost(1 << 20, 2 << 20),
    )
    first, second = permute(first, spread(0)), permute(second, spread(1))
    others = permute(squares, lambda z, y, x, c: (z, y, x, 1 - c))
    told = call(
        tell_kernel,
        shape((NX, 4, HD), F32),
        (squares, others, doc_ids),
        cost=cost(0, 1 << 14),
        smem=0,
    )
    told = lax.all_to_all(told, "x", 0, 0, tiled=True)
    first, second, right_a, left_b = tie(first, second, right_a, left_b)
    far_a, far_b = along_x(right_a, 1), along_x(left_b, -1)
    rows = call(merge_kernel, shape((64, COLS), BF), (where, first, second), cost=cost(0, 1 << 18))
    w_z = copies(rows, "z", NZ).reshape(512, COLS)
    w_z, right_b, left_a, told = tie(w_z, right_b, left_a, told)
    around = []
    for cols in (slice(512, COLS), slice(0, 512)):
        own = w_z[:, cols]
        up, down = along_y(own, 1), along_y(own, -1)
        around.append((own, up, down, along_y(up[:256], 1), along_y(down[256:], -1)))
    x_all = call(
        norm_kernel,
        shape((1024, HALF), BF),
        (where, told, norm_gain.reshape(1, WIDTH))
        + (seq_a, right_a, left_a, far_a, seq_b, right_b, left_b, far_b),
        cost=cost(1 << 22, 8 << 20),
    )

    position = (512 * (z * NY + y) + jnp.arange(512, dtype=jnp.int32)).astype(F32)
    inverse = THETA ** (-jnp.arange(64, dtype=F32) * 2.0 / HD)
    angle = position[:, None] * inverse[None, :]
    cos, sin = jnp.cos(angle), jnp.sin(angle)

    x_all, cos, sin = tie(x_all, cos, sin)
    keep, send = call(
        project_kernel,
        (shape((512, 256), F32), shape((512, 256), F32)),
        (where, x_all, *around[0]),
        (pltpu.VMEM((NZ, 256, 256), BF),),
        cost(2 * 1024 * HALF * 256, 10 << 20),
    )
    got = permute(send, lambda z, y, x, c: (z, y, x, 1 - c))
    own = call(
        rotate_kv_kernel,
        shape((ROWS, HD), BF),
        (where, keep, got, cos, sin, told),
        cost=cost(1 << 20, 2 << 20),
    )
    far = along_z(own, 1)
    keep, send = call(
        project_kernel,
        (shape((512, 512), F32), shape((512, 512), F32)),
        (where, x_all, *around[1]),
        (pltpu.VMEM((NZ, 256, 512), BF),),
        cost(2 * 1024 * HALF * 512, 10 << 20),
    )
    got = permute(send, lambda z, y, x, c: (z, y, x, 1 - c))
    later = (jnp.arange(NY) > y)[:, None, None]
    near = lax.all_to_all(jnp.where(later, own[None], far[None]), "y", 0, 0, tiled=True)
    query = call(
        rotate_q_kernel,
        shape((4, 512, HD), BF),
        (keep, got, cos, sin),
        cost=cost(4 << 20, 3 << 20),
        smem=0,
    )
    block = shape((128, 512), BF)
    scores = pltpu.VMEM((2560, 512), F32)
    out0, out1, kv, start = call(
        attend_first_kernel,
        (block, block, shape((20, 2, 128, HD), BF), shape((4, 1, 512), jnp.int32)),
        (where, query, own, near, far),
        (scores, pltpu.VMEM((128, HD), F32)),
        cost(1 << 30, 4 << 20),
        mib=16,
    )
    out0, out1 = permute(out0, back(0)), permute(out1, back(1))
    out2, out3 = call(
        attend_second_kernel,
        (block, block),
        (where, query, kv, start),
        (scores,),
        cost(1 << 33, 4 << 20),
        mib=16,
    )
    out0, out1, out2, out3 = tie(out0, out1, out2, out3)
    out2, out3 = permute(out2, back(2)), permute(out3, back(3))
    return call(
        place_kernel, shape((2, 128, 1024), BF), (where, out0, out1, out2, out3), cost=cost(0, 1 << 20)
    )


def solution(mesh):
    fine = Mesh(mesh.devices.reshape(NZ, NY, NX, NC), AXES)
    ctx = ("z", "y", "x")
    return jax.shard_map(
        local,
        mesh=fine,
        in_specs=(
            P(None, ctx, "head"),
            P(),
            P(ctx, "head"),
            P(ctx, "head"),
            P(ctx, "head"),
            P(None, ctx),
        ),
        out_specs=P(None, ctx, "head"),
        check_vma=False,
    )
```

```python
import functools

import jax
import jax.numpy as jnp
from jax import lax
from jax.experimental import pallas as pl
from jax.experimental.pallas import tpu as pltpu
from jax.sharding import Mesh, PartitionSpec as P

HD = 128
NZ, NY, NX, NC = 8, 4, 4, 2
AXES = ("z", "y", "x", "head")
THETA = 500000.0
EPS = 1e-05
WIDTH = 4096
HALF = WIDTH // 2
COLS = 6 * HD
LOG2E = 1.4426950408889634
BF = jnp.bfloat16
F32 = jnp.float32


def flat(z, y, x, c):
    return ((z * NY + y) * NX + x) * NC + c


def permute(value, to):
    pairs = [
        (flat(z, y, x, c), flat(*to(z, y, x, c)))
        for z in range(NZ)
        for y in range(NY)
        for x in range(NX)
        for c in range(NC)
    ]
    return lax.ppermute(value, AXES, pairs)


def along_x(value, by):
    return permute(value, lambda z, y, x, c: (z, y, (x + by) % NX, c))


def along_z(value, by):
    return permute(value, lambda z, y, x, c: ((z + by) % NZ, y, x, c))


def along_y(value, by):
    return permute(value, lambda z, y, x, c: (z, (y + by) % NY, x, c))


def spread(by):
    def to(z, y, x, c):
        b = (x + by) % 2
        return 2 * (z % 4) + y // 2, 2 * (y % 2) + x // 2, 2 * c + b, z // 4

    return to


def back(k):
    def to(z, y, x, c):
        return z, y, (2 * (x % 2) + c) ^ k, x // 2

    return to


VMEM = pl.BlockSpec(memory_space=pltpu.VMEM)
SMEM = pl.BlockSpec(memory_space=pltpu.SMEM)
ROWS = 8 * HD + 16


def begin_kernel(idx, hidden, query, key, value, first, second, squares):
    x = idx[2]
    for by, out in ((0, first), (1, second)):
        b = lax.rem(x + by, 2)
        out[:, :512] = query[:, pl.ds(pl.multiple_of(b * 512, 512), 512)]
        out[:, 512:640] = key[:, pl.ds(pl.multiple_of(b * 128, 128), 128)]
        out[:, 640:] = value[:, pl.ds(pl.multiple_of(b * 128, 128), 128)]

    for s in range(2):
        wide = hidden[s].astype(F32)
        total = jnp.sum(wide * wide, axis=-1, keepdims=True)
        squares[s : s + 1, :] = jnp.broadcast_to(total, (HD, HD)).T[:1, :]


def tell_kernel(squares, others, docs, out):
    scale = lax.rsqrt((squares[...] + others[...]) * (1.0 / WIDTH) + EPS)
    out[0:2, :] = docs[...].astype(F32)
    out[2:4, :] = scale


def merge_kernel(idx, first, second, out):
    odd = lax.rem(idx[2], 2) == 1
    top, low = first[...].astype(F32), second[...].astype(F32)
    out[:32, :] = jnp.where(odd, low, top).astype(BF)
    out[32:, :] = jnp.where(odd, top, low).astype(BF)


def norm_kernel(idx, gain, *refs):
    told, hidden, x_all = refs[:4], refs[4:12], refs[12]
    x, c = idx[2], idx[3]
    g = gain[:, pl.ds(pl.multiple_of(c * HALF, HALF), HALF)].astype(F32)
    for n, ref in enumerate(hidden):
        s, d = n // 4, (0, -1, 1, 2)[n % 4]
        chip = lax.rem(x + d + NX, NX)
        base = jnp.where(c == s, 0, 512) + chip * 128
        scale = jnp.broadcast_to(told[-d % NX][2 + s : 3 + s, :], (HD, HD)).T
        for t in range(4):
            rows = slice(t * 32, t * 32 + 32)
            wide = ref[rows, :].astype(F32) * scale[rows, :1] * g
            x_all[pl.ds(pl.multiple_of(base + t * 32, 32), 32), :] = wide.astype(BF)


def multiply(x_all, w_all, keep, send):
    for t in range(2):
        at = t * 256
        send[at : at + 256, :] = jnp.dot(
            x_all[512 + at : 768 + at, :], w_all, preferred_element_type=F32
        )
    for t in range(2):
        at = t * 256
        keep[at : at + 256, :] = jnp.dot(
            x_all[at : at + 256, :], w_all, preferred_element_type=F32
        )


def project_kernel(idx, x_all, own, up, down, far_up, far_down, keep, send, w_all):
    columns = own.shape[1]
    for ref, d, first in ((own, 0, 0), (up, -1, 0), (down, 1, 0), (far_up, 2, 0), (far_down, 2, 4)):
        shift = pl.multiple_of(lax.rem(idx[1] + d + NY, NY) * 64, 64)
        for z in range(ref.shape[0] // 64):
            w_all[first + z, pl.ds(shift, 64), :] = ref[z * 64 : z * 64 + 64, :]
    multiply(x_all, w_all[...].reshape(HALF, columns), keep, send)


def turned(value, cos, sin):
    cosine = jnp.concatenate([cos, cos], axis=1)
    sine = jnp.concatenate([-sin, sin], axis=1)
    return value * cosine + pltpu.roll(value, 64, 1) * sine


def rotate_kv_kernel(idx, keep, got, cos, sin, *refs):
    told, kv = refs[:4], refs[4]
    for i in range(4):
        rows = slice(i * 128, i * 128 + 128)
        value = keep[rows, :] + got[rows, :]
        at = i * 256
        kv[at : at + 128, :] = turned(value[:, :128], cos[rows, :], sin[rows, :]).astype(BF)
        kv[at + 128 : at + 256, :] = value[:, 128:].T.astype(BF)
    docs = jnp.zeros((16, HD), F32)
    row = lax.broadcasted_iota(jnp.int32, (16, HD), 0)
    for n in range(NX):
        piece = jnp.where(idx[3] == 0, told[n][0:1, :], told[n][1:2, :])
        docs = jnp.where(row == lax.rem(idx[2] - n + NX, NX), piece, docs)
    kv[1024:1040, :] = docs.astype(BF)


def rotate_q_kernel(keep, got, cos, sin, query):
    for i in range(4):
        rows = slice(i * 128, i * 128 + 128)
        for h in range(4):
            cols = slice(h * 128, h * 128 + 128)
            value = keep[rows, cols] + got[rows, cols]
            query[i, h * 128 : h * 128 + 128, :] = turned(value, cos[rows, :], sin[rows, :]).astype(BF)


def attend(idx, query, start, kv, scores, acc, outs, part):
    c = idx[3]
    m = jnp.bitwise_xor(lax.rem(idx[2], 2), part)
    first = jnp.concatenate([start[2 * m], start[2 * m + 1]], axis=1)
    rows = query[pl.ds(2 * m, 2)].reshape(1024, HD)
    sub = lax.broadcasted_iota(jnp.int32, (256, 1024), 0)
    lane = lax.broadcasted_iota(jnp.int32, (256, 1024), 1)
    lane = lax.div(lane, 512) * 128 + lax.rem(lane, 128)
    last = 8 + m
    low = jnp.minimum(lax.div(jnp.maximum(jnp.min(first), 0), 256), last)
    contract = (((1,), (1,)), ((), ()))

    def score(p):
        keys = kv[pl.ds(2 * p, 2), 0].reshape(256, HD)
        return lax.dot_general(keys, rows, contract, preferred_element_type=F32)

    def top(s):
        return jnp.max(s.reshape(32, 8, 1024), axis=0)

    def scan(p, best):
        s = jnp.where(sub >= first - 256 * p, score(p), -1e30)
        scores[pl.ds(pl.multiple_of(p * 256, 256), 256), :] = s
        return jnp.maximum(best, top(s))

    s = jnp.where((sub >= first - 256 * last) & (sub <= lane), score(last), -1e30)
    scores[pl.ds(pl.multiple_of(256 * last, 256), 256), :] = s
    best = lax.fori_loop(low, last, scan, top(s))
    best = jnp.max(best, axis=0, keepdims=True)
    acc[...] = jnp.zeros((HD, 1024), F32)

    def gather(p, total):
        s = scores[pl.ds(pl.multiple_of(p * 256, 256), 256), :]
        e = jnp.exp2((s - best) * (LOG2E * HD**-0.5))
        values = jnp.concatenate([kv[2 * p, 1], kv[2 * p + 1, 1]], axis=1)
        acc[...] += jnp.dot(values, e.astype(BF), preferred_element_type=F32)
        return total + jnp.sum(e.reshape(32, 8, 1024), axis=0)

    total = lax.fori_loop(low, last + 1, gather, jnp.zeros((8, 1024), F32))
    mixed = acc[...] / jnp.sum(total, axis=0, keepdims=True)
    for h in range(4):
        cols = slice(h * 128, h * 128 + 128)
        blocks = [mixed[:, j * 512 + h * 128 : j * 512 + h * 128 + 128].T for j in range(2)]
        outs[0][:, cols] = jnp.where(c == 0, blocks[0], blocks[1]).astype(BF)
        outs[1][:, cols] = jnp.where(c == 0, blocks[1], blocks[0]).astype(BF)


def collect_kernel(idx, *refs):
    pieces, (kv, start, docs) = refs[:5], refs[5:]
    z, y = idx[0], idx[1]
    docs[...] = jnp.zeros((128, HD), F32)
    for n, piece in enumerate(pieces):
        kv[4 * n : 4 * n + 4] = piece[:1024, :].reshape(4, 2, 128, HD)
        before = (z == 0) & (y + n < 4)
        docs[4 * n : 4 * n + 4, :] = jnp.where(before, -1.0, piece[1024:1040, :].astype(F32)[:4, :])
    columns = docs[...].T
    mine = jnp.concatenate([docs[16 + i : 17 + i, :] for i in range(4)], axis=1)
    count = jnp.zeros((8, 512), F32)
    for n in range(20):
        smaller = jnp.where(columns[:, n : n + 1] < mine, 1.0, 0.0)
        count = count + jnp.sum(smaller.reshape(16, 8, 512), axis=0)
    count = jnp.sum(count, axis=0, keepdims=True).astype(jnp.int32)
    for i in range(4):
        row = count[:, i * 128 : i * 128 + 128]
        start[i] = jnp.concatenate([row] * 4, axis=1)


def attend_kernel(part, idx, query, kv, start, out0, out1, scores, acc):
    attend(idx, query, start, kv, scores, acc, (out0, out1), part)


def place_kernel(idx, *refs):
    out = refs[4]
    for k in range(4):
        slot = jnp.bitwise_xor(idx[2], k)
        at = pl.multiple_of(lax.div(slot, 2) * 512, 512)
        out[lax.rem(slot, 2), :, pl.ds(at, 512)] = refs[k][...]


def call(kernel, shapes, args, scratch=(), cost=None, smem=1, mib=16):
    return pl.pallas_call(
        kernel,
        out_shape=shapes,
        in_specs=[SMEM] * smem + [VMEM] * (len(args) - smem),
        out_specs=jax.tree.map(lambda _: VMEM, shapes),
        scratch_shapes=list(scratch),
        cost_estimate=cost,
        compiler_params=pltpu.CompilerParams(vmem_limit_bytes=mib * 1024 * 1024),
    )(*args)


def cost(flops, nbytes):
    return pl.CostEstimate(flops=flops, bytes_accessed=nbytes, transcendentals=0)


def tie(*values):
    return lax.optimization_barrier(values)


def copies(value, axis, count):
    return lax.all_to_all(
        jnp.broadcast_to(value[None], (count, *value.shape)), axis, 0, 0, tiled=True
    )


def local(hidden_in, norm_gain, w_query, w_key, w_value, doc_ids):
    z, y, x, c = (lax.axis_index(a) for a in AXES)
    shape = jax.ShapeDtypeStruct
    where = jnp.stack([z, y, x, c]).astype(jnp.int32)

    seq_a, seq_b = hidden_in[0], hidden_in[1]
    right_a, left_b = along_x(seq_a, 1), along_x(seq_b, -1)
    right_b, left_a = along_x(seq_b, 1), along_x(seq_a, -1)

    piece = shape((32, COLS), BF)
    first, second, squares = call(
        begin_kernel,
        (piece, piece, shape((2, HD), F32)),
        (where, hidden_in, w_query, w_key, w_value),
        cost=cost(1 << 20, 2 << 20),
    )
    first, second = permute(first, spread(0)), permute(second, spread(1))
    others = permute(squares, lambda z, y, x, c: (z, y, x, 1 - c))
    told = call(
        tell_kernel,
        shape((4, HD), F32),
        (squares, others, doc_ids),
        cost=cost(0, 1 << 14),
        smem=0,
    )
    told1, told2, told3 = (along_x(told, n) for n in (1, 2, 3))
    first, second, right_a, left_b = tie(first, second, right_a, left_b)
    far_a, far_b = along_x(right_a, 1), along_x(left_b, -1)
    rows = call(merge_kernel, shape((64, COLS), BF), (where, first, second), cost=cost(0, 1 << 18))
    w_z = copies(rows, "z", NZ).reshape(512, COLS)
    w_z, right_b, left_a, told1, told2, told3 = tie(w_z, right_b, left_a, told1, told2, told3)
    told = (told, told1, told2, told3)
    around = []
    for cols in (slice(512, COLS), slice(0, 512)):
        own = w_z[:, cols]
        if around:
            own, up, down = tie(own, *around[0][1:3])
            around[0] = (around[0][0], up, down, *around[0][3:])
        up, down = along_y(own, 1), along_y(own, -1)
        around.append((own, up, down, along_y(up[:256], 1), along_y(down[256:], -1)))
    x_all = call(
        norm_kernel,
        shape((1024, HALF), BF),
        (where, norm_gain.reshape(1, WIDTH), *told)
        + (seq_a, right_a, left_a, far_a, seq_b, right_b, left_b, far_b),
        cost=cost(1 << 22, 8 << 20),
    )

    position = (512 * (z * NY + y) + jnp.arange(512, dtype=jnp.int32)).astype(F32)
    inverse = THETA ** (-jnp.arange(64, dtype=F32) * 2.0 / HD)
    angle = position[:, None] * inverse[None, :]
    cos, sin = jnp.cos(angle), jnp.sin(angle)

    x_all, cos, sin = tie(x_all, cos, sin)
    keep, send = call(
        project_kernel,
        (shape((512, 256), F32), shape((512, 256), F32)),
        (where, x_all, *around[0]),
        (pltpu.VMEM((NZ, 256, 256), BF),),
        cost(2 * 1024 * HALF * 256, 10 << 20),
    )
    got = permute(send, lambda z, y, x, c: (z, y, x, 1 - c))
    own = call(
        rotate_kv_kernel,
        shape((ROWS, HD), BF),
        (where, keep, got, cos, sin, *told),
        cost=cost(1 << 20, 2 << 20),
    )
    x_all, own = tie(x_all, own)
    earlier = [
        permute(own, lambda z, y, x, c: (*divmod((z * NY + y + n) % (NZ * NY), NY), x, c))
        for n in (4, 3, 2, 1)
    ]
    keep, send = call(
        project_kernel,
        (shape((512, 512), F32), shape((512, 512), F32)),
        (where, x_all, *around[1]),
        (pltpu.VMEM((NZ, 256, 512), BF),),
        cost(2 * 1024 * HALF * 512, 10 << 20),
    )
    got = permute(send, lambda z, y, x, c: (z, y, x, 1 - c))
    query = call(
        rotate_q_kernel,
        shape((4, 512, HD), BF),
        (keep, got, cos, sin),
        cost=cost(4 << 20, 3 << 20),
        smem=0,
    )
    kv, start = call(
        collect_kernel,
        (shape((20, 2, 128, HD), BF), shape((4, 1, 512), jnp.int32)),
        (where, *earlier, own),
        (pltpu.VMEM((128, HD), F32),),
        cost(1 << 36, 4 << 20),
    )
    block = shape((128, 512), BF)

    def blocks(part, flops):
        return call(
            functools.partial(attend_kernel, part),
            (block, block),
            (where, query, kv, start),
            (pltpu.VMEM((2560, 1024), F32), pltpu.VMEM((HD, 1024), F32)),
            cost(flops, 4 << 20),
            mib=24,
        )

    out0, out1 = blocks(0, 1 << 30)
    out0, out1 = permute(out0, back(0)), permute(out1, back(1))
    out2, out3 = blocks(1, 1 << 33)
    out0, out1, out2, out3 = tie(out0, out1, out2, out3)
    out2, out3 = permute(out2, back(2)), permute(out3, back(3))
    return call(
        place_kernel, shape((2, 128, 1024), BF), (where, out0, out1, out2, out3), cost=cost(0, 1 << 20)
    )


def solution(mesh):
    fine = Mesh(mesh.devices.reshape(NZ, NY, NX, NC), AXES)
    ctx = ("z", "y", "x")
    return jax.shard_map(
        local,
        mesh=fine,
        in_specs=(
            P(None, ctx, "head"),
            P(),
            P(ctx, "head"),
            P(ctx, "head"),
            P(ctx, "head"),
            P(None, ctx),
        ),
        out_specs=P(None, ctx, "head"),
        check_vma=False,
    )
```

```python
import jax
import jax.numpy as jnp
from jax import lax
from jax.experimental import pallas as pl
from jax.experimental.pallas import tpu as pltpu
from jax.sharding import Mesh, PartitionSpec as P

HD = 128
NZ, NY, NX, NC = 8, 4, 4, 2
AXES = ("z", "y", "x", "head")
THETA = 500000.0
EPS = 1e-05
WIDTH = 4096
HALF = WIDTH // 2
COLS = 6 * HD
LOG2E = 1.4426950408889634
BF = jnp.bfloat16
F32 = jnp.float32


def flat(z, y, x, c):
    return ((z * NY + y) * NX + x) * NC + c


def permute(value, to):
    pairs = [
        (flat(z, y, x, c), flat(*to(z, y, x, c)))
        for z in range(NZ)
        for y in range(NY)
        for x in range(NX)
        for c in range(NC)
    ]
    return lax.ppermute(value, AXES, pairs)


def along_x(value, by):
    return permute(value, lambda z, y, x, c: (z, y, (x + by) % NX, c))


def along_z(value, by):
    return permute(value, lambda z, y, x, c: ((z + by) % NZ, y, x, c))


def along_y(value, by):
    return permute(value, lambda z, y, x, c: (z, (y + by) % NY, x, c))


def spread(by):
    def to(z, y, x, c):
        b = (x + by) % 2
        return 2 * (z % 4) + y // 2, 2 * (y % 2) + x // 2, 2 * c + b, z // 4

    return to


def back(k):
    def to(z, y, x, c):
        return z, y, (2 * (x % 2) + c) ^ k, x // 2

    return to


VMEM = pl.BlockSpec(memory_space=pltpu.VMEM)
SMEM = pl.BlockSpec(memory_space=pltpu.SMEM)
ROWS = 8 * HD + 16


def begin_kernel(idx, hidden, query, key, value, first, second, squares):
    x = idx[2]
    for by, out in ((0, first), (1, second)):
        b = lax.rem(x + by, 2)
        out[:, :512] = query[:, pl.ds(pl.multiple_of(b * 512, 512), 512)]
        out[:, 512:640] = key[:, pl.ds(pl.multiple_of(b * 128, 128), 128)]
        out[:, 640:] = value[:, pl.ds(pl.multiple_of(b * 128, 128), 128)]

    for s in range(2):
        wide = hidden[s].astype(F32)
        total = jnp.sum(wide * wide, axis=-1, keepdims=True)
        squares[s : s + 1, :] = jnp.broadcast_to(total, (HD, HD)).T[:1, :]


def tell_kernel(squares, others, docs, out):
    scale = lax.rsqrt((squares[...] + others[...]) * (1.0 / WIDTH) + EPS)
    for n in range(NX):
        out[n, 0:2, :] = docs[...].astype(F32)
        out[n, 2:4, :] = scale


def merge_kernel(idx, first, second, out):
    odd = lax.rem(idx[2], 2) == 1
    top, low = first[...].astype(F32), second[...].astype(F32)
    out[:32, :] = jnp.where(odd, low, top).astype(BF)
    out[32:, :] = jnp.where(odd, top, low).astype(BF)


def norm_kernel(idx, told, gain, *refs):
    hidden, x_all = refs[:8], refs[8]
    x, c = idx[2], idx[3]
    g = gain[:, pl.ds(pl.multiple_of(c * HALF, HALF), HALF)].astype(F32)
    for n, ref in enumerate(hidden):
        s, d = n // 4, (0, -1, 1, 2)[n % 4]
        chip = lax.rem(x + d + NX, NX)
        base = jnp.where(c == s, 0, 512) + chip * 128
        scale = jnp.broadcast_to(told[chip, 2 + s : 3 + s, :], (HD, HD)).T
        for t in range(4):
            rows = slice(t * 32, t * 32 + 32)
            wide = ref[rows, :].astype(F32) * scale[rows, :1] * g
            x_all[pl.ds(pl.multiple_of(base + t * 32, 32), 32), :] = wide.astype(BF)


def multiply(x_all, w_all, keep, send):
    for t in range(2):
        at = t * 256
        send[at : at + 256, :] = jnp.dot(
            x_all[512 + at : 768 + at, :], w_all, preferred_element_type=F32
        )
    for t in range(2):
        at = t * 256
        keep[at : at + 256, :] = jnp.dot(
            x_all[at : at + 256, :], w_all, preferred_element_type=F32
        )


def project_kernel(idx, x_all, own, up, down, far_up, far_down, keep, send, w_all):
    columns = own.shape[1]
    for ref, d, first in ((own, 0, 0), (up, -1, 0), (down, 1, 0), (far_up, 2, 0), (far_down, 2, 4)):
        shift = pl.multiple_of(lax.rem(idx[1] + d + NY, NY) * 64, 64)
        for z in range(ref.shape[0] // 64):
            w_all[first + z, pl.ds(shift, 64), :] = ref[z * 64 : z * 64 + 64, :]
    multiply(x_all, w_all[...].reshape(HALF, columns), keep, send)


def turned(value, cos, sin):
    cosine = jnp.concatenate([cos, cos], axis=1)
    sine = jnp.concatenate([-sin, sin], axis=1)
    return value * cosine + pltpu.roll(value, 64, 1) * sine


def rotate_kv_kernel(idx, keep, got, cos, sin, told, kv):
    for i in range(4):
        rows = slice(i * 128, i * 128 + 128)
        value = keep[rows, :] + got[rows, :]
        at = i * 256
        kv[at : at + 128, :] = turned(value[:, :128], cos[rows, :], sin[rows, :]).astype(BF)
        kv[at + 128 : at + 256, :] = value[:, 128:].T.astype(BF)
    docs = jnp.where(idx[3] == 0, told[:, 0, :], told[:, 1, :])
    kv[1024:1040, :] = jnp.concatenate([docs, jnp.zeros((12, HD), F32)], axis=0).astype(BF)


def rotate_q_kernel(keep, got, cos, sin, query):
    for i in range(4):
        rows = slice(i * 128, i * 128 + 128)
        for h in range(4):
            cols = slice(h * 128, h * 128 + 128)
            value = keep[rows, cols] + got[rows, cols]
            query[i, h * 128 : h * 128 + 128, :] = turned(value, cos[rows, :], sin[rows, :]).astype(BF)


def attend(idx, query, start, kv, scores, acc, outs, part):
    c = idx[3]
    m = jnp.bitwise_xor(lax.rem(idx[2], 2), part)
    first = jnp.concatenate([start[2 * m], start[2 * m + 1]], axis=1)
    rows = query[pl.ds(2 * m, 2)].reshape(1024, HD)
    sub = lax.broadcasted_iota(jnp.int32, (256, 1024), 0)
    lane = lax.broadcasted_iota(jnp.int32, (256, 1024), 1)
    lane = lax.div(lane, 512) * 128 + lax.rem(lane, 128)
    last = 8 + m
    low = jnp.minimum(lax.div(jnp.maximum(jnp.min(first), 0), 256), last)
    contract = (((1,), (1,)), ((), ()))

    def score(p):
        keys = kv[pl.ds(2 * p, 2), 0].reshape(256, HD)
        return lax.dot_general(keys, rows, contract, preferred_element_type=F32)

    def top(s):
        return jnp.max(s.reshape(32, 8, 1024), axis=0)

    def scan(p, best):
        s = jnp.where(sub >= first - 256 * p, score(p), -1e30)
        scores[pl.ds(pl.multiple_of(p * 256, 256), 256), :] = s
        return jnp.maximum(best, top(s))

    s = jnp.where((sub >= first - 256 * last) & (sub <= lane), score(last), -1e30)
    scores[pl.ds(pl.multiple_of(256 * last, 256), 256), :] = s
    best = lax.fori_loop(low, last, scan, top(s))
    best = jnp.max(best, axis=0, keepdims=True)
    acc[...] = jnp.zeros((HD, 1024), F32)

    def gather(p, total):
        s = scores[pl.ds(pl.multiple_of(p * 256, 256), 256), :]
        e = jnp.exp2((s - best) * (LOG2E * HD**-0.5))
        values = jnp.concatenate([kv[2 * p, 1], kv[2 * p + 1, 1]], axis=1)
        acc[...] += jnp.dot(values, e.astype(BF), preferred_element_type=F32)
        return total + jnp.sum(e.reshape(32, 8, 1024), axis=0)

    total = lax.fori_loop(low, last + 1, gather, jnp.zeros((8, 1024), F32))
    mixed = acc[...] / jnp.sum(total, axis=0, keepdims=True)
    for h in range(4):
        cols = slice(h * 128, h * 128 + 128)
        blocks = [mixed[:, j * 512 + h * 128 : j * 512 + h * 128 + 128].T for j in range(2)]
        outs[0][:, cols] = jnp.where(c == 0, blocks[0], blocks[1]).astype(BF)
        outs[1][:, cols] = jnp.where(c == 0, blocks[1], blocks[0]).astype(BF)


def collect_kernel(idx, *refs):
    pieces, (kv, start, docs) = refs[:5], refs[5:]
    z, y = idx[0], idx[1]
    docs[...] = jnp.zeros((128, HD), F32)
    for n, piece in enumerate(pieces):
        kv[4 * n : 4 * n + 4] = piece[:1024, :].reshape(4, 2, 128, HD)
        before = (z == 0) & (y + n < 4)
        docs[4 * n : 4 * n + 4, :] = jnp.where(before, -1.0, piece[1024:1040, :].astype(F32)[:4, :])
    columns = docs[...].T
    mine = jnp.concatenate([docs[16 + i : 17 + i, :] for i in range(4)], axis=1)
    count = jnp.zeros((8, 512), F32)
    for n in range(20):
        smaller = jnp.where(columns[:, n : n + 1] < mine, 1.0, 0.0)
        count = count + jnp.sum(smaller.reshape(16, 8, 512), axis=0)
    count = jnp.sum(count, axis=0, keepdims=True).astype(jnp.int32)
    for i in range(4):
        row = count[:, i * 128 : i * 128 + 128]
        start[i] = jnp.concatenate([row] * 4, axis=1)


def attend_kernel(idx, query, kv, start, out0, out1, out2, out3, scores, acc):
    attend(idx, query, start, kv, scores, acc, (out0, out1), 0)
    attend(idx, query, start, kv, scores, acc, (out2, out3), 1)


def place_kernel(idx, *refs):
    out = refs[4]
    for k in range(4):
        slot = jnp.bitwise_xor(idx[2], k)
        at = pl.multiple_of(lax.div(slot, 2) * 512, 512)
        out[lax.rem(slot, 2), :, pl.ds(at, 512)] = refs[k][...]


def call(kernel, shapes, args, scratch=(), cost=None, smem=1, mib=16):
    return pl.pallas_call(
        kernel,
        out_shape=shapes,
        in_specs=[SMEM] * smem + [VMEM] * (len(args) - smem),
        out_specs=jax.tree.map(lambda _: VMEM, shapes),
        scratch_shapes=list(scratch),
        cost_estimate=cost,
        compiler_params=pltpu.CompilerParams(vmem_limit_bytes=mib * 1024 * 1024),
    )(*args)


def cost(flops, nbytes):
    return pl.CostEstimate(flops=flops, bytes_accessed=nbytes, transcendentals=0)


def tie(*values):
    return lax.optimization_barrier(values)


def copies(value, axis, count):
    return lax.all_to_all(
        jnp.broadcast_to(value[None], (count, *value.shape)), axis, 0, 0, tiled=True
    )


def local(hidden_in, norm_gain, w_query, w_key, w_value, doc_ids):
    z, y, x, c = (lax.axis_index(a) for a in AXES)
    shape = jax.ShapeDtypeStruct
    where = jnp.stack([z, y, x, c]).astype(jnp.int32)

    seq_a, seq_b = hidden_in[0], hidden_in[1]
    right_a, left_b = along_x(seq_a, 1), along_x(seq_b, -1)
    right_b, left_a = along_x(seq_b, 1), along_x(seq_a, -1)

    piece = shape((32, COLS), BF)
    first, second, squares = call(
        begin_kernel,
        (piece, piece, shape((2, HD), F32)),
        (where, hidden_in, w_query, w_key, w_value),
        cost=cost(1 << 20, 2 << 20),
    )
    first, second = permute(first, spread(0)), permute(second, spread(1))
    others = permute(squares, lambda z, y, x, c: (z, y, x, 1 - c))
    told = call(
        tell_kernel,
        shape((NX, 4, HD), F32),
        (squares, others, doc_ids),
        cost=cost(0, 1 << 14),
        smem=0,
    )
    told = lax.all_to_all(told, "x", 0, 0, tiled=True)
    first, second, right_a, left_b = tie(first, second, right_a, left_b)
    far_a, far_b = along_x(right_a, 1), along_x(left_b, -1)
    rows = call(merge_kernel, shape((64, COLS), BF), (where, first, second), cost=cost(0, 1 << 18))
    w_z = copies(rows, "z", NZ).reshape(512, COLS)
    w_z, right_b, left_a, told = tie(w_z, right_b, left_a, told)
    around = []
    for cols in (slice(512, COLS), slice(0, 512)):
        own = w_z[:, cols]
        if around:
            own, up, down = tie(own, *around[0][1:3])
            around[0] = (around[0][0], up, down, *around[0][3:])
        up, down = along_y(own, 1), along_y(own, -1)
        around.append((own, up, down, along_y(up[:256], 1), along_y(down[256:], -1)))
    x_all = call(
        norm_kernel,
        shape((1024, HALF), BF),
        (where, told, norm_gain.reshape(1, WIDTH))
        + (seq_a, right_a, left_a, far_a, seq_b, right_b, left_b, far_b),
        cost=cost(1 << 22, 8 << 20),
    )

    position = (512 * (z * NY + y) + jnp.arange(512, dtype=jnp.int32)).astype(F32)
    inverse = THETA ** (-jnp.arange(64, dtype=F32) * 2.0 / HD)
    angle = position[:, None] * inverse[None, :]
    cos, sin = jnp.cos(angle), jnp.sin(angle)

    x_all, cos, sin = tie(x_all, cos, sin)
    keep, send = call(
        project_kernel,
        (shape((512, 256), F32), shape((512, 256), F32)),
        (where, x_all, *around[0]),
        (pltpu.VMEM((NZ, 256, 256), BF),),
        cost(2 * 1024 * HALF * 256, 10 << 20),
    )
    got = permute(send, lambda z, y, x, c: (z, y, x, 1 - c))
    own = call(
        rotate_kv_kernel,
        shape((ROWS, HD), BF),
        (where, keep, got, cos, sin, told),
        cost=cost(1 << 20, 2 << 20),
    )
    x_all, own = tie(x_all, own)
    earlier = [
        permute(own, lambda z, y, x, c: (*divmod((z * NY + y + n) % (NZ * NY), NY), x, c))
        for n in (4, 3, 2, 1)
    ]
    keep, send = call(
        project_kernel,
        (shape((512, 512), F32), shape((512, 512), F32)),
        (where, x_all, *around[1]),
        (pltpu.VMEM((NZ, 256, 512), BF),),
        cost(2 * 1024 * HALF * 512, 10 << 20),
    )
    got = permute(send, lambda z, y, x, c: (z, y, x, 1 - c))
    query = call(
        rotate_q_kernel,
        shape((4, 512, HD), BF),
        (keep, got, cos, sin),
        cost=cost(4 << 20, 3 << 20),
        smem=0,
    )
    kv, start = call(
        collect_kernel,
        (shape((20, 2, 128, HD), BF), shape((4, 1, 512), jnp.int32)),
        (where, *earlier, own),
        (pltpu.VMEM((128, HD), F32),),
        cost(1 << 36, 4 << 20),
    )
    block = shape((128, 512), BF)
    outs = call(
        attend_kernel,
        (block,) * 4,
        (where, query, kv, start),
        (pltpu.VMEM((2560, 1024), F32), pltpu.VMEM((HD, 1024), F32)),
        cost(1 << 31, 4 << 20),
        mib=24,
    )
    outs = [permute(out, back(k)) for k, out in enumerate(outs)]
    return call(
        place_kernel, shape((2, 128, 1024), BF), (where, *outs), cost=cost(0, 1 << 20)
    )


def solution(mesh):
    fine = Mesh(mesh.devices.reshape(NZ, NY, NX, NC), AXES)
    ctx = ("z", "y", "x")
    return jax.shard_map(
        local,
        mesh=fine,
        in_specs=(
            P(None, ctx, "head"),
            P(),
            P(ctx, "head"),
            P(ctx, "head"),
            P(ctx, "head"),
            P(None, ctx),
        ),
        out_specs=P(None, ctx, "head"),
        check_vma=False,
    )
```

```python
import jax
import jax.numpy as jnp
from jax import lax
from jax.experimental import pallas as pl
from jax.experimental.pallas import tpu as pltpu
from jax.sharding import Mesh, PartitionSpec as P

HD = 128
NZ, NY, NX, NC = 8, 4, 4, 2
AXES = ("z", "y", "x", "head")
THETA = 500000.0
EPS = 1e-05
WIDTH = 4096
HALF = WIDTH // 2
COLS = 6 * HD
LOG2E = 1.4426950408889634
BF = jnp.bfloat16
F32 = jnp.float32


def flat(z, y, x, c):
    return ((z * NY + y) * NX + x) * NC + c


def permute(value, to):
    pairs = [
        (flat(z, y, x, c), flat(*to(z, y, x, c)))
        for z in range(NZ)
        for y in range(NY)
        for x in range(NX)
        for c in range(NC)
    ]
    return lax.ppermute(value, AXES, pairs)


def along_x(value, by):
    return permute(value, lambda z, y, x, c: (z, y, (x + by) % NX, c))


def along_z(value, by):
    return permute(value, lambda z, y, x, c: ((z + by) % NZ, y, x, c))


def along_y(value, by):
    return permute(value, lambda z, y, x, c: (z, (y + by) % NY, x, c))


def spread(by):
    def to(z, y, x, c):
        b = (x + by) % 2
        return 2 * (z % 4) + y // 2, 2 * (y % 2) + x // 2, 2 * c + b, z // 4

    return to


def back(k):
    def to(z, y, x, c):
        return z, y, (2 * (x % 2) + c) ^ k, x // 2

    return to


VMEM = pl.BlockSpec(memory_space=pltpu.VMEM)
SMEM = pl.BlockSpec(memory_space=pltpu.SMEM)
ROWS = 8 * HD + 16


def pack_kernel(idx, query, key, value, first, second):
    x = idx[2]
    for by, out in ((0, first), (1, second)):
        b = lax.rem(x + by, 2)
        out[:, :512] = query[:, pl.ds(pl.multiple_of(b * 512, 512), 512)]
        out[:, 512:640] = key[:, pl.ds(pl.multiple_of(b * 128, 128), 128)]
        out[:, 640:] = value[:, pl.ds(pl.multiple_of(b * 128, 128), 128)]


def squares_kernel(hidden, squares):
    for s in range(2):
        wide = hidden[s].astype(F32)
        total = jnp.sum(wide * wide, axis=-1, keepdims=True)
        squares[s * 128 : s * 128 + 128, :] = jnp.broadcast_to(total, (HD, HD))


def norm_kernel(idx, hidden, squares, others, docs, gain, seq_a, seq_b):
    g = gain[:, pl.ds(pl.multiple_of(idx[3] * HALF, HALF), HALF)].astype(F32)
    for s, out in ((0, seq_a), (1, seq_b)):
        for t in range(4):
            rows = slice(t * 32, t * 32 + 32)
            both = slice(s * 128 + t * 32, s * 128 + t * 32 + 32)
            scale = lax.rsqrt((squares[both, :] + others[both, :]) * (1.0 / WIDTH) + EPS)
            wide = hidden[s, rows, :].astype(F32)
            out[rows, :] = (wide * scale[:, :1] * g).astype(BF)
    extra = jnp.concatenate([docs[...].astype(F32), jnp.zeros((14, HD), F32)], axis=0)
    seq_a[128:144, :HD] = extra.astype(BF)
    seq_a[128:144, HD:] = jnp.zeros((16, HALF - HD), BF)


def merge_kernel(idx, first, second, out):
    odd = lax.rem(idx[2], 2) == 1
    top, low = first[...].astype(F32), second[...].astype(F32)
    out[:32, :] = jnp.where(odd, low, top).astype(BF)
    out[32:, :] = jnp.where(odd, top, low).astype(BF)


def stack_kernel(idx, *refs):
    hidden, (x_all, docs) = refs[:8], refs[8:]
    x, c = idx[2], idx[3]
    row = lax.broadcasted_iota(jnp.int32, (16, HD), 0)
    found = jnp.zeros((16, HD), F32)
    for n, ref in enumerate(hidden):
        s, d = n // 4, (0, -1, 1, 2)[n % 4]
        chip = lax.rem(x + d + NX, NX)
        base = jnp.where(c == s, 0, 512) + chip * 128
        x_all[pl.ds(pl.multiple_of(base, 128), 128), :] = ref[:128, :]
        if s == 0:
            tile = ref[128:144, :HD].astype(F32)
            mine = jnp.where(c == 0, tile[0:1, :], tile[1:2, :])
            found = jnp.where(row == chip, mine, found)
    docs[...] = found.astype(BF)


def multiply(x_all, w_all, keep, send):
    for t in range(2):
        at = t * 256
        send[at : at + 256, :] = jnp.dot(
            x_all[512 + at : 768 + at, :], w_all, preferred_element_type=F32
        )
    for t in range(2):
        at = t * 256
        keep[at : at + 256, :] = jnp.dot(
            x_all[at : at + 256, :], w_all, preferred_element_type=F32
        )


def project_kernel(idx, x_all, own, up, down, far_up, far_down, keep, send, w_all):
    columns = own.shape[1]
    for ref, d, first in ((own, 0, 0), (up, -1, 0), (down, 1, 0), (far_up, 2, 0), (far_down, 2, 4)):
        shift = pl.multiple_of(lax.rem(idx[1] + d + NY, NY) * 64, 64)
        for z in range(ref.shape[0] // 64):
            w_all[first + z, pl.ds(shift, 64), :] = ref[z * 64 : z * 64 + 64, :]
    multiply(x_all, w_all[...].reshape(HALF, columns), keep, send)


def turned(value, cos, sin):
    cosine = jnp.concatenate([cos, cos], axis=1)
    sine = jnp.concatenate([-sin, sin], axis=1)
    return value * cosine + pltpu.roll(value, 64, 1) * sine


def rotate_kv_kernel(keep, got, cos, sin, docs, kv):
    for i in range(4):
        rows = slice(i * 128, i * 128 + 128)
        value = keep[rows, :] + got[rows, :]
        at = i * 256
        kv[at : at + 128, :] = turned(value[:, :128], cos[rows, :], sin[rows, :]).astype(BF)
        kv[at + 128 : at + 256, :] = value[:, 128:].T.astype(BF)
    kv[1024:1040, :] = docs[...]


def rotate_q_kernel(keep, got, cos, sin, query):
    for i in range(4):
        rows = slice(i * 128, i * 128 + 128)
        for h in range(4):
            cols = slice(h * 128, h * 128 + 128)
            value = keep[rows, cols] + got[rows, cols]
            query[i, h * 128 : h * 128 + 128, :] = turned(value, cos[rows, :], sin[rows, :]).astype(BF)


def attend(idx, query, start, kv, scores, acc, outs, part):
    c = idx[3]
    m = jnp.bitwise_xor(lax.rem(idx[2], 2), part)
    first = jnp.concatenate([start[2 * m], start[2 * m + 1]], axis=1)
    rows = query[pl.ds(2 * m, 2)].reshape(1024, HD)
    sub = lax.broadcasted_iota(jnp.int32, (256, 1024), 0)
    lane = lax.broadcasted_iota(jnp.int32, (256, 1024), 1)
    lane = lax.div(lane, 512) * 128 + lax.rem(lane, 128)
    last = 8 + m
    low = jnp.minimum(lax.div(jnp.maximum(jnp.min(first), 0), 256), last)
    contract = (((1,), (1,)), ((), ()))

    def score(p):
        keys = kv[pl.ds(2 * p, 2), 0].reshape(256, HD)
        return lax.dot_general(keys, rows, contract, preferred_element_type=F32)

    def top(s):
        return jnp.max(s.reshape(32, 8, 1024), axis=0)

    def keep(p, s, best):
        scores[pl.ds(pl.multiple_of(p * 256, 256), 256), :] = s
        return jnp.maximum(best, top(s))

    def masked(p, best):
        return keep(p, jnp.where(sub >= first - 256 * p, score(p), -1e30), best)

    def whole(p, best):
        return keep(p, score(p), best)

    s = jnp.where((sub >= first - 256 * last) & (sub <= lane), score(last), -1e30)
    scores[pl.ds(pl.multiple_of(256 * last, 256), 256), :] = s
    inside = jnp.clip(lax.div(jnp.max(first) + 255, 256), low, last)
    best = lax.fori_loop(low, inside, masked, top(s))
    best = lax.fori_loop(inside, last, whole, best)
    best = jnp.max(best, axis=0, keepdims=True)
    acc[...] = jnp.zeros((HD, 1024), F32)

    def gather(p, total):
        s = scores[pl.ds(pl.multiple_of(p * 256, 256), 256), :]
        e = jnp.exp2((s - best) * (LOG2E * HD**-0.5))
        values = jnp.concatenate([kv[2 * p, 1], kv[2 * p + 1, 1]], axis=1)
        acc[...] += jnp.dot(values, e.astype(BF), preferred_element_type=F32)
        return total + jnp.sum(e.reshape(32, 8, 1024), axis=0)

    total = lax.fori_loop(low, last + 1, gather, jnp.zeros((8, 1024), F32))
    mixed = acc[...] / jnp.sum(total, axis=0, keepdims=True)
    for h in range(4):
        cols = slice(h * 128, h * 128 + 128)
        blocks = [mixed[:, j * 512 + h * 128 : j * 512 + h * 128 + 128].T for j in range(2)]
        outs[0][:, cols] = jnp.where(c == 0, blocks[0], blocks[1]).astype(BF)
        outs[1][:, cols] = jnp.where(c == 0, blocks[1], blocks[0]).astype(BF)


def collect_kernel(idx, *refs):
    pieces, (kv, start, docs) = refs[:5], refs[5:]
    z, y = idx[0], idx[1]
    docs[...] = jnp.zeros((128, HD), F32)
    for n, piece in enumerate(pieces):
        kv[4 * n : 4 * n + 4] = piece[:1024, :].reshape(4, 2, 128, HD)
        before = (z == 0) & (y + n < 4)
        docs[4 * n : 4 * n + 4, :] = jnp.where(before, -1.0, piece[1024:1040, :].astype(F32)[:4, :])
    columns = docs[...].T
    mine = jnp.concatenate([docs[16 + i : 17 + i, :] for i in range(4)], axis=1)
    count = jnp.zeros((8, 512), F32)
    for n in range(20):
        smaller = jnp.where(columns[:, n : n + 1] < mine, 1.0, 0.0)
        count = count + jnp.sum(smaller.reshape(16, 8, 512), axis=0)
    count = jnp.sum(count, axis=0, keepdims=True).astype(jnp.int32)
    for i in range(4):
        row = count[:, i * 128 : i * 128 + 128]
        start[i] = jnp.concatenate([row] * 4, axis=1)


def attend_kernel(idx, query, kv, start, out0, out1, out2, out3, scores, acc):
    attend(idx, query, start, kv, scores, acc, (out0, out1), 0)
    attend(idx, query, start, kv, scores, acc, (out2, out3), 1)


def place_kernel(idx, *refs):
    out = refs[4]
    for k in range(4):
        slot = jnp.bitwise_xor(idx[2], k)
        at = pl.multiple_of(lax.div(slot, 2) * 512, 512)
        out[lax.rem(slot, 2), :, pl.ds(at, 512)] = refs[k][...]


def call(kernel, shapes, args, scratch=(), cost=None, smem=1, mib=16):
    return pl.pallas_call(
        kernel,
        out_shape=shapes,
        in_specs=[SMEM] * smem + [VMEM] * (len(args) - smem),
        out_specs=jax.tree.map(lambda _: VMEM, shapes),
        scratch_shapes=list(scratch),
        cost_estimate=cost,
        compiler_params=pltpu.CompilerParams(vmem_limit_bytes=mib * 1024 * 1024),
    )(*args)


def cost(flops, nbytes):
    return pl.CostEstimate(flops=flops, bytes_accessed=nbytes, transcendentals=0)


def tie(*values):
    return lax.optimization_barrier(values)


def copies(value, axis, count):
    return lax.all_to_all(
        jnp.broadcast_to(value[None], (count, *value.shape)), axis, 0, 0, tiled=True
    )


def local(hidden_in, norm_gain, w_query, w_key, w_value, doc_ids):
    z, y, x, c = (lax.axis_index(a) for a in AXES)
    shape = jax.ShapeDtypeStruct
    where = jnp.stack([z, y, x, c]).astype(jnp.int32)

    piece = shape((32, COLS), BF)
    first, second = call(
        pack_kernel, (piece, piece), (where, w_query, w_key, w_value), cost=cost(0, 1 << 18)
    )
    first, second = permute(first, spread(0)), permute(second, spread(1))
    squares = call(
        squares_kernel,
        shape((256, HD), F32),
        (hidden_in,),
        cost=cost(1 << 20, 2 << 20),
        smem=0,
    )
    others = permute(squares, lambda z, y, x, c: (z, y, x, 1 - c))

    seq_a, seq_b = call(
        norm_kernel,
        (shape((144, HALF), BF), shape((128, HALF), BF)),
        (where, hidden_in, squares, others, doc_ids, norm_gain.reshape(1, WIDTH)),
        cost=cost(1 << 20, 3 << 20),
    )
    first, second, seq_a, seq_b = tie(first, second, seq_a, seq_b)
    right_a, left_b = along_x(seq_a, 1), along_x(seq_b, -1)
    right_b, left_a = along_x(seq_b, 1), along_x(seq_a, -1)
    rows = call(merge_kernel, shape((64, COLS), BF), (where, first, second), cost=cost(0, 1 << 18))
    w_z = copies(rows, "z", NZ).reshape(512, COLS)
    w_z, right_a, left_b = tie(w_z, right_a, left_b)
    far_a, far_b = along_x(right_a, 1), along_x(left_b, -1)

    kv0, q0 = w_z[:, 512:], w_z[:, :512]
    kv_up, kv_down = along_y(kv0, 1), along_y(kv0, -1)
    kv_up, kv_down, right_b, left_a = tie(kv_up, kv_down, right_b, left_a)
    kv_far_up, kv_far_down = along_y(kv_up[:256], 1), along_y(kv_down[256:], -1)
    q0, kv_far_up, kv_far_down = tie(q0, kv_far_up, kv_far_down)
    q_up, q_down = along_y(q0, 1), along_y(q0, -1)
    q_far_up, q_far_down = along_y(q_up[:256], 1), along_y(q_down[256:], -1)
    x_all, docs = call(
        stack_kernel,
        (shape((1024, HALF), BF), shape((16, HD), BF)),
        (where, seq_a, right_a, left_a, far_a, seq_b, right_b, left_b, far_b),
        cost=cost(0, 8 << 20),
    )

    position = (512 * (z * NY + y) + jnp.arange(512, dtype=jnp.int32)).astype(F32)
    inverse = THETA ** (-jnp.arange(64, dtype=F32) * 2.0 / HD)
    angle = position[:, None] * inverse[None, :]
    cos, sin = jnp.cos(angle), jnp.sin(angle)

    x_all, cos, sin = tie(x_all, cos, sin)
    keep, send = call(
        project_kernel,
        (shape((512, 256), F32), shape((512, 256), F32)),
        (where, x_all, kv0, kv_up, kv_down, kv_far_up, kv_far_down),
        (pltpu.VMEM((NZ, 256, 256), BF),),
        cost(2 * 1024 * HALF * 256, 10 << 20),
    )
    got = permute(send, lambda z, y, x, c: (z, y, x, 1 - c))
    own = call(
        rotate_kv_kernel,
        shape((ROWS, HD), BF),
        (keep, got, cos, sin, docs),
        cost=cost(1 << 20, 2 << 20),
        smem=0,
    )
    x_all, own = tie(x_all, own)
    earlier = [
        permute(own, lambda z, y, x, c: (*divmod((z * NY + y + n) % (NZ * NY), NY), x, c))
        for n in (4, 3, 2, 1)
    ]
    keep, send = call(
        project_kernel,
        (shape((512, 512), F32), shape((512, 512), F32)),
        (where, x_all, q0, q_up, q_down, q_far_up, q_far_down),
        (pltpu.VMEM((NZ, 256, 512), BF),),
        cost(0, 0),
    )
    got = permute(send, lambda z, y, x, c: (z, y, x, 1 - c))
    query = call(
        rotate_q_kernel,
        shape((4, 512, HD), BF),
        (keep, got, cos, sin),
        cost=cost(4 << 20, 3 << 20),
        smem=0,
    )
    kv, start = call(
        collect_kernel,
        (shape((20, 2, 128, HD), BF), shape((4, 1, 512), jnp.int32)),
        (where, *earlier, own),
        (pltpu.VMEM((128, HD), F32),),
        cost(1 << 36, 4 << 20),
    )
    block = shape((128, 512), BF)
    outs = call(
        attend_kernel,
        (block,) * 4,
        (where, query, kv, start),
        (pltpu.VMEM((2560, 1024), F32), pltpu.VMEM((HD, 1024), F32)),
        cost(1 << 31, 4 << 20),
        mib=24,
    )
    outs = [permute(out, back(k)) for k, out in enumerate(outs)]
    return call(
        place_kernel, shape((2, 128, 1024), BF), (where, *outs), cost=cost(0, 1 << 20)
    )


def solution(mesh):
    fine = Mesh(mesh.devices.reshape(NZ, NY, NX, NC), AXES)
    ctx = ("z", "y", "x")
    return jax.shard_map(
        local,
        mesh=fine,
        in_specs=(
            P(None, ctx, "head"),
            P(),
            P(ctx, "head"),
            P(ctx, "head"),
            P(ctx, "head"),
            P(None, ctx),
        ),
        out_specs=P(None, ctx, "head"),
        check_vma=False,
    )
```

```python
import jax
import jax.numpy as jnp
from jax import lax
from jax.experimental import pallas as pl
from jax.experimental.pallas import tpu as pltpu
from jax.sharding import Mesh, PartitionSpec as P

HD = 128
NZ, NY, NX, NC = 8, 4, 4, 2
AXES = ("z", "y", "x", "head")
THETA = 500000.0
EPS = 1e-05
WIDTH = 4096
HALF = WIDTH // 2
COLS = 6 * HD
LOG2E = 1.4426950408889634
BF = jnp.bfloat16
F32 = jnp.float32


def flat(z, y, x, c):
    return ((z * NY + y) * NX + x) * NC + c


def permute(value, to):
    pairs = [
        (flat(z, y, x, c), flat(*to(z, y, x, c)))
        for z in range(NZ)
        for y in range(NY)
        for x in range(NX)
        for c in range(NC)
    ]
    return lax.ppermute(value, AXES, pairs)


def along_x(value, by):
    return permute(value, lambda z, y, x, c: (z, y, (x + by) % NX, c))


def along_z(value, by):
    return permute(value, lambda z, y, x, c: ((z + by) % NZ, y, x, c))


def along_y(value, by):
    return permute(value, lambda z, y, x, c: (z, (y + by) % NY, x, c))


def spread(by):
    def to(z, y, x, c):
        b = (x + by) % 2
        return 2 * (z % 4) + y // 2, 2 * (y % 2) + x // 2, 2 * c + b, z // 4

    return to


def back(k):
    def to(z, y, x, c):
        return z, y, (2 * (x % 2) + c) ^ k, x // 2

    return to


VMEM = pl.BlockSpec(memory_space=pltpu.VMEM)
SMEM = pl.BlockSpec(memory_space=pltpu.SMEM)
ROWS = 8 * HD + 16


def pack_kernel(idx, query, key, value, first, second):
    x = idx[2]
    for by, out in ((0, first), (1, second)):
        b = lax.rem(x + by, 2)
        out[:, :512] = query[:, pl.ds(pl.multiple_of(b * 512, 512), 512)]
        out[:, 512:640] = key[:, pl.ds(pl.multiple_of(b * 128, 128), 128)]
        out[:, 640:] = value[:, pl.ds(pl.multiple_of(b * 128, 128), 128)]


def squares_kernel(hidden, squares):
    for s in range(2):
        wide = hidden[s].astype(F32)
        total = jnp.sum(wide * wide, axis=-1, keepdims=True)
        squares[s * 128 : s * 128 + 128, :] = jnp.broadcast_to(total, (HD, HD))


def norm_kernel(idx, hidden, squares, others, docs, gain, seq_a, seq_b):
    g = gain[:, pl.ds(pl.multiple_of(idx[3] * HALF, HALF), HALF)].astype(F32)
    for s, out in ((0, seq_a), (1, seq_b)):
        for t in range(4):
            rows = slice(t * 32, t * 32 + 32)
            both = slice(s * 128 + t * 32, s * 128 + t * 32 + 32)
            scale = lax.rsqrt((squares[both, :] + others[both, :]) * (1.0 / WIDTH) + EPS)
            wide = hidden[s, rows, :].astype(F32)
            out[rows, :] = (wide * scale[:, :1] * g).astype(BF)
    extra = jnp.concatenate([docs[...].astype(F32), jnp.zeros((14, HD), F32)], axis=0)
    seq_a[128:144, :HD] = extra.astype(BF)
    seq_a[128:144, HD:] = jnp.zeros((16, HALF - HD), BF)


def merge_kernel(idx, first, second, out):
    odd = lax.rem(idx[2], 2) == 1
    top, low = first[...].astype(F32), second[...].astype(F32)
    out[:32, :] = jnp.where(odd, low, top).astype(BF)
    out[32:, :] = jnp.where(odd, top, low).astype(BF)


def stack_kernel(idx, *refs):
    hidden, (x_all, docs) = refs[:8], refs[8:]
    x, c = idx[2], idx[3]
    row = lax.broadcasted_iota(jnp.int32, (16, HD), 0)
    found = jnp.zeros((16, HD), F32)
    for n, ref in enumerate(hidden):
        s, d = n // 4, (0, -1, 1, 2)[n % 4]
        chip = lax.rem(x + d + NX, NX)
        base = jnp.where(c == s, 0, 512) + chip * 128
        x_all[pl.ds(pl.multiple_of(base, 128), 128), :] = ref[:128, :]
        if s == 0:
            tile = ref[128:144, :HD].astype(F32)
            mine = jnp.where(c == 0, tile[0:1, :], tile[1:2, :])
            found = jnp.where(row == chip, mine, found)
    docs[...] = found.astype(BF)


def multiply(x_all, w_all, keep, send):
    for t in range(2):
        at = t * 256
        send[at : at + 256, :] = jnp.dot(
            x_all[512 + at : 768 + at, :], w_all, preferred_element_type=F32
        )
    for t in range(2):
        at = t * 256
        keep[at : at + 256, :] = jnp.dot(
            x_all[at : at + 256, :], w_all, preferred_element_type=F32
        )


def project_kernel(idx, x_all, own, up, down, far, keep, send, w_all):
    for ref, d in ((own, 0), (up, -1), (down, 1), (far, 2)):
        shift = pl.multiple_of(lax.rem(idx[1] + d + NY, NY) * 64, 64)
        for z in range(NZ):
            w_all[z, pl.ds(shift, 64), :] = ref[z * 64 : z * 64 + 64, :]
    multiply(x_all, w_all[...].reshape(HALF, own.shape[1]), keep, send)


def turned(value, cos, sin):
    cosine = jnp.concatenate([cos, cos], axis=1)
    sine = jnp.concatenate([-sin, sin], axis=1)
    return value * cosine + pltpu.roll(value, 64, 1) * sine


def rotate_kv_kernel(keep, got, cos, sin, docs, kv):
    for i in range(4):
        rows = slice(i * 128, i * 128 + 128)
        value = keep[rows, :] + got[rows, :]
        at = i * 256
        kv[at : at + 128, :] = turned(value[:, :128], cos[rows, :], sin[rows, :]).astype(BF)
        kv[at + 128 : at + 256, :] = value[:, 128:].T.astype(BF)
    kv[1024:1040, :] = docs[...]


def rotate_q_kernel(keep, got, cos, sin, query):
    for i in range(4):
        rows = slice(i * 128, i * 128 + 128)
        for h in range(4):
            cols = slice(h * 128, h * 128 + 128)
            value = keep[rows, cols] + got[rows, cols]
            query[i, h * 128 : h * 128 + 128, :] = turned(value, cos[rows, :], sin[rows, :]).astype(BF)


def attend(idx, query, start, kv, scores, acc, outs, part):
    c = idx[3]
    m = jnp.bitwise_xor(lax.rem(idx[2], 2), part)
    first = jnp.concatenate([start[2 * m], start[2 * m + 1]], axis=1)
    rows = query[pl.ds(2 * m, 2)].reshape(1024, HD)
    sub = lax.broadcasted_iota(jnp.int32, (256, 1024), 0)
    lane = lax.broadcasted_iota(jnp.int32, (256, 1024), 1)
    lane = lax.div(lane, 512) * 128 + lax.rem(lane, 128)
    last = 8 + m
    low = jnp.minimum(lax.div(jnp.maximum(jnp.min(first), 0), 256), last)
    contract = (((1,), (1,)), ((), ()))

    def score(p):
        keys = kv[pl.ds(2 * p, 2), 0].reshape(256, HD)
        return lax.dot_general(keys, rows, contract, preferred_element_type=F32)

    def top(s):
        return jnp.max(s.reshape(32, 8, 1024), axis=0)

    def keep(p, s, best):
        scores[pl.ds(pl.multiple_of(p * 256, 256), 256), :] = s
        return jnp.maximum(best, top(s))

    def masked(p, best):
        return keep(p, jnp.where(sub >= first - 256 * p, score(p), -1e30), best)

    def whole(p, best):
        return keep(p, score(p), best)

    s = jnp.where((sub >= first - 256 * last) & (sub <= lane), score(last), -1e30)
    scores[pl.ds(pl.multiple_of(256 * last, 256), 256), :] = s
    inside = jnp.clip(lax.div(jnp.max(first) + 255, 256), low, last)
    best = lax.fori_loop(low, inside, masked, top(s))
    best = lax.fori_loop(inside, last, whole, best)
    best = jnp.max(best, axis=0, keepdims=True)
    acc[...] = jnp.zeros((HD, 1024), F32)

    def gather(p, total):
        s = scores[pl.ds(pl.multiple_of(p * 256, 256), 256), :]
        e = jnp.exp2((s - best) * (LOG2E * HD**-0.5))
        values = jnp.concatenate([kv[2 * p, 1], kv[2 * p + 1, 1]], axis=1)
        acc[...] += jnp.dot(values, e.astype(BF), preferred_element_type=F32)
        return total + jnp.sum(e.reshape(32, 8, 1024), axis=0)

    total = lax.fori_loop(low, last + 1, gather, jnp.zeros((8, 1024), F32))
    mixed = acc[...] / jnp.sum(total, axis=0, keepdims=True)
    for h in range(4):
        cols = slice(h * 128, h * 128 + 128)
        blocks = [mixed[:, j * 512 + h * 128 : j * 512 + h * 128 + 128].T for j in range(2)]
        outs[0][:, cols] = jnp.where(c == 0, blocks[0], blocks[1]).astype(BF)
        outs[1][:, cols] = jnp.where(c == 0, blocks[1], blocks[0]).astype(BF)


def collect_kernel(idx, *refs):
    pieces, (kv, start, docs) = refs[:5], refs[5:]
    z, y = idx[0], idx[1]
    docs[...] = jnp.zeros((128, HD), F32)
    for n, piece in enumerate(pieces):
        kv[4 * n : 4 * n + 4] = piece[:1024, :].reshape(4, 2, 128, HD)
        before = (z == 0) & (y + n < 4)
        docs[4 * n : 4 * n + 4, :] = jnp.where(before, -1.0, piece[1024:1040, :].astype(F32)[:4, :])
    columns = docs[...].T
    mine = jnp.concatenate([docs[16 + i : 17 + i, :] for i in range(4)], axis=1)
    count = jnp.zeros((8, 512), F32)
    for n in range(20):
        smaller = jnp.where(columns[:, n : n + 1] < mine, 1.0, 0.0)
        count = count + jnp.sum(smaller.reshape(16, 8, 512), axis=0)
    count = jnp.sum(count, axis=0, keepdims=True).astype(jnp.int32)
    for i in range(4):
        row = count[:, i * 128 : i * 128 + 128]
        start[i] = jnp.concatenate([row] * 4, axis=1)


def attend_kernel(idx, query, kv, start, out0, out1, out2, out3, scores, acc):
    attend(idx, query, start, kv, scores, acc, (out0, out1), 0)
    attend(idx, query, start, kv, scores, acc, (out2, out3), 1)


def place_kernel(idx, *refs):
    out = refs[4]
    for k in range(4):
        slot = jnp.bitwise_xor(idx[2], k)
        at = pl.multiple_of(lax.div(slot, 2) * 512, 512)
        out[lax.rem(slot, 2), :, pl.ds(at, 512)] = refs[k][...]


def call(kernel, shapes, args, scratch=(), cost=None, smem=1, mib=16):
    return pl.pallas_call(
        kernel,
        out_shape=shapes,
        in_specs=[SMEM] * smem + [VMEM] * (len(args) - smem),
        out_specs=jax.tree.map(lambda _: VMEM, shapes),
        scratch_shapes=list(scratch),
        cost_estimate=cost,
        compiler_params=pltpu.CompilerParams(vmem_limit_bytes=mib * 1024 * 1024),
    )(*args)


def cost(flops, nbytes):
    return pl.CostEstimate(flops=flops, bytes_accessed=nbytes, transcendentals=0)


def tie(*values):
    return lax.optimization_barrier(values)


def copies(value, axis, count):
    return lax.all_to_all(
        jnp.broadcast_to(value[None], (count, *value.shape)), axis, 0, 0, tiled=True
    )


def local(hidden_in, norm_gain, w_query, w_key, w_value, doc_ids):
    z, y, x, c = (lax.axis_index(a) for a in AXES)
    shape = jax.ShapeDtypeStruct
    where = jnp.stack([z, y, x, c]).astype(jnp.int32)

    piece = shape((32, COLS), BF)
    first, second = call(
        pack_kernel, (piece, piece), (where, w_query, w_key, w_value), cost=cost(0, 1 << 18)
    )
    first, second = permute(first, spread(0)), permute(second, spread(1))
    squares = call(
        squares_kernel,
        shape((256, HD), F32),
        (hidden_in,),
        cost=cost(1 << 20, 2 << 20),
        smem=0,
    )
    others = permute(squares, lambda z, y, x, c: (z, y, x, 1 - c))

    seq_a, seq_b = call(
        norm_kernel,
        (shape((144, HALF), BF), shape((128, HALF), BF)),
        (where, hidden_in, squares, others, doc_ids, norm_gain.reshape(1, WIDTH)),
        cost=cost(1 << 20, 3 << 20),
    )
    first, second, seq_a, seq_b = tie(first, second, seq_a, seq_b)
    right_a, left_b = along_x(seq_a, 1), along_x(seq_b, -1)
    right_b, left_a = along_x(seq_b, 1), along_x(seq_a, -1)
    rows = call(merge_kernel, shape((64, COLS), BF), (where, first, second), cost=cost(0, 1 << 18))
    w_z = copies(rows, "z", NZ).reshape(512, COLS)
    w_z, right_a, left_b = tie(w_z, right_a, left_b)
    far_a, far_b = along_x(right_a, 1), along_x(left_b, -1)

    kv0, q0 = w_z[:, 512:], w_z[:, :512]
    kv_up, kv_down = along_y(kv0, 1), along_y(kv0, -1)
    kv_up, kv_down, right_b, left_a, q0 = tie(kv_up, kv_down, right_b, left_a, q0)
    kv_far = along_y(kv_up, 1)
    q_up, q_down = along_y(q0, 1), along_y(q0, -1)
    q_far = along_y(q_down, -1)
    x_all, docs = call(
        stack_kernel,
        (shape((1024, HALF), BF), shape((16, HD), BF)),
        (where, seq_a, right_a, left_a, far_a, seq_b, right_b, left_b, far_b),
        cost=cost(0, 8 << 20),
    )

    position = (512 * (z * NY + y) + jnp.arange(512, dtype=jnp.int32)).astype(F32)
    inverse = THETA ** (-jnp.arange(64, dtype=F32) * 2.0 / HD)
    angle = position[:, None] * inverse[None, :]
    cos, sin = jnp.cos(angle), jnp.sin(angle)

    x_all, cos, sin = tie(x_all, cos, sin)
    keep, send = call(
        project_kernel,
        (shape((512, 256), F32), shape((512, 256), F32)),
        (where, x_all, kv0, kv_up, kv_down, kv_far),
        (pltpu.VMEM((NZ, 256, 256), BF),),
        cost(2 * 1024 * HALF * 256, 10 << 20),
    )
    got = permute(send, lambda z, y, x, c: (z, y, x, 1 - c))
    own = call(
        rotate_kv_kernel,
        shape((ROWS, HD), BF),
        (keep, got, cos, sin, docs),
        cost=cost(1 << 20, 2 << 20),
        smem=0,
    )
    x_all, own = tie(x_all, own)
    earlier = [
        permute(own, lambda z, y, x, c: (*divmod((z * NY + y + n) % (NZ * NY), NY), x, c))
        for n in (4, 3, 2, 1)
    ]
    keep, send = call(
        project_kernel,
        (shape((512, 512), F32), shape((512, 512), F32)),
        (where, x_all, q0, q_up, q_down, q_far),
        (pltpu.VMEM((NZ, 256, 512), BF),),
        cost(2 * 1024 * HALF * 512, 10 << 20),
    )
    got = permute(send, lambda z, y, x, c: (z, y, x, 1 - c))
    query = call(
        rotate_q_kernel,
        shape((4, 512, HD), BF),
        (keep, got, cos, sin),
        cost=cost(4 << 20, 3 << 20),
        smem=0,
    )
    kv, start = call(
        collect_kernel,
        (shape((20, 2, 128, HD), BF), shape((4, 1, 512), jnp.int32)),
        (where, *earlier, own),
        (pltpu.VMEM((128, HD), F32),),
        cost(1 << 36, 4 << 20),
    )
    block = shape((128, 512), BF)
    outs = call(
        attend_kernel,
        (block,) * 4,
        (where, query, kv, start),
        (pltpu.VMEM((2560, 1024), F32), pltpu.VMEM((HD, 1024), F32)),
        cost(1 << 31, 4 << 20),
        mib=24,
    )
    outs = [permute(out, back(k)) for k, out in enumerate(outs)]
    return call(
        place_kernel, shape((2, 128, 1024), BF), (where, *outs), cost=cost(0, 1 << 20)
    )


def solution(mesh):
    fine = Mesh(mesh.devices.reshape(NZ, NY, NX, NC), AXES)
    ctx = ("z", "y", "x")
    return jax.shard_map(
        local,
        mesh=fine,
        in_specs=(
            P(None, ctx, "head"),
            P(),
            P(ctx, "head"),
            P(ctx, "head"),
            P(ctx, "head"),
            P(None, ctx),
        ),
        out_specs=P(None, ctx, "head"),
        check_vma=False,
    )
```

```python
import jax
import jax.numpy as jnp
from jax import lax
from jax.experimental import pallas as pl
from jax.experimental.pallas import tpu as pltpu
from jax.sharding import Mesh, PartitionSpec as P

HD = 128
NZ, NY, NX, NC = 8, 4, 4, 2
AXES = ("z", "y", "x", "head")
THETA = 500000.0
EPS = 1e-05
WIDTH = 4096
HALF = WIDTH // 2
COLS = 6 * HD
LOG2E = 1.4426950408889634
BF = jnp.bfloat16
F32 = jnp.float32


def flat(z, y, x, c):
    return ((z * NY + y) * NX + x) * NC + c


def permute(value, to):
    pairs = [
        (flat(z, y, x, c), flat(*to(z, y, x, c)))
        for z in range(NZ)
        for y in range(NY)
        for x in range(NX)
        for c in range(NC)
    ]
    return lax.ppermute(value, AXES, pairs)


def along_x(value, by):
    return permute(value, lambda z, y, x, c: (z, y, (x + by) % NX, c))


def along_z(value, by):
    return permute(value, lambda z, y, x, c: ((z + by) % NZ, y, x, c))


def along_y(value, by):
    return permute(value, lambda z, y, x, c: (z, (y + by) % NY, x, c))


def spread(by):
    def to(z, y, x, c):
        b = (x + by) % 2
        return 2 * (z % 4) + y // 2, 2 * (y % 2) + x // 2, 2 * c + b, z // 4

    return to


def back(k):
    def to(z, y, x, c):
        return z, y, (2 * (x % 2) + c) ^ k, x // 2

    return to


VMEM = pl.BlockSpec(memory_space=pltpu.VMEM)
SMEM = pl.BlockSpec(memory_space=pltpu.SMEM)
ROWS = 8 * HD + 16


def pack_kernel(idx, query, key, value, first, second):
    x = idx[2]
    for by, out in ((0, first), (1, second)):
        b = lax.rem(x + by, 2)
        out[:, :512] = query[:, pl.ds(pl.multiple_of(b * 512, 512), 512)]
        out[:, 512:640] = key[:, pl.ds(pl.multiple_of(b * 128, 128), 128)]
        out[:, 640:] = value[:, pl.ds(pl.multiple_of(b * 128, 128), 128)]


def squares_kernel(hidden, squares):
    for s in range(2):
        wide = hidden[s].astype(F32)
        total = jnp.sum(wide * wide, axis=-1, keepdims=True)
        squares[s * 128 : s * 128 + 128, :] = jnp.broadcast_to(total, (HD, HD))


def norm_kernel(idx, hidden, squares, others, docs, gain, seq_a, seq_b):
    g = gain[:, pl.ds(pl.multiple_of(idx[3] * HALF, HALF), HALF)].astype(F32)
    for s, out in ((0, seq_a), (1, seq_b)):
        for t in range(4):
            rows = slice(t * 32, t * 32 + 32)
            both = slice(s * 128 + t * 32, s * 128 + t * 32 + 32)
            scale = lax.rsqrt((squares[both, :] + others[both, :]) * (1.0 / WIDTH) + EPS)
            wide = hidden[s, rows, :].astype(F32)
            out[rows, :] = (wide * scale[:, :1] * g).astype(BF)
    extra = jnp.concatenate([docs[...].astype(F32), jnp.zeros((14, HD), F32)], axis=0)
    seq_a[128:144, :HD] = extra.astype(BF)
    seq_a[128:144, HD:] = jnp.zeros((16, HALF - HD), BF)


def merge_kernel(idx, first, second, out):
    odd = lax.rem(idx[2], 2) == 1
    top, low = first[...].astype(F32), second[...].astype(F32)
    out[:32, :] = jnp.where(odd, low, top).astype(BF)
    out[32:, :] = jnp.where(odd, top, low).astype(BF)


def stack_kernel(idx, *refs):
    hidden, (x_all, docs) = refs[:8], refs[8:]
    x, c = idx[2], idx[3]
    row = lax.broadcasted_iota(jnp.int32, (16, HD), 0)
    found = jnp.zeros((16, HD), F32)
    for n, ref in enumerate(hidden):
        s, d = n // 4, (0, -1, 1, 2)[n % 4]
        chip = lax.rem(x + d + NX, NX)
        base = jnp.where(c == s, 0, 512) + chip * 128
        x_all[pl.ds(pl.multiple_of(base, 128), 128), :] = ref[:128, :]
        if s == 0:
            tile = ref[128:144, :HD].astype(F32)
            mine = jnp.where(c == 0, tile[0:1, :], tile[1:2, :])
            found = jnp.where(row == chip, mine, found)
    docs[...] = found.astype(BF)


def multiply(x_all, w_all, keep, send):
    for t in range(2):
        at = t * 256
        send[at : at + 256, :] = jnp.dot(
            x_all[512 + at : 768 + at, :], w_all, preferred_element_type=F32
        )
    for t in range(2):
        at = t * 256
        keep[at : at + 256, :] = jnp.dot(
            x_all[at : at + 256, :], w_all, preferred_element_type=F32
        )


def project_kernel(idx, x_all, own, up, down, far, keep, send, w_all):
    for ref, d in ((own, 0), (up, -1), (down, 1), (far, 2)):
        shift = pl.multiple_of(lax.rem(idx[1] + d + NY, NY) * 64, 64)
        for z in range(NZ):
            w_all[z, pl.ds(shift, 64), :] = ref[z * 64 : z * 64 + 64, :]
    multiply(x_all, w_all[...].reshape(HALF, own.shape[1]), keep, send)


def turned(value, cos, sin):
    cosine = jnp.concatenate([cos, cos], axis=1)
    sine = jnp.concatenate([-sin, sin], axis=1)
    return value * cosine + pltpu.roll(value, 64, 1) * sine


def rotate_kv_kernel(keep, got, cos, sin, docs, kv):
    for i in range(4):
        rows = slice(i * 128, i * 128 + 128)
        value = keep[rows, :] + got[rows, :]
        at = i * 256
        kv[at : at + 128, :] = turned(value[:, :128], cos[rows, :], sin[rows, :]).astype(BF)
        kv[at + 128 : at + 256, :] = value[:, 128:].T.astype(BF)
    kv[1024:1040, :] = docs[...]


def rotate_q_kernel(keep, got, cos, sin, query):
    for i in range(4):
        rows = slice(i * 128, i * 128 + 128)
        for h in range(4):
            cols = slice(h * 128, h * 128 + 128)
            value = keep[rows, cols] + got[rows, cols]
            query[i, h * 128 : h * 128 + 128, :] = turned(value, cos[rows, :], sin[rows, :]).astype(BF)


def attend(idx, query, start, kv, scores, acc, outs, part):
    c = idx[3]
    m = jnp.bitwise_xor(lax.rem(idx[2], 2), part)
    first = jnp.concatenate([start[2 * m], start[2 * m + 1]], axis=1)
    rows = query[pl.ds(2 * m, 2)].reshape(1024, HD)
    sub = lax.broadcasted_iota(jnp.int32, (256, 1024), 0)
    lane = lax.broadcasted_iota(jnp.int32, (256, 1024), 1)
    lane = lax.div(lane, 512) * 128 + lax.rem(lane, 128)
    last = 8 + m
    low = jnp.minimum(lax.div(jnp.maximum(jnp.min(first), 0), 256), last)
    contract = (((1,), (1,)), ((), ()))

    def score(p):
        keys = kv[pl.ds(2 * p, 2), 0].reshape(256, HD)
        return lax.dot_general(keys, rows, contract, preferred_element_type=F32)

    def top(s):
        return jnp.max(s.reshape(32, 8, 1024), axis=0)

    def keep(p, s, best):
        scores[pl.ds(pl.multiple_of(p * 256, 256), 256), :] = s
        return jnp.maximum(best, top(s))

    def masked(p, best):
        return keep(p, jnp.where(sub >= first - 256 * p, score(p), -1e30), best)

    def whole(p, best):
        return keep(p, score(p), best)

    s = jnp.where((sub >= first - 256 * last) & (sub <= lane), score(last), -1e30)
    scores[pl.ds(pl.multiple_of(256 * last, 256), 256), :] = s
    inside = jnp.clip(lax.div(jnp.max(first) + 255, 256), low, last)
    best = lax.fori_loop(low, inside, masked, top(s))
    best = lax.fori_loop(inside, last, whole, best)
    best = jnp.max(best, axis=0, keepdims=True)
    acc[...] = jnp.zeros((HD, 1024), F32)

    def gather(p, total):
        s = scores[pl.ds(pl.multiple_of(p * 256, 256), 256), :]
        e = jnp.exp2((s - best) * (LOG2E * HD**-0.5))
        values = jnp.concatenate([kv[2 * p, 1], kv[2 * p + 1, 1]], axis=1)
        acc[...] += jnp.dot(values, e.astype(BF), preferred_element_type=F32)
        return total + jnp.sum(e.reshape(32, 8, 1024), axis=0)

    total = lax.fori_loop(low, last + 1, gather, jnp.zeros((8, 1024), F32))
    mixed = acc[...] / jnp.sum(total, axis=0, keepdims=True)
    for h in range(4):
        cols = slice(h * 128, h * 128 + 128)
        blocks = [mixed[:, j * 512 + h * 128 : j * 512 + h * 128 + 128].T for j in range(2)]
        outs[0][:, cols] = jnp.where(c == 0, blocks[0], blocks[1]).astype(BF)
        outs[1][:, cols] = jnp.where(c == 0, blocks[1], blocks[0]).astype(BF)


def collect_kernel(idx, *refs):
    pieces, (kv, start, docs) = refs[:5], refs[5:]
    z, y = idx[0], idx[1]
    docs[...] = jnp.zeros((128, HD), F32)
    for n, piece in enumerate(pieces):
        kv[4 * n : 4 * n + 4] = piece[:1024, :].reshape(4, 2, 128, HD)
        before = (z == 0) & (y + n < 4)
        docs[4 * n : 4 * n + 4, :] = jnp.where(before, -1.0, piece[1024:1040, :].astype(F32)[:4, :])
    columns = docs[...].T
    mine = jnp.concatenate([docs[16 + i : 17 + i, :] for i in range(4)], axis=1)
    count = jnp.zeros((8, 512), F32)
    for n in range(20):
        smaller = jnp.where(columns[:, n : n + 1] < mine, 1.0, 0.0)
        count = count + jnp.sum(smaller.reshape(16, 8, 512), axis=0)
    count = jnp.sum(count, axis=0, keepdims=True).astype(jnp.int32)
    for i in range(4):
        row = count[:, i * 128 : i * 128 + 128]
        start[i] = jnp.concatenate([row] * 4, axis=1)


def attend_kernel(idx, query, kv, start, out0, out1, out2, out3, scores, acc):
    attend(idx, query, start, kv, scores, acc, (out0, out1), 0)
    attend(idx, query, start, kv, scores, acc, (out2, out3), 1)


def place_kernel(idx, *refs):
    out = refs[4]
    for k in range(4):
        slot = jnp.bitwise_xor(idx[2], k)
        at = pl.multiple_of(lax.div(slot, 2) * 512, 512)
        out[lax.rem(slot, 2), :, pl.ds(at, 512)] = refs[k][...]


def call(kernel, shapes, args, scratch=(), cost=None, smem=1, mib=16):
    return pl.pallas_call(
        kernel,
        out_shape=shapes,
        in_specs=[SMEM] * smem + [VMEM] * (len(args) - smem),
        out_specs=jax.tree.map(lambda _: VMEM, shapes),
        scratch_shapes=list(scratch),
        cost_estimate=cost,
        compiler_params=pltpu.CompilerParams(vmem_limit_bytes=mib * 1024 * 1024),
    )(*args)


def cost(flops, nbytes):
    return pl.CostEstimate(flops=flops, bytes_accessed=nbytes, transcendentals=0)


def tie(*values):
    return lax.optimization_barrier(values)


def copies(value, axis, count):
    return lax.all_to_all(
        jnp.broadcast_to(value[None], (count, *value.shape)), axis, 0, 0, tiled=True
    )


def local(hidden_in, norm_gain, w_query, w_key, w_value, doc_ids):
    z, y, x, c = (lax.axis_index(a) for a in AXES)
    shape = jax.ShapeDtypeStruct
    where = jnp.stack([z, y, x, c]).astype(jnp.int32)

    piece = shape((32, COLS), BF)
    first, second = call(
        pack_kernel, (piece, piece), (where, w_query, w_key, w_value), cost=cost(0, 1 << 18)
    )
    first, second = permute(first, spread(0)), permute(second, spread(1))
    squares = call(
        squares_kernel,
        shape((256, HD), F32),
        (hidden_in,),
        cost=cost(1 << 20, 2 << 20),
        smem=0,
    )
    others = permute(squares, lambda z, y, x, c: (z, y, x, 1 - c))

    seq_a, seq_b = call(
        norm_kernel,
        (shape((144, HALF), BF), shape((128, HALF), BF)),
        (where, hidden_in, squares, others, doc_ids, norm_gain.reshape(1, WIDTH)),
        cost=cost(1 << 20, 3 << 20),
    )
    first, second, seq_a, seq_b = tie(first, second, seq_a, seq_b)
    right_a, left_b = along_x(seq_a, 1), along_x(seq_b, -1)
    right_b, left_a = along_x(seq_b, 1), along_x(seq_a, -1)
    rows = call(merge_kernel, shape((64, COLS), BF), (where, first, second), cost=cost(0, 1 << 18))
    w_z = copies(rows, "z", NZ).reshape(512, COLS)
    w_z, right_a, left_b = tie(w_z, right_a, left_b)
    far_a, far_b = along_x(right_a, 1), along_x(left_b, -1)

    kv0, q0 = w_z[:, 512:], w_z[:, :512]
    kv_up, kv_down = along_y(kv0, 1), along_y(kv0, -1)
    kv_up, kv_down, right_b, left_a, q0 = tie(kv_up, kv_down, right_b, left_a, q0)
    kv_far = along_y(kv_up, 1)
    q_up, q_down = along_y(q0, 1), along_y(q0, -1)
    x_all, docs = call(
        stack_kernel,
        (shape((1024, HALF), BF), shape((16, HD), BF)),
        (where, seq_a, right_a, left_a, far_a, seq_b, right_b, left_b, far_b),
        cost=cost(0, 8 << 20),
    )

    position = (512 * (z * NY + y) + jnp.arange(512, dtype=jnp.int32)).astype(F32)
    inverse = THETA ** (-jnp.arange(64, dtype=F32) * 2.0 / HD)
    angle = position[:, None] * inverse[None, :]
    cos, sin = jnp.cos(angle), jnp.sin(angle)

    x_all, cos, sin = tie(x_all, cos, sin)
    keep, send = call(
        project_kernel,
        (shape((512, 256), F32), shape((512, 256), F32)),
        (where, x_all, kv0, kv_up, kv_down, kv_far),
        (pltpu.VMEM((NZ, 256, 256), BF),),
        cost(2 * 1024 * HALF * 256, 10 << 20),
    )
    got = permute(send, lambda z, y, x, c: (z, y, x, 1 - c))
    got, q_up, q_down = tie(got, q_up, q_down)
    q_far = along_y(q_down, -1)
    own = call(
        rotate_kv_kernel,
        shape((ROWS, HD), BF),
        (keep, got, cos, sin, docs),
        cost=cost(1 << 20, 2 << 20),
        smem=0,
    )
    x_all, own = tie(x_all, own)
    earlier = [
        permute(own, lambda z, y, x, c: (*divmod((z * NY + y + n) % (NZ * NY), NY), x, c))
        for n in (4, 3, 2, 1)
    ]
    keep, send = call(
        project_kernel,
        (shape((512, 512), F32), shape((512, 512), F32)),
        (where, x_all, q0, q_up, q_down, q_far),
        (pltpu.VMEM((NZ, 256, 512), BF),),
        cost(2 * 1024 * HALF * 512, 10 << 20),
    )
    got = permute(send, lambda z, y, x, c: (z, y, x, 1 - c))
    query = call(
        rotate_q_kernel,
        shape((4, 512, HD), BF),
        (keep, got, cos, sin),
        cost=cost(4 << 20, 3 << 20),
        smem=0,
    )
    kv, start = call(
        collect_kernel,
        (shape((20, 2, 128, HD), BF), shape((4, 1, 512), jnp.int32)),
        (where, *earlier, own),
        (pltpu.VMEM((128, HD), F32),),
        cost(1 << 36, 4 << 20),
    )
    block = shape((128, 512), BF)
    outs = call(
        attend_kernel,
        (block,) * 4,
        (where, query, kv, start),
        (pltpu.VMEM((2560, 1024), F32), pltpu.VMEM((HD, 1024), F32)),
        cost(1 << 31, 4 << 20),
        mib=24,
    )
    outs = [permute(out, back(k)) for k, out in enumerate(outs)]
    return call(
        place_kernel, shape((2, 128, 1024), BF), (where, *outs), cost=cost(0, 1 << 20)
    )


def solution(mesh):
    fine = Mesh(mesh.devices.reshape(NZ, NY, NX, NC), AXES)
    ctx = ("z", "y", "x")
    return jax.shard_map(
        local,
        mesh=fine,
        in_specs=(
            P(None, ctx, "head"),
            P(),
            P(ctx, "head"),
            P(ctx, "head"),
            P(ctx, "head"),
            P(None, ctx),
        ),
        out_specs=P(None, ctx, "head"),
        check_vma=False,
    )
```

```python
import jax
import jax.numpy as jnp
from jax import lax
from jax.experimental import pallas as pl
from jax.experimental.pallas import tpu as pltpu
from jax.sharding import Mesh, PartitionSpec as P

HD = 128
NZ, NY, NX, NC = 8, 4, 4, 2
AXES = ("z", "y", "x", "head")
THETA = 500000.0
EPS = 1e-05
WIDTH = 4096
HALF = WIDTH // 2
COLS = 6 * HD
LOG2E = 1.4426950408889634
BF = jnp.bfloat16
F32 = jnp.float32


def flat(z, y, x, c):
    return ((z * NY + y) * NX + x) * NC + c


def permute(value, to):
    pairs = [
        (flat(z, y, x, c), flat(*to(z, y, x, c)))
        for z in range(NZ)
        for y in range(NY)
        for x in range(NX)
        for c in range(NC)
    ]
    return lax.ppermute(value, AXES, pairs)


def along_x(value, by):
    return permute(value, lambda z, y, x, c: (z, y, (x + by) % NX, c))


def along_z(value, by):
    return permute(value, lambda z, y, x, c: ((z + by) % NZ, y, x, c))


def along_y(value, by):
    return permute(value, lambda z, y, x, c: (z, (y + by) % NY, x, c))


def spread(by):
    def to(z, y, x, c):
        b = (x + by) % 2
        return 2 * (z % 4) + y // 2, 2 * (y % 2) + x // 2, 2 * c + b, z // 4

    return to


def back(k):
    def to(z, y, x, c):
        return z, y, (2 * (x % 2) + c) ^ k, x // 2

    return to


VMEM = pl.BlockSpec(memory_space=pltpu.VMEM)
SMEM = pl.BlockSpec(memory_space=pltpu.SMEM)
ROWS = 8 * HD + 16


def pack_kernel(idx, query, key, value, first, second):
    x = idx[2]
    for by, out in ((0, first), (1, second)):
        b = lax.rem(x + by, 2)
        out[:, :512] = query[:, pl.ds(pl.multiple_of(b * 512, 512), 512)]
        out[:, 512:640] = key[:, pl.ds(pl.multiple_of(b * 128, 128), 128)]
        out[:, 640:] = value[:, pl.ds(pl.multiple_of(b * 128, 128), 128)]


def squares_kernel(hidden, squares):
    for s in range(2):
        wide = hidden[s].astype(F32)
        total = jnp.sum(wide * wide, axis=-1, keepdims=True)
        squares[s * 128 : s * 128 + 128, :] = jnp.broadcast_to(total, (HD, HD))


def norm_kernel(idx, hidden, squares, others, docs, gain, seq_a, seq_b):
    g = gain[:, pl.ds(pl.multiple_of(idx[3] * HALF, HALF), HALF)].astype(F32)
    for s, out in ((0, seq_a), (1, seq_b)):
        for t in range(4):
            rows = slice(t * 32, t * 32 + 32)
            both = slice(s * 128 + t * 32, s * 128 + t * 32 + 32)
            scale = lax.rsqrt((squares[both, :] + others[both, :]) * (1.0 / WIDTH) + EPS)
            wide = hidden[s, rows, :].astype(F32)
            out[rows, :] = (wide * scale[:, :1] * g).astype(BF)
    extra = jnp.concatenate([docs[...].astype(F32), jnp.zeros((14, HD), F32)], axis=0)
    seq_a[128:144, :HD] = extra.astype(BF)
    seq_a[128:144, HD:] = jnp.zeros((16, HALF - HD), BF)


def merge_kernel(idx, first, second, out):
    odd = lax.rem(idx[2], 2) == 1
    top, low = first[...].astype(F32), second[...].astype(F32)
    out[:32, :] = jnp.where(odd, low, top).astype(BF)
    out[32:, :] = jnp.where(odd, top, low).astype(BF)


def stack_kernel(idx, *refs):
    hidden, (x_all, docs) = refs[:8], refs[8:]
    x, c = idx[2], idx[3]
    row = lax.broadcasted_iota(jnp.int32, (16, HD), 0)
    found = jnp.zeros((16, HD), F32)
    for n, ref in enumerate(hidden):
        s, d = n // 4, (0, -1, 1, 2)[n % 4]
        chip = lax.rem(x + d + NX, NX)
        base = jnp.where(c == s, 0, 512) + chip * 128
        x_all[pl.ds(pl.multiple_of(base, 128), 128), :] = ref[:128, :]
        if s == 0:
            tile = ref[128:144, :HD].astype(F32)
            mine = jnp.where(c == 0, tile[0:1, :], tile[1:2, :])
            found = jnp.where(row == chip, mine, found)
    docs[...] = found.astype(BF)


def multiply(x_all, w_all, keep, send):
    for t in range(2):
        at = t * 256
        send[at : at + 256, :] = jnp.dot(
            x_all[512 + at : 768 + at, :], w_all, preferred_element_type=F32
        )
    for t in range(2):
        at = t * 256
        keep[at : at + 256, :] = jnp.dot(
            x_all[at : at + 256, :], w_all, preferred_element_type=F32
        )


def project_kernel(idx, x_all, own, up, down, far, keep, send, w_all):
    for ref, d in ((own, 0), (up, -1), (down, 1), (far, 2)):
        shift = pl.multiple_of(lax.rem(idx[1] + d + NY, NY) * 64, 64)
        for z in range(NZ):
            w_all[z, pl.ds(shift, 64), :] = ref[z * 64 : z * 64 + 64, :]
    multiply(x_all, w_all[...].reshape(HALF, own.shape[1]), keep, send)


def turned(value, cos, sin):
    cosine = jnp.concatenate([cos, cos], axis=1)
    sine = jnp.concatenate([-sin, sin], axis=1)
    return value * cosine + pltpu.roll(value, 64, 1) * sine


def rotate_kv_kernel(keep, got, cos, sin, docs, kv):
    for i in range(4):
        rows = slice(i * 128, i * 128 + 128)
        value = keep[rows, :] + got[rows, :]
        at = i * 256
        kv[at : at + 128, :] = turned(value[:, :128], cos[rows, :], sin[rows, :]).astype(BF)
        kv[at + 128 : at + 256, :] = value[:, 128:].T.astype(BF)
    kv[1024:1040, :] = docs[...]


def rotate_q_kernel(keep, got, cos, sin, query):
    for i in range(4):
        rows = slice(i * 128, i * 128 + 128)
        for h in range(4):
            cols = slice(h * 128, h * 128 + 128)
            value = keep[rows, cols] + got[rows, cols]
            query[i, h * 128 : h * 128 + 128, :] = turned(value, cos[rows, :], sin[rows, :]).astype(BF)


def attend(idx, query, start, kv, scores, acc, outs, part):
    c = idx[3]
    m = jnp.bitwise_xor(lax.rem(idx[2], 2), part)
    first = jnp.concatenate([start[2 * m], start[2 * m + 1]], axis=1)
    rows = query[pl.ds(2 * m, 2)].reshape(1024, HD)
    sub = lax.broadcasted_iota(jnp.int32, (256, 1024), 0)
    lane = lax.broadcasted_iota(jnp.int32, (256, 1024), 1)
    lane = lax.div(lane, 512) * 128 + lax.rem(lane, 128)
    last = 8 + m
    low = jnp.minimum(lax.div(jnp.maximum(jnp.min(first), 0), 256), last)
    contract = (((1,), (1,)), ((), ()))

    def score(p):
        keys = kv[pl.ds(2 * p, 2), 0].reshape(256, HD)
        return lax.dot_general(keys, rows, contract, preferred_element_type=F32)

    def top(s):
        return jnp.max(s.reshape(32, 8, 1024), axis=0)

    def keep(p, s, best):
        scores[pl.ds(pl.multiple_of(p * 256, 256), 256), :] = s
        return jnp.maximum(best, top(s))

    def masked(p, best):
        return keep(p, jnp.where(sub >= first - 256 * p, score(p), -1e30), best)

    def whole(p, best):
        return keep(p, score(p), best)

    s = jnp.where((sub >= first - 256 * last) & (sub <= lane), score(last), -1e30)
    scores[pl.ds(pl.multiple_of(256 * last, 256), 256), :] = s
    inside = jnp.clip(lax.div(jnp.max(first) + 255, 256), low, last)
    best = lax.fori_loop(low, inside, masked, top(s))
    best = lax.fori_loop(inside, last, whole, best)
    best = jnp.max(best, axis=0, keepdims=True)
    acc[...] = jnp.zeros((HD, 1024), F32)

    def gather(p, total):
        s = scores[pl.ds(pl.multiple_of(p * 256, 256), 256), :]
        e = jnp.exp2((s - best) * (LOG2E * HD**-0.5))
        values = jnp.concatenate([kv[2 * p, 1], kv[2 * p + 1, 1]], axis=1)
        acc[...] += jnp.dot(values, e.astype(BF), preferred_element_type=F32)
        return total + jnp.sum(e.reshape(32, 8, 1024), axis=0)

    total = lax.fori_loop(low, last + 1, gather, jnp.zeros((8, 1024), F32))
    mixed = acc[...] / jnp.sum(total, axis=0, keepdims=True)
    for h in range(4):
        cols = slice(h * 128, h * 128 + 128)
        blocks = [mixed[:, j * 512 + h * 128 : j * 512 + h * 128 + 128].T for j in range(2)]
        outs[0][:, cols] = jnp.where(c == 0, blocks[0], blocks[1]).astype(BF)
        outs[1][:, cols] = jnp.where(c == 0, blocks[1], blocks[0]).astype(BF)


def collect_kernel(idx, *refs):
    pieces, (kv, start, docs) = refs[:5], refs[5:]
    z, y = idx[0], idx[1]
    docs[...] = jnp.zeros((128, HD), F32)
    for n, piece in enumerate(pieces):
        kv[4 * n : 4 * n + 4] = piece[:1024, :].reshape(4, 2, 128, HD)
        before = (z == 0) & (y + n < 4)
        docs[4 * n : 4 * n + 4, :] = jnp.where(before, -1.0, piece[1024:1040, :].astype(F32)[:4, :])
    columns = docs[...].T
    mine = jnp.concatenate([docs[16 + i : 17 + i, :] for i in range(4)], axis=1)
    count = jnp.zeros((8, 512), F32)
    for n in range(20):
        smaller = jnp.where(columns[:, n : n + 1] < mine, 1.0, 0.0)
        count = count + jnp.sum(smaller.reshape(16, 8, 512), axis=0)
    count = jnp.sum(count, axis=0, keepdims=True).astype(jnp.int32)
    for i in range(4):
        row = count[:, i * 128 : i * 128 + 128]
        start[i] = jnp.concatenate([row] * 4, axis=1)


def attend_kernel(idx, query, kv, start, out0, out1, out2, out3, scores, acc):
    attend(idx, query, start, kv, scores, acc, (out0, out1), 0)
    attend(idx, query, start, kv, scores, acc, (out2, out3), 1)


def place_kernel(idx, *refs):
    out = refs[4]
    for k in range(4):
        slot = jnp.bitwise_xor(idx[2], k)
        at = pl.multiple_of(lax.div(slot, 2) * 512, 512)
        out[lax.rem(slot, 2), :, pl.ds(at, 512)] = refs[k][...]


def call(kernel, shapes, args, scratch=(), cost=None, smem=1, mib=16):
    return pl.pallas_call(
        kernel,
        out_shape=shapes,
        in_specs=[SMEM] * smem + [VMEM] * (len(args) - smem),
        out_specs=jax.tree.map(lambda _: VMEM, shapes),
        scratch_shapes=list(scratch),
        cost_estimate=cost,
        compiler_params=pltpu.CompilerParams(vmem_limit_bytes=mib * 1024 * 1024),
    )(*args)


def cost(flops, nbytes):
    return pl.CostEstimate(flops=flops, bytes_accessed=nbytes, transcendentals=0)


def tie(*values):
    return lax.optimization_barrier(values)


def copies(value, axis, count):
    return lax.all_to_all(
        jnp.broadcast_to(value[None], (count, *value.shape)), axis, 0, 0, tiled=True
    )


def local(hidden_in, norm_gain, w_query, w_key, w_value, doc_ids):
    z, y, x, c = (lax.axis_index(a) for a in AXES)
    shape = jax.ShapeDtypeStruct
    where = jnp.stack([z, y, x, c]).astype(jnp.int32)

    piece = shape((32, COLS), BF)
    first, second = call(
        pack_kernel, (piece, piece), (where, w_query, w_key, w_value), cost=cost(0, 1 << 18)
    )
    first, second = permute(first, spread(0)), permute(second, spread(1))
    squares = call(
        squares_kernel,
        shape((256, HD), F32),
        (hidden_in,),
        cost=cost(1 << 20, 2 << 20),
        smem=0,
    )
    others = permute(squares, lambda z, y, x, c: (z, y, x, 1 - c))

    seq_a, seq_b = call(
        norm_kernel,
        (shape((144, HALF), BF), shape((128, HALF), BF)),
        (where, hidden_in, squares, others, doc_ids, norm_gain.reshape(1, WIDTH)),
        cost=cost(1 << 20, 3 << 20),
    )
    first, second, seq_a, seq_b = tie(first, second, seq_a, seq_b)
    right_a, left_b = along_x(seq_a, 1), along_x(seq_b, -1)
    right_b, left_a = along_x(seq_b, 1), along_x(seq_a, -1)
    rows = call(merge_kernel, shape((64, COLS), BF), (where, first, second), cost=cost(0, 1 << 18))
    w_z = copies(rows, "z", NZ).reshape(512, COLS)
    w_z, right_a, left_b = tie(w_z, right_a, left_b)
    far_a, far_b = along_x(right_a, 1), along_x(left_b, -1)

    kv0, q0 = w_z[:, 512:], w_z[:, :512]
    kv_up, kv_down = along_y(kv0, 1), along_y(kv0, -1)
    kv_up, kv_down, right_b, left_a, q0 = tie(kv_up, kv_down, right_b, left_a, q0)
    kv_far = along_y(kv_up, 1)
    q_up, q_down = along_y(q0, 1), along_y(q0, -1)
    x_all, docs = call(
        stack_kernel,
        (shape((1024, HALF), BF), shape((16, HD), BF)),
        (where, seq_a, right_a, left_a, far_a, seq_b, right_b, left_b, far_b),
        cost=cost(0, 8 << 20),
    )

    position = (512 * (z * NY + y) + jnp.arange(512, dtype=jnp.int32)).astype(F32)
    inverse = THETA ** (-jnp.arange(64, dtype=F32) * 2.0 / HD)
    angle = position[:, None] * inverse[None, :]
    cos, sin = jnp.cos(angle), jnp.sin(angle)

    x_all, cos, sin = tie(x_all, cos, sin)
    keep, send = call(
        project_kernel,
        (shape((512, 256), F32), shape((512, 256), F32)),
        (where, x_all, kv0, kv_up, kv_down, kv_far),
        (pltpu.VMEM((NZ, 256, 256), BF),),
        cost(2 * 1024 * HALF * 256, 10 << 20),
    )
    got = permute(send, lambda z, y, x, c: (z, y, x, 1 - c))
    got, q_up, q_down = tie(got, q_up, q_down)
    q_far = along_y(q_up, 1)
    own = call(
        rotate_kv_kernel,
        shape((ROWS, HD), BF),
        (keep, got, cos, sin, docs),
        cost=cost(1 << 20, 2 << 20),
        smem=0,
    )
    x_all, own = tie(x_all, own)
    earlier = [
        permute(own, lambda z, y, x, c: (*divmod((z * NY + y + n) % (NZ * NY), NY), x, c))
        for n in (4, 3, 2, 1)
    ]
    keep, send = call(
        project_kernel,
        (shape((512, 512), F32), shape((512, 512), F32)),
        (where, x_all, q0, q_up, q_down, q_far),
        (pltpu.VMEM((NZ, 256, 512), BF),),
        cost(2 * 1024 * HALF * 512, 10 << 20),
    )
    got = permute(send, lambda z, y, x, c: (z, y, x, 1 - c))
    query = call(
        rotate_q_kernel,
        shape((4, 512, HD), BF),
        (keep, got, cos, sin),
        cost=cost(4 << 20, 3 << 20),
        smem=0,
    )
    kv, start = call(
        collect_kernel,
        (shape((20, 2, 128, HD), BF), shape((4, 1, 512), jnp.int32)),
        (where, *earlier, own),
        (pltpu.VMEM((128, HD), F32),),
        cost(1 << 36, 4 << 20),
    )
    block = shape((128, 512), BF)
    outs = call(
        attend_kernel,
        (block,) * 4,
        (where, query, kv, start),
        (pltpu.VMEM((2560, 1024), F32), pltpu.VMEM((HD, 1024), F32)),
        cost(1 << 31, 4 << 20),
        mib=24,
    )
    outs = [permute(out, back(k)) for k, out in enumerate(outs)]
    return call(
        place_kernel, shape((2, 128, 1024), BF), (where, *outs), cost=cost(0, 1 << 20)
    )


def solution(mesh):
    fine = Mesh(mesh.devices.reshape(NZ, NY, NX, NC), AXES)
    ctx = ("z", "y", "x")
    return jax.shard_map(
        local,
        mesh=fine,
        in_specs=(
            P(None, ctx, "head"),
            P(),
            P(ctx, "head"),
            P(ctx, "head"),
            P(ctx, "head"),
            P(None, ctx),
        ),
        out_specs=P(None, ctx, "head"),
        check_vma=False,
    )
```

```python
import jax
import jax.numpy as jnp
from jax import lax
from jax.experimental import pallas as pl
from jax.experimental.pallas import tpu as pltpu
from jax.sharding import Mesh, PartitionSpec as P

HD = 128
NZ, NY, NX, NC = 8, 4, 4, 2
AXES = ("z", "y", "x", "head")
THETA = 500000.0
EPS = 1e-05
WIDTH = 4096
HALF = WIDTH // 2
COLS = 6 * HD
LOG2E = 1.4426950408889634
BF = jnp.bfloat16
F32 = jnp.float32


def flat(z, y, x, c):
    return ((z * NY + y) * NX + x) * NC + c


def permute(value, to):
    pairs = [
        (flat(z, y, x, c), flat(*to(z, y, x, c)))
        for z in range(NZ)
        for y in range(NY)
        for x in range(NX)
        for c in range(NC)
    ]
    return lax.ppermute(value, AXES, pairs)


def along_x(value, by):
    return permute(value, lambda z, y, x, c: (z, y, (x + by) % NX, c))


def along_z(value, by):
    return permute(value, lambda z, y, x, c: ((z + by) % NZ, y, x, c))


def along_y(value, by):
    return permute(value, lambda z, y, x, c: (z, (y + by) % NY, x, c))


def spread(by):
    def to(z, y, x, c):
        b = (x + by) % 2
        return 2 * (z % 4) + y // 2, 2 * (y % 2) + x // 2, 2 * c + b, z // 4

    return to


def back(k):
    def to(z, y, x, c):
        return z, y, (2 * (x % 2) + c) ^ k, x // 2

    return to


VMEM = pl.BlockSpec(memory_space=pltpu.VMEM)
SMEM = pl.BlockSpec(memory_space=pltpu.SMEM)
ROWS = 8 * HD + 16


def pack_kernel(idx, query, key, value, first, second):
    x = idx[2]
    for by, out in ((0, first), (1, second)):
        b = lax.rem(x + by, 2)
        out[:, :512] = query[:, pl.ds(pl.multiple_of(b * 512, 512), 512)]
        out[:, 512:640] = key[:, pl.ds(pl.multiple_of(b * 128, 128), 128)]
        out[:, 640:] = value[:, pl.ds(pl.multiple_of(b * 128, 128), 128)]


def squares_kernel(hidden, squares):
    for s in range(2):
        wide = hidden[s].astype(F32)
        total = jnp.sum(wide * wide, axis=-1, keepdims=True)
        squares[s * 128 : s * 128 + 128, :] = jnp.broadcast_to(total, (HD, HD))


def norm_kernel(idx, hidden, squares, others, docs, gain, seq_a, seq_b):
    g = gain[:, pl.ds(pl.multiple_of(idx[3] * HALF, HALF), HALF)].astype(F32)
    for s, out in ((0, seq_a), (1, seq_b)):
        for t in range(4):
            rows = slice(t * 32, t * 32 + 32)
            both = slice(s * 128 + t * 32, s * 128 + t * 32 + 32)
            scale = lax.rsqrt((squares[both, :] + others[both, :]) * (1.0 / WIDTH) + EPS)
            wide = hidden[s, rows, :].astype(F32)
            out[rows, :] = (wide * scale[:, :1] * g).astype(BF)
    extra = jnp.concatenate([docs[...].astype(F32), jnp.zeros((14, HD), F32)], axis=0)
    seq_a[128:144, :HD] = extra.astype(BF)
    seq_a[128:144, HD:] = jnp.zeros((16, HALF - HD), BF)


def merge_kernel(idx, first, second, out):
    odd = lax.rem(idx[2], 2) == 1
    top, low = first[...].astype(F32), second[...].astype(F32)
    out[:32, :] = jnp.where(odd, low, top).astype(BF)
    out[32:, :] = jnp.where(odd, top, low).astype(BF)


def stack_kernel(idx, *refs):
    hidden, (x_all, docs) = refs[:8], refs[8:]
    x, c = idx[2], idx[3]
    row = lax.broadcasted_iota(jnp.int32, (16, HD), 0)
    found = jnp.zeros((16, HD), F32)
    for n, ref in enumerate(hidden):
        s, d = n // 4, (0, -1, 1, 2)[n % 4]
        chip = lax.rem(x + d + NX, NX)
        base = jnp.where(c == s, 0, 512) + chip * 128
        x_all[pl.ds(pl.multiple_of(base, 128), 128), :] = ref[:128, :]
        if s == 0:
            tile = ref[128:144, :HD].astype(F32)
            mine = jnp.where(c == 0, tile[0:1, :], tile[1:2, :])
            found = jnp.where(row == chip, mine, found)
    docs[...] = found.astype(BF)


def multiply(x_all, w_all, keep, send):
    for t in range(2):
        at = t * 256
        send[at : at + 256, :] = jnp.dot(
            x_all[512 + at : 768 + at, :], w_all, preferred_element_type=F32
        )
    for t in range(2):
        at = t * 256
        keep[at : at + 256, :] = jnp.dot(
            x_all[at : at + 256, :], w_all, preferred_element_type=F32
        )


def project_kernel(idx, x_all, own, up, down, far, keep, send, w_all):
    for ref, d in ((own, 0), (up, -1), (down, 1), (far, 2)):
        shift = pl.multiple_of(lax.rem(idx[1] + d + NY, NY) * 64, 64)
        for z in range(NZ):
            w_all[z, pl.ds(shift, 64), :] = ref[z * 64 : z * 64 + 64, :]
    multiply(x_all, w_all[...].reshape(HALF, own.shape[1]), keep, send)


def turned(value, cos, sin):
    cosine = jnp.concatenate([cos, cos], axis=1)
    sine = jnp.concatenate([-sin, sin], axis=1)
    return value * cosine + pltpu.roll(value, 64, 1) * sine


def rotate_kv_kernel(keep, got, cos, sin, docs, kv):
    for i in range(4):
        rows = slice(i * 128, i * 128 + 128)
        value = keep[rows, :] + got[rows, :]
        at = i * 256
        kv[at : at + 128, :] = turned(value[:, :128], cos[rows, :], sin[rows, :]).astype(BF)
        kv[at + 128 : at + 256, :] = value[:, 128:].T.astype(BF)
    kv[1024:1040, :] = docs[...]


def rotate_q_kernel(keep, got, cos, sin, query):
    for i in range(4):
        rows = slice(i * 128, i * 128 + 128)
        for h in range(4):
            cols = slice(h * 128, h * 128 + 128)
            value = keep[rows, cols] + got[rows, cols]
            query[i, h * 128 : h * 128 + 128, :] = turned(value, cos[rows, :], sin[rows, :]).astype(BF)


def attend(idx, query, start, kv, scores, acc, outs, part):
    c = idx[3]
    m = jnp.bitwise_xor(lax.rem(idx[2], 2), part)
    first = jnp.concatenate([start[2 * m], start[2 * m + 1]], axis=1)
    rows = query[pl.ds(2 * m, 2)].reshape(1024, HD)
    sub = lax.broadcasted_iota(jnp.int32, (256, 1024), 0)
    lane = lax.broadcasted_iota(jnp.int32, (256, 1024), 1)
    lane = lax.div(lane, 512) * 128 + lax.rem(lane, 128)
    last = 8 + m
    low = jnp.minimum(lax.div(jnp.maximum(jnp.min(first), 0), 256), last)
    contract = (((1,), (1,)), ((), ()))

    def score(p):
        keys = kv[pl.ds(2 * p, 2), 0].reshape(256, HD)
        return lax.dot_general(keys, rows, contract, preferred_element_type=F32)

    def top(s):
        return jnp.max(s.reshape(32, 8, 1024), axis=0)

    def keep(p, s, best):
        scores[pl.ds(pl.multiple_of(p * 256, 256), 256), :] = s
        return jnp.maximum(best, top(s))

    def masked(p, best):
        return keep(p, jnp.where(sub >= first - 256 * p, score(p), -1e30), best)

    def whole(p, best):
        return keep(p, score(p), best)

    s = jnp.where((sub >= first - 256 * last) & (sub <= lane), score(last), -1e30)
    scores[pl.ds(pl.multiple_of(256 * last, 256), 256), :] = s
    inside = jnp.clip(lax.div(jnp.max(first) + 255, 256), low, last)
    best = lax.fori_loop(low, inside, masked, top(s))
    best = lax.fori_loop(inside, last, whole, best)
    best = jnp.max(best, axis=0, keepdims=True)
    acc[...] = jnp.zeros((HD, 1024), F32)

    def gather(p, total):
        s = scores[pl.ds(pl.multiple_of(p * 256, 256), 256), :]
        e = jnp.exp2((s - best) * (LOG2E * HD**-0.5))
        values = jnp.concatenate([kv[2 * p, 1], kv[2 * p + 1, 1]], axis=1)
        acc[...] += jnp.dot(values, e.astype(BF), preferred_element_type=F32)
        return total + jnp.sum(e.reshape(32, 8, 1024), axis=0)

    total = lax.fori_loop(low, last + 1, gather, jnp.zeros((8, 1024), F32))
    mixed = acc[...] / jnp.sum(total, axis=0, keepdims=True)
    for h in range(4):
        cols = slice(h * 128, h * 128 + 128)
        blocks = [mixed[:, j * 512 + h * 128 : j * 512 + h * 128 + 128].T for j in range(2)]
        outs[0][:, cols] = jnp.where(c == 0, blocks[0], blocks[1]).astype(BF)
        outs[1][:, cols] = jnp.where(c == 0, blocks[1], blocks[0]).astype(BF)


def collect_kernel(idx, *refs):
    pieces, (kv, start, docs) = refs[:5], refs[5:]
    z, y = idx[0], idx[1]
    docs[...] = jnp.zeros((128, HD), F32)
    for n, piece in enumerate(pieces):
        kv[4 * n : 4 * n + 4] = piece[:1024, :].reshape(4, 2, 128, HD)
        before = (z == 0) & (y + n < 4)
        docs[4 * n : 4 * n + 4, :] = jnp.where(before, -1.0, piece[1024:1040, :].astype(F32)[:4, :])
    columns = docs[...].T
    mine = jnp.concatenate([docs[16 + i : 17 + i, :] for i in range(4)], axis=1)
    count = jnp.zeros((8, 512), F32)
    for n in range(20):
        smaller = jnp.where(columns[:, n : n + 1] < mine, 1.0, 0.0)
        count = count + jnp.sum(smaller.reshape(16, 8, 512), axis=0)
    count = jnp.sum(count, axis=0, keepdims=True).astype(jnp.int32)
    for i in range(4):
        row = count[:, i * 128 : i * 128 + 128]
        start[i] = jnp.concatenate([row] * 4, axis=1)


def attend_kernel(idx, query, kv, start, out0, out1, out2, out3, scores, acc):
    attend(idx, query, start, kv, scores, acc, (out0, out1), 0)
    attend(idx, query, start, kv, scores, acc, (out2, out3), 1)


def place_kernel(idx, *refs):
    out = refs[4]
    for k in range(4):
        slot = jnp.bitwise_xor(idx[2], k)
        at = pl.multiple_of(lax.div(slot, 2) * 512, 512)
        out[lax.rem(slot, 2), :, pl.ds(at, 512)] = refs[k][...]


def call(kernel, shapes, args, scratch=(), cost=None, smem=1, mib=16):
    return pl.pallas_call(
        kernel,
        out_shape=shapes,
        in_specs=[SMEM] * smem + [VMEM] * (len(args) - smem),
        out_specs=jax.tree.map(lambda _: VMEM, shapes),
        scratch_shapes=list(scratch),
        cost_estimate=cost,
        compiler_params=pltpu.CompilerParams(vmem_limit_bytes=mib * 1024 * 1024),
    )(*args)


def cost(flops, nbytes):
    return pl.CostEstimate(flops=flops, bytes_accessed=nbytes, transcendentals=0)


def tie(*values):
    return lax.optimization_barrier(values)


def copies(value, axis, count):
    return lax.all_to_all(
        jnp.broadcast_to(value[None], (count, *value.shape)), axis, 0, 0, tiled=True
    )


def local(hidden_in, norm_gain, w_query, w_key, w_value, doc_ids):
    z, y, x, c = (lax.axis_index(a) for a in AXES)
    shape = jax.ShapeDtypeStruct
    where = jnp.stack([z, y, x, c]).astype(jnp.int32)

    piece = shape((32, COLS), BF)
    first, second = call(
        pack_kernel, (piece, piece), (where, w_query, w_key, w_value), cost=cost(0, 1 << 18)
    )
    first, second = permute(first, spread(0)), permute(second, spread(1))
    squares = call(
        squares_kernel,
        shape((256, HD), F32),
        (hidden_in,),
        cost=cost(1 << 20, 2 << 20),
        smem=0,
    )
    others = permute(squares, lambda z, y, x, c: (z, y, x, 1 - c))

    seq_a, seq_b = call(
        norm_kernel,
        (shape((144, HALF), BF), shape((128, HALF), BF)),
        (where, hidden_in, squares, others, doc_ids, norm_gain.reshape(1, WIDTH)),
        cost=cost(1 << 20, 3 << 20),
    )
    first, second, seq_a, seq_b = tie(first, second, seq_a, seq_b)
    right_a, left_b = along_x(seq_a, 1), along_x(seq_b, -1)
    right_b, left_a = along_x(seq_b, 1), along_x(seq_a, -1)
    rows = call(merge_kernel, shape((64, COLS), BF), (where, first, second), cost=cost(0, 1 << 18))
    w_z = copies(rows, "z", NZ).reshape(512, COLS)
    w_z, right_a, left_b = tie(w_z, right_a, left_b)
    far_a, far_b = along_x(right_a, 1), along_x(left_b, -1)

    kv0, q0 = w_z[:, 512:], w_z[:, :512]
    kv_up, kv_down = along_y(kv0, 1), along_y(kv0, -1)
    kv_up, right_b, left_a, q0 = tie(kv_up, right_b, left_a, q0)
    kv_far = along_y(kv_up, 1)
    q_up, q_down = along_y(q0, 1), along_y(q0, -1)
    x_all, docs = call(
        stack_kernel,
        (shape((1024, HALF), BF), shape((16, HD), BF)),
        (where, seq_a, right_a, left_a, far_a, seq_b, right_b, left_b, far_b),
        cost=cost(0, 8 << 20),
    )

    position = (512 * (z * NY + y) + jnp.arange(512, dtype=jnp.int32)).astype(F32)
    inverse = THETA ** (-jnp.arange(64, dtype=F32) * 2.0 / HD)
    angle = position[:, None] * inverse[None, :]
    cos, sin = jnp.cos(angle), jnp.sin(angle)

    x_all, cos, sin = tie(x_all, cos, sin)
    keep, send = call(
        project_kernel,
        (shape((512, 256), F32), shape((512, 256), F32)),
        (where, x_all, kv0, kv_up, kv_down, kv_far),
        (pltpu.VMEM((NZ, 256, 256), BF),),
        cost(2 * 1024 * HALF * 256, 10 << 20),
    )
    got = permute(send, lambda z, y, x, c: (z, y, x, 1 - c))
    got, q_up, q_down = tie(got, q_up, q_down)
    q_far = along_y(q_up, 1)
    own = call(
        rotate_kv_kernel,
        shape((ROWS, HD), BF),
        (keep, got, cos, sin, docs),
        cost=cost(1 << 20, 2 << 20),
        smem=0,
    )
    x_all, own = tie(x_all, own)
    earlier = [
        permute(own, lambda z, y, x, c: (*divmod((z * NY + y + n) % (NZ * NY), NY), x, c))
        for n in (4, 3, 2, 1)
    ]
    keep, send = call(
        project_kernel,
        (shape((512, 512), F32), shape((512, 512), F32)),
        (where, x_all, q0, q_up, q_down, q_far),
        (pltpu.VMEM((NZ, 256, 512), BF),),
        cost(2 * 1024 * HALF * 512, 10 << 20),
    )
    got = permute(send, lambda z, y, x, c: (z, y, x, 1 - c))
    query = call(
        rotate_q_kernel,
        shape((4, 512, HD), BF),
        (keep, got, cos, sin),
        cost=cost(4 << 20, 3 << 20),
        smem=0,
    )
    kv, start = call(
        collect_kernel,
        (shape((20, 2, 128, HD), BF), shape((4, 1, 512), jnp.int32)),
        (where, *earlier, own),
        (pltpu.VMEM((128, HD), F32),),
        cost(1 << 36, 4 << 20),
    )
    block = shape((128, 512), BF)
    outs = call(
        attend_kernel,
        (block,) * 4,
        (where, query, kv, start),
        (pltpu.VMEM((2560, 1024), F32), pltpu.VMEM((HD, 1024), F32)),
        cost(1 << 31, 4 << 20),
        mib=24,
    )
    outs = [permute(out, back(k)) for k, out in enumerate(outs)]
    return call(
        place_kernel, shape((2, 128, 1024), BF), (where, *outs), cost=cost(0, 1 << 20)
    )


def solution(mesh):
    fine = Mesh(mesh.devices.reshape(NZ, NY, NX, NC), AXES)
    ctx = ("z", "y", "x")
    return jax.shard_map(
        local,
        mesh=fine,
        in_specs=(
            P(None, ctx, "head"),
            P(),
            P(ctx, "head"),
            P(ctx, "head"),
            P(ctx, "head"),
            P(None, ctx),
        ),
        out_specs=P(None, ctx, "head"),
        check_vma=False,
    )
```

```python
import jax
import jax.numpy as jnp
from jax import lax
from jax.experimental import pallas as pl
from jax.experimental.pallas import tpu as pltpu
from jax.sharding import Mesh, PartitionSpec as P

HD = 128
NZ, NY, NX, NC = 8, 4, 4, 2
AXES = ("z", "y", "x", "head")
THETA = 500000.0
EPS = 1e-05
WIDTH = 4096
HALF = WIDTH // 2
COLS = 6 * HD
LOG2E = 1.4426950408889634
BF = jnp.bfloat16
F32 = jnp.float32


def flat(z, y, x, c):
    return ((z * NY + y) * NX + x) * NC + c


def permute(value, to):
    pairs = [
        (flat(z, y, x, c), flat(*to(z, y, x, c)))
        for z in range(NZ)
        for y in range(NY)
        for x in range(NX)
        for c in range(NC)
    ]
    return lax.ppermute(value, AXES, pairs)


def along_x(value, by):
    return permute(value, lambda z, y, x, c: (z, y, (x + by) % NX, c))


def along_z(value, by):
    return permute(value, lambda z, y, x, c: ((z + by) % NZ, y, x, c))


def along_y(value, by):
    return permute(value, lambda z, y, x, c: (z, (y + by) % NY, x, c))


def spread(by):
    def to(z, y, x, c):
        b = (x + by) % 2
        return 2 * (z % 4) + y // 2, 2 * (y % 2) + x // 2, 2 * c + b, z // 4

    return to


def back(k):
    def to(z, y, x, c):
        return z, y, (2 * (x % 2) + c) ^ k, x // 2

    return to


VMEM = pl.BlockSpec(memory_space=pltpu.VMEM)
SMEM = pl.BlockSpec(memory_space=pltpu.SMEM)
ROWS = 8 * HD + 16


def pack_kernel(idx, query, key, value, first, second):
    x = idx[2]
    for by, out in ((0, first), (1, second)):
        b = lax.rem(x + by, 2)
        out[:, :512] = query[:, pl.ds(pl.multiple_of(b * 512, 512), 512)]
        out[:, 512:640] = key[:, pl.ds(pl.multiple_of(b * 128, 128), 128)]
        out[:, 640:] = value[:, pl.ds(pl.multiple_of(b * 128, 128), 128)]


def squares_kernel(hidden, squares):
    for s in range(2):
        wide = hidden[s].astype(F32)
        total = jnp.sum(wide * wide, axis=-1, keepdims=True)
        squares[s * 128 : s * 128 + 128, :] = jnp.broadcast_to(total, (HD, HD))


def norm_kernel(idx, hidden, squares, others, docs, gain, seq_a, seq_b):
    g = gain[:, pl.ds(pl.multiple_of(idx[3] * HALF, HALF), HALF)].astype(F32)
    for s, out in ((0, seq_a), (1, seq_b)):
        for t in range(4):
            rows = slice(t * 32, t * 32 + 32)
            both = slice(s * 128 + t * 32, s * 128 + t * 32 + 32)
            scale = lax.rsqrt((squares[both, :] + others[both, :]) * (1.0 / WIDTH) + EPS)
            wide = hidden[s, rows, :].astype(F32)
            out[rows, :] = (wide * scale[:, :1] * g).astype(BF)
    extra = jnp.concatenate([docs[...].astype(F32), jnp.zeros((14, HD), F32)], axis=0)
    seq_a[128:144, :HD] = extra.astype(BF)
    seq_a[128:144, HD:] = jnp.zeros((16, HALF - HD), BF)


def merge_kernel(idx, first, second, out):
    odd = lax.rem(idx[2], 2) == 1
    top, low = first[...].astype(F32), second[...].astype(F32)
    out[:32, :] = jnp.where(odd, low, top).astype(BF)
    out[32:, :] = jnp.where(odd, top, low).astype(BF)


def stack_kernel(idx, *refs):
    hidden, (x_all, docs) = refs[:8], refs[8:]
    x, c = idx[2], idx[3]
    row = lax.broadcasted_iota(jnp.int32, (16, HD), 0)
    found = jnp.zeros((16, HD), F32)
    for n, ref in enumerate(hidden):
        s, d = n // 4, (0, -1, 1, 2)[n % 4]
        chip = lax.rem(x + d + NX, NX)
        base = jnp.where(c == s, 0, 512) + chip * 128
        x_all[pl.ds(pl.multiple_of(base, 128), 128), :] = ref[:128, :]
        if s == 0:
            tile = ref[128:144, :HD].astype(F32)
            mine = jnp.where(c == 0, tile[0:1, :], tile[1:2, :])
            found = jnp.where(row == chip, mine, found)
    docs[...] = found.astype(BF)


def multiply(x_all, w_all, keep, send):
    for t in range(2):
        at = t * 256
        send[at : at + 256, :] = jnp.dot(
            x_all[512 + at : 768 + at, :], w_all, preferred_element_type=F32
        )
    for t in range(2):
        at = t * 256
        keep[at : at + 256, :] = jnp.dot(
            x_all[at : at + 256, :], w_all, preferred_element_type=F32
        )


def project_kernel(idx, x_all, own, up, down, far, keep, send, w_all):
    for ref, d in ((own, 0), (up, -1), (down, 1), (far, 2)):
        shift = pl.multiple_of(lax.rem(idx[1] + d + NY, NY) * 64, 64)
        for z in range(NZ):
            w_all[z, pl.ds(shift, 64), :] = ref[z * 64 : z * 64 + 64, :]
    multiply(x_all, w_all[...].reshape(HALF, own.shape[1]), keep, send)


def turned(value, cos, sin):
    cosine = jnp.concatenate([cos, cos], axis=1)
    sine = jnp.concatenate([-sin, sin], axis=1)
    return value * cosine + pltpu.roll(value, 64, 1) * sine


def rotate_kv_kernel(keep, got, cos, sin, docs, kv):
    for i in range(4):
        rows = slice(i * 128, i * 128 + 128)
        value = keep[rows, :] + got[rows, :]
        at = i * 256
        kv[at : at + 128, :] = turned(value[:, :128], cos[rows, :], sin[rows, :]).astype(BF)
        kv[at + 128 : at + 256, :] = value[:, 128:].T.astype(BF)
    kv[1024:1040, :] = docs[...]


def rotate_q_kernel(keep, got, cos, sin, query):
    for i in range(4):
        rows = slice(i * 128, i * 128 + 128)
        for h in range(4):
            cols = slice(h * 128, h * 128 + 128)
            value = keep[rows, cols] + got[rows, cols]
            query[i, h * 128 : h * 128 + 128, :] = turned(value, cos[rows, :], sin[rows, :]).astype(BF)


def attend(idx, query, start, kv, scores, acc, outs, part):
    c = idx[3]
    m = jnp.bitwise_xor(lax.rem(idx[2], 2), part)
    first = jnp.concatenate([start[2 * m], start[2 * m + 1]], axis=1)
    rows = query[pl.ds(2 * m, 2)].reshape(1024, HD)
    sub = lax.broadcasted_iota(jnp.int32, (256, 1024), 0)
    lane = lax.broadcasted_iota(jnp.int32, (256, 1024), 1)
    lane = lax.div(lane, 512) * 128 + lax.rem(lane, 128)
    last = 8 + m
    low = jnp.minimum(lax.div(jnp.maximum(jnp.min(first), 0), 256), last)
    contract = (((1,), (1,)), ((), ()))

    def score(p, pairs=1):
        keys = kv[pl.ds(2 * p, 2 * pairs), 0].reshape(256 * pairs, HD)
        return lax.dot_general(keys, rows, contract, preferred_element_type=F32)

    def top(s):
        return jnp.max(s.reshape(-1, 8, 1024), axis=0)

    def keep(p, s, best):
        scores[pl.ds(pl.multiple_of(p * 256, 256), s.shape[0]), :] = s
        return jnp.maximum(best, top(s))

    def masked(p, best):
        return keep(p, jnp.where(sub >= first - 256 * p, score(p), -1e30), best)

    def whole(p, best):
        return keep(p, score(p), best)

    s = jnp.where((sub >= first - 256 * last) & (sub <= lane), score(last), -1e30)
    scores[pl.ds(pl.multiple_of(256 * last, 256), 256), :] = s
    inside = jnp.clip(lax.div(jnp.max(first) + 255, 256), low, last)
    best = lax.fori_loop(low, inside, masked, top(s))
    twice = lax.div(last - inside, 2)
    best = lax.fori_loop(
        0, twice, lambda t, b: keep(inside + 2 * t, score(inside + 2 * t, 2), b), best
    )
    best = lax.fori_loop(inside + 2 * twice, last, whole, best)
    best = jnp.max(best, axis=0, keepdims=True)
    acc[...] = jnp.zeros((HD, 1024), F32)

    def gather(p, total, pairs=1):
        s = scores[pl.ds(pl.multiple_of(p * 256, 256), 256 * pairs), :]
        e = jnp.exp2((s - best) * (LOG2E * HD**-0.5))
        values = jnp.concatenate([kv[2 * p + j, 1] for j in range(2 * pairs)], axis=1)
        acc[...] += jnp.dot(values, e.astype(BF), preferred_element_type=F32)
        return total + jnp.sum(e.reshape(-1, 8, 1024), axis=0)

    twice = lax.div(last + 1 - low, 2)
    total = lax.fori_loop(
        0, twice, lambda t, sums: gather(low + 2 * t, sums, 2), jnp.zeros((8, 1024), F32)
    )
    total = lax.fori_loop(low + 2 * twice, last + 1, gather, total)
    mixed = acc[...] / jnp.sum(total, axis=0, keepdims=True)
    for h in range(4):
        cols = slice(h * 128, h * 128 + 128)
        blocks = [mixed[:, j * 512 + h * 128 : j * 512 + h * 128 + 128].T for j in range(2)]
        outs[0][:, cols] = jnp.where(c == 0, blocks[0], blocks[1]).astype(BF)
        outs[1][:, cols] = jnp.where(c == 0, blocks[1], blocks[0]).astype(BF)


def collect_kernel(idx, *refs):
    pieces, (kv, start, docs) = refs[:5], refs[5:]
    z, y = idx[0], idx[1]
    docs[...] = jnp.zeros((128, HD), F32)
    for n, piece in enumerate(pieces):
        kv[4 * n : 4 * n + 4] = piece[:1024, :].reshape(4, 2, 128, HD)
        before = (z == 0) & (y + n < 4)
        docs[4 * n : 4 * n + 4, :] = jnp.where(before, -1.0, piece[1024:1040, :].astype(F32)[:4, :])
    columns = docs[...].T
    mine = jnp.concatenate([docs[16 + i : 17 + i, :] for i in range(4)], axis=1)
    count = jnp.zeros((8, 512), F32)
    for n in range(20):
        smaller = jnp.where(columns[:, n : n + 1] < mine, 1.0, 0.0)
        count = count + jnp.sum(smaller.reshape(16, 8, 512), axis=0)
    count = jnp.sum(count, axis=0, keepdims=True).astype(jnp.int32)
    for i in range(4):
        row = count[:, i * 128 : i * 128 + 128]
        start[i] = jnp.concatenate([row] * 4, axis=1)


def attend_kernel(idx, query, kv, start, out0, out1, out2, out3, scores, acc):
    attend(idx, query, start, kv, scores, acc, (out0, out1), 0)
    attend(idx, query, start, kv, scores, acc, (out2, out3), 1)


def place_kernel(idx, *refs):
    out = refs[4]
    for k in range(4):
        slot = jnp.bitwise_xor(idx[2], k)
        at = pl.multiple_of(lax.div(slot, 2) * 512, 512)
        out[lax.rem(slot, 2), :, pl.ds(at, 512)] = refs[k][...]


def call(kernel, shapes, args, scratch=(), cost=None, smem=1, mib=16):
    return pl.pallas_call(
        kernel,
        out_shape=shapes,
        in_specs=[SMEM] * smem + [VMEM] * (len(args) - smem),
        out_specs=jax.tree.map(lambda _: VMEM, shapes),
        scratch_shapes=list(scratch),
        cost_estimate=cost,
        compiler_params=pltpu.CompilerParams(vmem_limit_bytes=mib * 1024 * 1024),
    )(*args)


def cost(flops, nbytes):
    return pl.CostEstimate(flops=flops, bytes_accessed=nbytes, transcendentals=0)


def tie(*values):
    return lax.optimization_barrier(values)


def copies(value, axis, count):
    return lax.all_to_all(
        jnp.broadcast_to(value[None], (count, *value.shape)), axis, 0, 0, tiled=True
    )


def local(hidden_in, norm_gain, w_query, w_key, w_value, doc_ids):
    z, y, x, c = (lax.axis_index(a) for a in AXES)
    shape = jax.ShapeDtypeStruct
    where = jnp.stack([z, y, x, c]).astype(jnp.int32)

    piece = shape((32, COLS), BF)
    first, second = call(
        pack_kernel, (piece, piece), (where, w_query, w_key, w_value), cost=cost(0, 1 << 18)
    )
    first, second = permute(first, spread(0)), permute(second, spread(1))
    squares = call(
        squares_kernel,
        shape((256, HD), F32),
        (hidden_in,),
        cost=cost(1 << 20, 2 << 20),
        smem=0,
    )
    others = permute(squares, lambda z, y, x, c: (z, y, x, 1 - c))

    seq_a, seq_b = call(
        norm_kernel,
        (shape((144, HALF), BF), shape((128, HALF), BF)),
        (where, hidden_in, squares, others, doc_ids, norm_gain.reshape(1, WIDTH)),
        cost=cost(1 << 20, 3 << 20),
    )
    first, second, seq_a, seq_b = tie(first, second, seq_a, seq_b)
    right_a, left_b = along_x(seq_a, 1), along_x(seq_b, -1)
    right_b, left_a = along_x(seq_b, 1), along_x(seq_a, -1)
    rows = call(merge_kernel, shape((64, COLS), BF), (where, first, second), cost=cost(0, 1 << 18))
    w_z = copies(rows, "z", NZ).reshape(512, COLS)
    w_z, right_a, left_b = tie(w_z, right_a, left_b)
    far_a, far_b = along_x(right_a, 1), along_x(left_b, -1)

    kv0, q0 = w_z[:, 512:], w_z[:, :512]
    kv_up, kv_down = along_y(kv0, 1), along_y(kv0, -1)
    kv_up, kv_down, right_b, left_a, q0 = tie(kv_up, kv_down, right_b, left_a, q0)
    kv_far = along_y(kv_up, 1)
    q_up, q_down = along_y(q0, 1), along_y(q0, -1)
    x_all, docs = call(
        stack_kernel,
        (shape((1024, HALF), BF), shape((16, HD), BF)),
        (where, seq_a, right_a, left_a, far_a, seq_b, right_b, left_b, far_b),
        cost=cost(0, 8 << 20),
    )

    position = (512 * (z * NY + y) + jnp.arange(512, dtype=jnp.int32)).astype(F32)
    inverse = THETA ** (-jnp.arange(64, dtype=F32) * 2.0 / HD)
    angle = position[:, None] * inverse[None, :]
    cos, sin = jnp.cos(angle), jnp.sin(angle)

    x_all, cos, sin = tie(x_all, cos, sin)
    keep, send = call(
        project_kernel,
        (shape((512, 256), F32), shape((512, 256), F32)),
        (where, x_all, kv0, kv_up, kv_down, kv_far),
        (pltpu.VMEM((NZ, 256, 256), BF),),
        cost(2 * 1024 * HALF * 256, 10 << 20),
    )
    got = permute(send, lambda z, y, x, c: (z, y, x, 1 - c))
    got, q_up, q_down = tie(got, q_up, q_down)
    q_far = along_y(q_up, 1)
    own = call(
        rotate_kv_kernel,
        shape((ROWS, HD), BF),
        (keep, got, cos, sin, docs),
        cost=cost(1 << 20, 2 << 20),
        smem=0,
    )
    x_all, own = tie(x_all, own)
    earlier = [
        permute(own, lambda z, y, x, c: (*divmod((z * NY + y + n) % (NZ * NY), NY), x, c))
        for n in (4, 3, 2, 1)
    ]
    keep, send = call(
        project_kernel,
        (shape((512, 512), F32), shape((512, 512), F32)),
        (where, x_all, q0, q_up, q_down, q_far),
        (pltpu.VMEM((NZ, 256, 512), BF),),
        cost(2 * 1024 * HALF * 512, 10 << 20),
    )
    got = permute(send, lambda z, y, x, c: (z, y, x, 1 - c))
    query = call(
        rotate_q_kernel,
        shape((4, 512, HD), BF),
        (keep, got, cos, sin),
        cost=cost(4 << 20, 3 << 20),
        smem=0,
    )
    kv, start = call(
        collect_kernel,
        (shape((20, 2, 128, HD), BF), shape((4, 1, 512), jnp.int32)),
        (where, *earlier, own),
        (pltpu.VMEM((128, HD), F32),),
        cost(1 << 36, 4 << 20),
    )
    block = shape((128, 512), BF)
    outs = call(
        attend_kernel,
        (block,) * 4,
        (where, query, kv, start),
        (pltpu.VMEM((2560, 1024), F32), pltpu.VMEM((HD, 1024), F32)),
        cost(1 << 31, 4 << 20),
        mib=24,
    )
    outs = [permute(out, back(k)) for k, out in enumerate(outs)]
    return call(
        place_kernel, shape((2, 128, 1024), BF), (where, *outs), cost=cost(0, 1 << 20)
    )


def solution(mesh):
    fine = Mesh(mesh.devices.reshape(NZ, NY, NX, NC), AXES)
    ctx = ("z", "y", "x")
    return jax.shard_map(
        local,
        mesh=fine,
        in_specs=(
            P(None, ctx, "head"),
            P(),
            P(ctx, "head"),
            P(ctx, "head"),
            P(ctx, "head"),
            P(None, ctx),
        ),
        out_specs=P(None, ctx, "head"),
        check_vma=False,
    )
```

```python
import jax
import jax.numpy as jnp
from jax import lax
from jax.experimental import pallas as pl
from jax.experimental.pallas import tpu as pltpu
from jax.sharding import Mesh, PartitionSpec as P

HD = 128
NZ, NY, NX, NC = 8, 4, 4, 2
AXES = ("z", "y", "x", "head")
THETA = 500000.0
EPS = 1e-05
WIDTH = 4096
HALF = WIDTH // 2
COLS = 6 * HD
LOG2E = 1.4426950408889634
BF = jnp.bfloat16
F32 = jnp.float32


def flat(z, y, x, c):
    return ((z * NY + y) * NX + x) * NC + c


def permute(value, to):
    pairs = [
        (flat(z, y, x, c), flat(*to(z, y, x, c)))
        for z in range(NZ)
        for y in range(NY)
        for x in range(NX)
        for c in range(NC)
    ]
    return lax.ppermute(value, AXES, pairs)


def along_x(value, by):
    return permute(value, lambda z, y, x, c: (z, y, (x + by) % NX, c))


def along_z(value, by):
    return permute(value, lambda z, y, x, c: ((z + by) % NZ, y, x, c))


def along_y(value, by):
    return permute(value, lambda z, y, x, c: (z, (y + by) % NY, x, c))


def spread(by):
    def to(z, y, x, c):
        b = (x + by) % 2
        return 2 * (z % 4) + y // 2, 2 * (y % 2) + x // 2, 2 * c + b, z // 4

    return to


def back(k):
    def to(z, y, x, c):
        return z, y, (2 * (x % 2) + c) ^ k, x // 2

    return to


VMEM = pl.BlockSpec(memory_space=pltpu.VMEM)
SMEM = pl.BlockSpec(memory_space=pltpu.SMEM)
ROWS = 8 * HD + 16


def pack_kernel(idx, query, key, value, first, second):
    x = idx[2]
    for by, out in ((0, first), (1, second)):
        b = lax.rem(x + by, 2)
        out[:, :512] = query[:, pl.ds(pl.multiple_of(b * 512, 512), 512)]
        out[:, 512:640] = key[:, pl.ds(pl.multiple_of(b * 128, 128), 128)]
        out[:, 640:] = value[:, pl.ds(pl.multiple_of(b * 128, 128), 128)]


def squares_kernel(hidden, squares):
    for s in range(2):
        wide = hidden[s].astype(F32)
        total = jnp.sum(wide * wide, axis=-1, keepdims=True)
        squares[s * 128 : s * 128 + 128, :] = jnp.broadcast_to(total, (HD, HD))


def norm_kernel(idx, hidden, squares, others, docs, gain, seq_a, seq_b):
    g = gain[:, pl.ds(pl.multiple_of(idx[3] * HALF, HALF), HALF)].astype(F32)
    for s, out in ((0, seq_a), (1, seq_b)):
        for t in range(4):
            rows = slice(t * 32, t * 32 + 32)
            both = slice(s * 128 + t * 32, s * 128 + t * 32 + 32)
            scale = lax.rsqrt((squares[both, :] + others[both, :]) * (1.0 / WIDTH) + EPS)
            wide = hidden[s, rows, :].astype(F32)
            out[rows, :] = (wide * scale[:, :1] * g).astype(BF)
    extra = jnp.concatenate([docs[...].astype(F32), jnp.zeros((14, HD), F32)], axis=0)
    seq_a[128:144, :HD] = extra.astype(BF)
    seq_a[128:144, HD:] = jnp.zeros((16, HALF - HD), BF)


def merge_kernel(idx, first, second, out):
    odd = lax.rem(idx[2], 2) == 1
    top, low = first[...].astype(F32), second[...].astype(F32)
    out[:32, :] = jnp.where(odd, low, top).astype(BF)
    out[32:, :] = jnp.where(odd, top, low).astype(BF)


def stack_kernel(idx, *refs):
    hidden, (x_all, docs) = refs[:8], refs[8:]
    x, c = idx[2], idx[3]
    row = lax.broadcasted_iota(jnp.int32, (16, HD), 0)
    found = jnp.zeros((16, HD), F32)
    for n, ref in enumerate(hidden):
        s, d = n // 4, (0, -1, 1, 2)[n % 4]
        chip = lax.rem(x + d + NX, NX)
        base = jnp.where(c == s, 0, 512) + chip * 128
        x_all[pl.ds(pl.multiple_of(base, 128), 128), :] = ref[:128, :]
        if s == 0:
            tile = ref[128:144, :HD].astype(F32)
            mine = jnp.where(c == 0, tile[0:1, :], tile[1:2, :])
            found = jnp.where(row == chip, mine, found)
    docs[...] = found.astype(BF)


def multiply(x_all, w_all, keep, send):
    for t in range(2):
        at = t * 256
        send[at : at + 256, :] = jnp.dot(
            x_all[512 + at : 768 + at, :], w_all, preferred_element_type=F32
        )
    for t in range(2):
        at = t * 256
        keep[at : at + 256, :] = jnp.dot(
            x_all[at : at + 256, :], w_all, preferred_element_type=F32
        )


def project_kernel(idx, x_all, own, up, down, far, keep, send, w_all):
    for ref, d in ((own, 0), (up, -1), (down, 1), (far, 2)):
        shift = pl.multiple_of(lax.rem(idx[1] + d + NY, NY) * 64, 64)
        for z in range(NZ):
            w_all[z, pl.ds(shift, 64), :] = ref[z * 64 : z * 64 + 64, :]
    multiply(x_all, w_all[...].reshape(HALF, own.shape[1]), keep, send)


def turned(value, cos, sin):
    cosine = jnp.concatenate([cos, cos], axis=1)
    sine = jnp.concatenate([-sin, sin], axis=1)
    return value * cosine + pltpu.roll(value, 64, 1) * sine


def rotate_kv_kernel(keep, got, cos, sin, docs, kv):
    for i in range(4):
        rows = slice(i * 128, i * 128 + 128)
        value = keep[rows, :] + got[rows, :]
        at = i * 256
        kv[at : at + 128, :] = turned(value[:, :128], cos[rows, :], sin[rows, :]).astype(BF)
        kv[at + 128 : at + 256, :] = value[:, 128:].T.astype(BF)
    kv[1024:1040, :] = docs[...]


def rotate_q_kernel(keep, got, cos, sin, query):
    for i in range(4):
        rows = slice(i * 128, i * 128 + 128)
        for h in range(4):
            cols = slice(h * 128, h * 128 + 128)
            value = keep[rows, cols] + got[rows, cols]
            query[i, h * 128 : h * 128 + 128, :] = turned(value, cos[rows, :], sin[rows, :]).astype(BF)


def attend(idx, query, start, kv, scores, acc, outs, part):
    c = idx[3]
    m = jnp.bitwise_xor(lax.rem(idx[2], 2), part)
    first = jnp.concatenate([start[2 * m], start[2 * m + 1]], axis=1)
    rows = query[pl.ds(2 * m, 2)].reshape(1024, HD)
    sub = lax.broadcasted_iota(jnp.int32, (256, 1024), 0)
    lane = lax.broadcasted_iota(jnp.int32, (256, 1024), 1)
    lane = lax.div(lane, 512) * 128 + lax.rem(lane, 128)
    last = 8 + m
    low = jnp.minimum(lax.div(jnp.maximum(jnp.min(first), 0), 256), last)
    contract = (((1,), (1,)), ((), ()))

    def score(p, pairs=1):
        keys = kv[pl.ds(2 * p, 2 * pairs), 0].reshape(256 * pairs, HD)
        return lax.dot_general(keys, rows, contract, preferred_element_type=F32)

    def top(s):
        return jnp.max(s.reshape(-1, 8, 1024), axis=0)

    def keep(p, s, best):
        scores[pl.ds(pl.multiple_of(p * 256, 256), s.shape[0]), :] = s
        return jnp.maximum(best, top(s))

    def masked(p, best):
        return keep(p, jnp.where(sub >= first - 256 * p, score(p), -1e30), best)

    s = jnp.where((sub >= first - 256 * last) & (sub <= lane), score(last), -1e30)
    scores[pl.ds(pl.multiple_of(256 * last, 256), 256), :] = s
    inside = jnp.clip(lax.div(jnp.max(first) + 255, 256), low, last)
    best = lax.fori_loop(low, inside, masked, top(s))
    at, many = inside, (4, 2, 1)
    for step in many:
        turns = lax.div(last - at, step)
        best = lax.fori_loop(
            0,
            turns,
            lambda t, b, at=at, step=step: keep(at + step * t, score(at + step * t, step), b),
            best,
        )
        at = at + step * turns
    best = jnp.max(best, axis=0, keepdims=True)
    acc[...] = jnp.zeros((HD, 1024), F32)

    def gather(p, total, pairs=1):
        s = scores[pl.ds(pl.multiple_of(p * 256, 256), 256 * pairs), :]
        e = jnp.exp2((s - best) * (LOG2E * HD**-0.5))
        values = jnp.concatenate([kv[2 * p + j, 1] for j in range(2 * pairs)], axis=1)
        acc[...] += jnp.dot(values, e.astype(BF), preferred_element_type=F32)
        return total + jnp.sum(e.reshape(-1, 8, 1024), axis=0)

    at, total = low, jnp.zeros((8, 1024), F32)
    for step in many:
        turns = lax.div(last + 1 - at, step)
        total = lax.fori_loop(
            0, turns, lambda t, b, at=at, step=step: gather(at + step * t, b, step), total
        )
        at = at + step * turns
    mixed = acc[...] / jnp.sum(total, axis=0, keepdims=True)
    for h in range(4):
        cols = slice(h * 128, h * 128 + 128)
        blocks = [mixed[:, j * 512 + h * 128 : j * 512 + h * 128 + 128].T for j in range(2)]
        outs[0][:, cols] = jnp.where(c == 0, blocks[0], blocks[1]).astype(BF)
        outs[1][:, cols] = jnp.where(c == 0, blocks[1], blocks[0]).astype(BF)


def collect_kernel(idx, *refs):
    pieces, (kv, start, docs) = refs[:5], refs[5:]
    z, y = idx[0], idx[1]
    docs[...] = jnp.zeros((128, HD), F32)
    for n, piece in enumerate(pieces):
        kv[4 * n : 4 * n + 4] = piece[:1024, :].reshape(4, 2, 128, HD)
        before = (z == 0) & (y + n < 4)
        docs[4 * n : 4 * n + 4, :] = jnp.where(before, -1.0, piece[1024:1040, :].astype(F32)[:4, :])
    columns = docs[...].T
    mine = jnp.concatenate([docs[16 + i : 17 + i, :] for i in range(4)], axis=1)
    count = jnp.zeros((8, 512), F32)
    for n in range(20):
        smaller = jnp.where(columns[:, n : n + 1] < mine, 1.0, 0.0)
        count = count + jnp.sum(smaller.reshape(16, 8, 512), axis=0)
    count = jnp.sum(count, axis=0, keepdims=True).astype(jnp.int32)
    for i in range(4):
        row = count[:, i * 128 : i * 128 + 128]
        start[i] = jnp.concatenate([row] * 4, axis=1)


def attend_kernel(idx, query, kv, start, out0, out1, out2, out3, scores, acc):
    attend(idx, query, start, kv, scores, acc, (out0, out1), 0)
    attend(idx, query, start, kv, scores, acc, (out2, out3), 1)


def place_kernel(idx, *refs):
    out = refs[4]
    for k in range(4):
        slot = jnp.bitwise_xor(idx[2], k)
        at = pl.multiple_of(lax.div(slot, 2) * 512, 512)
        out[lax.rem(slot, 2), :, pl.ds(at, 512)] = refs[k][...]


def call(kernel, shapes, args, scratch=(), cost=None, smem=1, mib=16):
    return pl.pallas_call(
        kernel,
        out_shape=shapes,
        in_specs=[SMEM] * smem + [VMEM] * (len(args) - smem),
        out_specs=jax.tree.map(lambda _: VMEM, shapes),
        scratch_shapes=list(scratch),
        cost_estimate=cost,
        compiler_params=pltpu.CompilerParams(vmem_limit_bytes=mib * 1024 * 1024),
    )(*args)


def cost(flops, nbytes):
    return pl.CostEstimate(flops=flops, bytes_accessed=nbytes, transcendentals=0)


def tie(*values):
    return lax.optimization_barrier(values)


def copies(value, axis, count):
    return lax.all_to_all(
        jnp.broadcast_to(value[None], (count, *value.shape)), axis, 0, 0, tiled=True
    )


def local(hidden_in, norm_gain, w_query, w_key, w_value, doc_ids):
    z, y, x, c = (lax.axis_index(a) for a in AXES)
    shape = jax.ShapeDtypeStruct
    where = jnp.stack([z, y, x, c]).astype(jnp.int32)

    piece = shape((32, COLS), BF)
    first, second = call(
        pack_kernel, (piece, piece), (where, w_query, w_key, w_value), cost=cost(0, 1 << 18)
    )
    first, second = permute(first, spread(0)), permute(second, spread(1))
    squares = call(
        squares_kernel,
        shape((256, HD), F32),
        (hidden_in,),
        cost=cost(1 << 20, 2 << 20),
        smem=0,
    )
    others = permute(squares, lambda z, y, x, c: (z, y, x, 1 - c))

    seq_a, seq_b = call(
        norm_kernel,
        (shape((144, HALF), BF), shape((128, HALF), BF)),
        (where, hidden_in, squares, others, doc_ids, norm_gain.reshape(1, WIDTH)),
        cost=cost(1 << 20, 3 << 20),
    )
    first, second, seq_a, seq_b = tie(first, second, seq_a, seq_b)
    right_a, left_b = along_x(seq_a, 1), along_x(seq_b, -1)
    right_b, left_a = along_x(seq_b, 1), along_x(seq_a, -1)
    rows = call(merge_kernel, shape((64, COLS), BF), (where, first, second), cost=cost(0, 1 << 18))
    w_z = copies(rows, "z", NZ).reshape(512, COLS)
    w_z, right_a, left_b = tie(w_z, right_a, left_b)
    far_a, far_b = along_x(right_a, 1), along_x(left_b, -1)

    kv0, q0 = w_z[:, 512:], w_z[:, :512]
    kv_up, kv_down = along_y(kv0, 1), along_y(kv0, -1)
    kv_up, kv_down, right_b, left_a, q0 = tie(kv_up, kv_down, right_b, left_a, q0)
    kv_far = along_y(kv_up, 1)
    q_up, q_down = along_y(q0, 1), along_y(q0, -1)
    x_all, docs = call(
        stack_kernel,
        (shape((1024, HALF), BF), shape((16, HD), BF)),
        (where, seq_a, right_a, left_a, far_a, seq_b, right_b, left_b, far_b),
        cost=cost(0, 8 << 20),
    )

    position = (512 * (z * NY + y) + jnp.arange(512, dtype=jnp.int32)).astype(F32)
    inverse = THETA ** (-jnp.arange(64, dtype=F32) * 2.0 / HD)
    angle = position[:, None] * inverse[None, :]
    cos, sin = jnp.cos(angle), jnp.sin(angle)

    x_all, cos, sin = tie(x_all, cos, sin)
    keep, send = call(
        project_kernel,
        (shape((512, 256), F32), shape((512, 256), F32)),
        (where, x_all, kv0, kv_up, kv_down, kv_far),
        (pltpu.VMEM((NZ, 256, 256), BF),),
        cost(2 * 1024 * HALF * 256, 10 << 20),
    )
    got = permute(send, lambda z, y, x, c: (z, y, x, 1 - c))
    got, q_up, q_down = tie(got, q_up, q_down)
    q_far = along_y(q_up, 1)
    own = call(
        rotate_kv_kernel,
        shape((ROWS, HD), BF),
        (keep, got, cos, sin, docs),
        cost=cost(1 << 20, 2 << 20),
        smem=0,
    )
    x_all, own = tie(x_all, own)
    earlier = [
        permute(own, lambda z, y, x, c: (*divmod((z * NY + y + n) % (NZ * NY), NY), x, c))
        for n in (4, 3, 2, 1)
    ]
    keep, send = call(
        project_kernel,
        (shape((512, 512), F32), shape((512, 512), F32)),
        (where, x_all, q0, q_up, q_down, q_far),
        (pltpu.VMEM((NZ, 256, 512), BF),),
        cost(2 * 1024 * HALF * 512, 10 << 20),
    )
    got = permute(send, lambda z, y, x, c: (z, y, x, 1 - c))
    query = call(
        rotate_q_kernel,
        shape((4, 512, HD), BF),
        (keep, got, cos, sin),
        cost=cost(4 << 20, 3 << 20),
        smem=0,
    )
    kv, start = call(
        collect_kernel,
        (shape((20, 2, 128, HD), BF), shape((4, 1, 512), jnp.int32)),
        (where, *earlier, own),
        (pltpu.VMEM((128, HD), F32),),
        cost(1 << 36, 4 << 20),
    )
    block = shape((128, 512), BF)
    outs = call(
        attend_kernel,
        (block,) * 4,
        (where, query, kv, start),
        (pltpu.VMEM((2560, 1024), F32), pltpu.VMEM((HD, 1024), F32)),
        cost(1 << 31, 4 << 20),
        mib=28,
    )
    outs = [permute(out, back(k)) for k, out in enumerate(outs)]
    return call(
        place_kernel, shape((2, 128, 1024), BF), (where, *outs), cost=cost(0, 1 << 20)
    )


def solution(mesh):
    fine = Mesh(mesh.devices.reshape(NZ, NY, NX, NC), AXES)
    ctx = ("z", "y", "x")
    return jax.shard_map(
        local,
        mesh=fine,
        in_specs=(
            P(None, ctx, "head"),
            P(),
            P(ctx, "head"),
            P(ctx, "head"),
            P(ctx, "head"),
            P(None, ctx),
        ),
        out_specs=P(None, ctx, "head"),
        check_vma=False,
    )
```
